32 devices in a mesh: ctx: 8 (over z, y), head: 4 (over x, core).
Axes of the slice: x: 2, y: 2, z: 4, core: 2. Of those that a mesh axis runs over, the one named last changes fastest.
Arguments:
- queries: bfloat16 [8192, 32, 128], P('ctx', 'head'), may hold values from -6 to 6
- keys: bfloat16 [8192, 32, 128], P('ctx', 'head'), may hold values from -6 to 6
- values: bfloat16 [8192, 32, 128], P('ctx', 'head'), may hold values from -6 to 6
- d_layer: bfloat16 [8192, 4096], P('ctx', 'head'), may hold values from -6 to 6
- out_weight: bfloat16 [4096, 4096], P('head'), may hold values from -0.09375 to 0.09375
Outputs:
- d_queries: bfloat16 [8192, 32, 128], P('ctx', 'head')
- d_keys: bfloat16 [8192, 32, 128], P('ctx', 'head')
- d_values: bfloat16 [8192, 32, 128], P('ctx', 'head')
The draws below stay inside these ranges and needn't reach their ends.
All inputs are finite; a program needn't handle non-finite values.
Results may differ from the reference program's by a relative error of at most 0.0071.
Values may be sent and summed in bfloat16 or wider, within the bound.
No kernel may reach another device: no remote copies, remote signals or barrier semaphores. Data moves between devices by JAX's collectives and lax.ppermute only.
A program may use at most 192 MiB of HBM per device.

```python
import jax
import jax.numpy as jnp
from jax import lax

D = 4096
HEADS = 32
DK = 128
TOK_DEV = 1024
LENGTH = 8192


def levels(own_key, extent, cuts, smallest, top_value):
    def one(dim, parts):
        draws = jax.random.uniform(jax.random.fold_in(jax.random.fold_in(own_key, 6), dim), (parts,), jnp.float32, smallest / len(cuts), top_value / len(cuts))
        return jnp.repeat(jnp.exp(draws), extent[dim] // parts).reshape((-1,) + (1,) * (len(extent) - dim - 1))

    loudness = one(*cuts[0])
    for cut in cuts[1:]:
        loudness = loudness * one(*cut)
    return loudness


def scatter_about(rng, dims, width, most, cuts=(), held_as=jnp.bfloat16):
    entries = jax.random.normal(rng, dims, jnp.float32) * width
    if len(cuts) > 0:
        entries = levels(rng, dims, cuts, -0.22, 0.18) * entries
    return jnp.clip(entries, min=-most, max=most).astype(held_as)


def setup_inputs(seed: int = 0) -> dict:
    key_of = jax.random.split(jax.random.key(seed), 6)
    return {
        "queries": scatter_about(key_of[0], (LENGTH, HEADS, DK), 1.0, 6.0, ((0, 8), (1, 4))),
        "keys": scatter_about(key_of[1], (LENGTH, HEADS, DK), 1.0, 6.0, ((0, 8), (1, 4))),
        "values": scatter_about(key_of[2], (LENGTH, HEADS, DK), 1.0, 6.0, ((0, 8), (1, 4))),
        "d_layer": scatter_about(key_of[3], (LENGTH, D), 1.0, 6.0, ((0, 8), (1, 4))),
        "out_weight": scatter_about(key_of[4], (HEADS * DK, D), (HEADS * DK) ** -0.5, 0.09375, ((0, 4),)),
    }


def reference(queries, keys, values, d_layer, out_weight):
    flat = jnp.dot(d_layer, out_weight.T, preferred_element_type=jnp.float32)
    d_heads = flat.astype(jnp.bfloat16).reshape(LENGTH, HEADS, DK)
    position = jnp.arange(LENGTH, dtype=jnp.int32)
    scale = lax.rsqrt((DK * (position + 1)).astype(jnp.float32))
    grad_scaled = (d_heads.astype(jnp.float32) * scale[:, None, None]).astype(jnp.bfloat16)
    blocks = LENGTH // TOK_DEV

    def split(array):
        return array.reshape(blocks, TOK_DEV, HEADS, DK)
    q_b, k_b, v_b = (split(queries), split(keys), split(values))
    g_b, d_b = (split(grad_scaled), split(d_heads))
    key_state = jnp.einsum('nthd,nthe->nhde', k_b.astype(jnp.float32), v_b.astype(jnp.float32)).astype(jnp.bfloat16)
    query_state = jnp.einsum('nthd,nthe->nhde', q_b.astype(jnp.float32), g_b.astype(jnp.float32)).astype(jnp.bfloat16)
    zeros = jnp.zeros((1, HEADS, DK, DK), jnp.float32)
    prefix = jnp.concatenate([zeros, jnp.cumsum(key_state.astype(jnp.float32), axis=0)[:-1]], axis=0)
    suffix = jnp.cumsum(query_state.astype(jnp.float32)[::-1], axis=0)[::-1]
    suffix = jnp.concatenate([suffix[1:], zeros], axis=0)
    prefix = prefix.astype(jnp.bfloat16)
    suffix = suffix.astype(jnp.bfloat16)
    scale_b = scale.reshape(blocks, TOK_DEV)
    lower = jnp.tril(jnp.ones((TOK_DEV, TOK_DEV), dtype=bool))

    def one_block(items):
        q_j, k_j, v_j, g_j, d_j, p_j, r_j, c_j = items
        qf, kf, vf = (q_j.astype(jnp.float32), k_j.astype(jnp.float32), v_j.astype(jnp.float32))
        gf, df = (g_j.astype(jnp.float32), d_j.astype(jnp.float32))
        pf, rf = (p_j.astype(jnp.float32), r_j.astype(jnp.float32))
        score_grad = jnp.where(lower[None], jnp.einsum('thd,shd->hts', gf, vf), 0.0).astype(jnp.bfloat16).astype(jnp.float32)
        score_keys = jnp.where(lower[None], jnp.einsum('thd,shd->hts', qf, kf), 0.0).astype(jnp.bfloat16).astype(jnp.float32)
        d_q = c_j[:, None, None] * jnp.einsum('the,hde->thd', df, pf) + jnp.einsum('hts,shd->thd', score_grad, kf)
        d_k = jnp.einsum('hts,thd->shd', score_grad, qf) + jnp.einsum('she,hde->shd', vf, rf)
        d_v = jnp.einsum('hts,the->she', score_keys, gf) + jnp.einsum('shd,hde->she', kf, rf)
        return (d_q.astype(jnp.bfloat16), d_k.astype(jnp.bfloat16), d_v.astype(jnp.bfloat16))
    d_q, d_k, d_v = lax.map(one_block, (q_b, k_b, v_b, g_b, d_b, prefix, suffix, scale_b))
    return (d_q.reshape(LENGTH, HEADS, DK), d_k.reshape(LENGTH, HEADS, DK), d_v.reshape(LENGTH, HEADS, DK))
```

```python
import jax
import jax.numpy as jnp
from jax import lax
from jax.sharding import PartitionSpec as P

ROW_CHUNKS = 4


def swap(array, axis, size, bit):
    return lax.ppermute(array, axis, [(i, i ^ bit) for i in range(size)])


def gather_features(d_layer, size):
    rows = d_layer.shape[0] // ROW_CHUNKS
    held = [[d_layer[i * rows : (i + 1) * rows] for i in range(ROW_CHUNKS)]]
    bits = []
    bit = 1
    while bit < size:
        bits.append(bit)
        bit *= 2
    order = [0]
    top = bits[-1]
    across = [swap(c, "head", size, top) for c in held[0]]
    own = {0: held[0], top: across}
    for bit in bits[:-1]:
        for offset in list(own):
            own[offset ^ bit] = [swap(c, "head", size, bit) for c in own[offset]]
    return own


def shifted(array, size, step):
    return lax.ppermute(array, "ctx", [(i, i + step) for i in range(size) if 0 <= i + step < size])


def scan_states(state, size, direction):
    total = state.astype(jnp.float32)
    exclusive = jnp.zeros_like(total)
    step = 1
    while step < size:
        came = shifted(total.astype(jnp.bfloat16), size, direction * step).astype(jnp.float32)
        exclusive = exclusive + came
        total = total + came
        step *= 2
    return exclusive.astype(jnp.bfloat16)


def body(n_ctx, n_head, queries, keys, values, d_layer, out_weight):
    tokens, heads_local, head_dim = queries.shape
    features = d_layer.shape[1]
    mine = lax.axis_index("head")
    pieces = gather_features(d_layer, n_head)

    key_state = jnp.einsum("thd,the->hde", keys, values, preferred_element_type=jnp.float32).astype(
        jnp.bfloat16
    )
    prefix_low = scan_states(key_state, n_ctx, 1)

    def weight_of(offset):
        return lax.dynamic_slice_in_dim(out_weight, (mine ^ offset) * features, features, axis=1)

    weights = {offset: weight_of(offset) for offset in pieces}
    flat = []
    for i in range(ROW_CHUNKS):
        total = None
        for offset in pieces:
            part = lax.dot_general(
                pieces[offset][i], weights[offset], (((1,), (1,)), ((), ())), preferred_element_type=jnp.float32
            )
            total = part if total is None else total + part
        flat.append(total.astype(jnp.bfloat16))
    d_heads = jnp.concatenate(flat, axis=0).reshape(tokens, heads_local, head_dim)
    block_index = lax.axis_index("ctx")
    position = block_index * tokens + jnp.arange(tokens, dtype=jnp.int32)
    scale = lax.rsqrt((head_dim * (position + 1)).astype(jnp.float32))
    grad_scaled = (d_heads.astype(jnp.float32) * scale[:, None, None]).astype(jnp.bfloat16)
    query_state = jnp.einsum(
        "thd,the->hde", queries, grad_scaled, preferred_element_type=jnp.float32
    ).astype(jnp.bfloat16)
    suffix_low = scan_states(query_state, n_ctx, -1)
    lower = jnp.tril(jnp.ones((tokens, tokens), dtype=bool))[None]
    score_grad = jnp.where(
        lower,
        jnp.einsum("thd,shd->hts", grad_scaled, values, preferred_element_type=jnp.float32),
        0.0,
    ).astype(jnp.bfloat16)
    score_keys = jnp.where(
        lower, jnp.einsum("thd,shd->hts", queries, keys, preferred_element_type=jnp.float32), 0.0
    ).astype(jnp.bfloat16)
    d_queries = scale[:, None, None] * jnp.einsum(
        "the,hde->thd", d_heads, prefix_low, preferred_element_type=jnp.float32
    )
    d_queries = d_queries + jnp.einsum(
        "hts,shd->thd", score_grad, keys, preferred_element_type=jnp.float32
    )
    d_keys = jnp.einsum("hts,thd->shd", score_grad, queries, preferred_element_type=jnp.float32)
    d_keys = d_keys + jnp.einsum(
        "she,hde->shd", values, suffix_low, preferred_element_type=jnp.float32
    )
    d_values = jnp.einsum(
        "hts,the->she", score_keys, grad_scaled, preferred_element_type=jnp.float32
    )
    d_values = d_values + jnp.einsum(
        "shd,hde->she", keys, suffix_low, preferred_element_type=jnp.float32
    )
    return (
        d_queries.astype(jnp.bfloat16),
        d_keys.astype(jnp.bfloat16),
        d_values.astype(jnp.bfloat16),
    )


def solution(mesh):
    in_specs = (
        P("ctx", "head", None),
        P("ctx", "head", None),
        P("ctx", "head", None),
        P("ctx", "head"),
        P("head", None),
    )
    out_specs = (P("ctx", "head", None), P("ctx", "head", None), P("ctx", "head", None))

    def program(queries, keys, values, d_layer, out_weight):
        return body(mesh.shape["ctx"], mesh.shape["head"], queries, keys, values, d_layer, out_weight)

    return jax.shard_map(program, mesh=mesh, in_specs=in_specs, out_specs=out_specs, check_vma=False)
```

```python
import functools

import jax
import jax.numpy as jnp
from jax import lax
from jax.experimental import pallas as pl
from jax.experimental.pallas import tpu as pltpu
from jax.sharding import PartitionSpec as P

CHUNK = 256
PAIR = 2
F32 = jnp.float32
BF16 = jnp.bfloat16
NT = (((1,), (1,)), ((), ()))
NN = (((1,), (0,)), ((), ()))
TN = (((0,), (0,)), ((), ()))
VMEM_LIMIT = 40 * 1024 * 1024


def dot(a, b, dims):
    return lax.dot_general(a, b, dims, preferred_element_type=F32)


def params():
    return pltpu.CompilerParams(vmem_limit_bytes=VMEM_LIMIT)


def shape(dims, dtype):
    return jax.ShapeDtypeStruct(dims, dtype)


def prepare_kernel(heads, dk, half_ref, q_ref, k_ref, v_ref, qf_ref, kf_ref, vf_ref, before_ref, keep_ref, send_ref, wide, acc):
    step = pl.program_id(0)
    rows = qf_ref.shape[0]

    @pl.when(step == 0)
    def _():
        acc[...] = jnp.zeros_like(acc)

    for source, target in ((q_ref, qf_ref), (k_ref, kf_ref), (v_ref, vf_ref)):
        wide[...] = source[...].astype(F32)
        for h in range(heads):
            target[:, h * dk : (h + 1) * dk] = wide[pl.ds(h, rows, stride=heads), :].astype(BF16)
    before_ref[0] = acc[...]
    for h in range(heads):
        cols = slice(h * dk, (h + 1) * dk)
        acc[h] += dot(kf_ref[:, cols], vf_ref[:, cols], TN)

    @pl.when(step == pl.num_programs(0) - 1)
    def _():
        low, high = acc[: heads // 2].astype(BF16), acc[heads // 2 :].astype(BF16)
        first = half_ref[0] == 0
        keep_ref[...] = jnp.where(first, low, high)
        send_ref[...] = jnp.where(first, high, low)


def prepare(half, q, k, v, tokens, heads, dk):
    n = tokens // CHUNK
    raw = pl.BlockSpec((CHUNK * heads, dk), lambda i, s: (i, 0))
    flat = pl.BlockSpec((CHUNK, heads * dk), lambda i, s: (i, 0))
    part = pl.BlockSpec((heads // 2, dk, dk), lambda i, s: (0, 0, 0))
    width = heads * dk
    return pl.pallas_call(
        functools.partial(prepare_kernel, heads, dk),
        grid_spec=pltpu.PrefetchScalarGridSpec(
            num_scalar_prefetch=1,
            grid=(n,),
            in_specs=[raw] * 3,
            out_specs=[flat] * 3 + [pl.BlockSpec((1, heads, dk, dk), lambda i, s: (i, 0, 0, 0)), part, part],
            scratch_shapes=[pltpu.VMEM((CHUNK * heads, dk), F32), pltpu.VMEM((heads, dk, dk), F32)],
        ),
        out_shape=[shape((tokens, width), BF16)] * 3
        + [shape((n, heads, dk, dk), F32)]
        + [shape((heads // 2, dk, dk), BF16)] * 2,
        compiler_params=params(),
        cost_estimate=pl.CostEstimate(
            flops=4 * tokens * width * dk, bytes_accessed=12 * tokens * width + 4 * n * width * dk, transcendentals=0
        ),
        name="prepare",
    )(half, q, k, v)


def early_kernel(index_ref, a_ref, b_ref, wa_ref, wb_ref, out_ref):
    out_ref[...] = dot(a_ref[...], wa_ref[...], NT) + dot(b_ref[...], wb_ref[...], NT)


def early(index, a, b, weight):
    tokens, features = a.shape
    width = weight.shape[0]
    tile = 256
    whole = pl.BlockSpec((tokens, features), lambda j, s: (0, 0))
    return pl.pallas_call(
        early_kernel,
        grid_spec=pltpu.PrefetchScalarGridSpec(
            num_scalar_prefetch=1,
            grid=(width // tile,),
            in_specs=[
                whole,
                whole,
                pl.BlockSpec((tile, features), lambda j, s: (j, s[0])),
                pl.BlockSpec((tile, features), lambda j, s: (j, s[1])),
            ],
            out_specs=pl.BlockSpec((tokens, tile), lambda j, s: (0, j)),
        ),
        out_shape=shape((tokens, width), F32),
        compiler_params=params(),
        cost_estimate=pl.CostEstimate(
            flops=4 * tokens * features * width,
            bytes_accessed=4 * tokens * features + 4 * features * width + 4 * tokens * width,
            transcendentals=0,
        ),
        name="early",
    )(index, a, b, weight, weight)


def late_kernel(last, dk, index_ref, a_ref, b_ref, wa_ref, wb_ref, part_ref, scale_ref, q_ref, *refs):
    j = pl.program_id(0)
    state_ref, refs = (refs[0], refs[1:]) if len(refs) == (4 if last else 3) else (None, refs)
    d_ref = refs[0]
    full = part_ref[...] + dot(a_ref[...], wa_ref[...], NT) + dot(b_ref[...], wb_ref[...], NT)
    low = full.astype(BF16)
    d_ref[...] = low
    states = []
    for i in range(PAIR):
        cols = slice(i * dk, (i + 1) * dk)
        grad = (low[:, cols].astype(F32) * scale_ref[...]).astype(BF16)
        state = dot(q_ref[:, cols], grad, TN)
        states.append(state if state_ref is None else state + state_ref[i])
    if not last:
        for i in range(PAIR):
            refs[1][i] = states[i]
        return
    keep_ref, send_ref = refs[1:]
    steps = pl.num_programs(0) // 2
    place = lax.rem(j, steps) * PAIR
    mine = (j // steps) == index_ref[2]

    @pl.when(mine)
    def _():
        for i in range(PAIR):
            keep_ref[place + i] = states[i].astype(BF16)

    @pl.when(jnp.logical_not(mine))
    def _():
        for i in range(PAIR):
            send_ref[place + i] = states[i].astype(BF16)


def late(chunk, last, index, a, b, weight, part, scale, q, state, heads, dk):
    rows, features = a.shape
    width = weight.shape[0]
    tile = PAIR * dk
    whole = pl.BlockSpec((rows, features), lambda j, s: (0, 0))
    in_specs = [
        whole,
        whole,
        pl.BlockSpec((tile, features), lambda j, s: (j, s[0])),
        pl.BlockSpec((tile, features), lambda j, s: (j, s[1])),
        pl.BlockSpec((rows, tile), lambda j, s: (chunk, j)),
        pl.BlockSpec((rows, dk), lambda j, s: (chunk, 0)),
        pl.BlockSpec((rows, tile), lambda j, s: (chunk, j)),
    ]
    pair = pl.BlockSpec((PAIR, dk, dk), lambda j, s: (j, 0, 0))
    args = [a, b, weight, weight, part, scale, q]
    if state is not None:
        in_specs.append(pair)
        args.append(state)
    out_specs = [pl.BlockSpec((rows, tile), lambda j, s: (0, j))]
    out_shape = [shape((rows, width), BF16)]
    if last:
        out_specs += [pl.BlockSpec((heads // 2, dk, dk), lambda j, s: (0, 0, 0))] * 2
        out_shape += [shape((heads // 2, dk, dk), BF16)] * 2
    else:
        out_specs.append(pair)
        out_shape.append(shape((heads, dk, dk), F32))
    return pl.pallas_call(
        functools.partial(late_kernel, last, dk),
        grid_spec=pltpu.PrefetchScalarGridSpec(
            num_scalar_prefetch=1, grid=(width // tile,), in_specs=in_specs, out_specs=out_specs
        ),
        out_shape=out_shape,
        compiler_params=params(),
        cost_estimate=pl.CostEstimate(
            flops=4 * rows * features * width, bytes_accessed=4 * rows * features + 4 * features * width, transcendentals=0
        ),
        name="late",
    )(index, *args)


def within_kernel(heads, dk, index_ref, q_ref, k_ref, v_ref, d_ref, scale_ref, before_ref, own_ref, other_ref, *refs):
    j = pl.program_id(0)
    state_ref = refs[0]
    dq_ref, dk_ref, dv_ref, wide = refs[-4:]
    rows = q_ref.shape[0]
    mine = (j // (pl.num_programs(0) // 2)) == index_ref[2]
    t = lax.broadcasted_iota(jnp.int32, (rows, rows), 0)
    s = lax.broadcasted_iota(jnp.int32, (rows, rows), 1)
    lower = s <= t
    scale = scale_ref[...]
    for i in range(PAIR):
        cols = slice(i * dk, (i + 1) * dk)
        q, k, v, d = q_ref[:, cols], k_ref[:, cols], v_ref[:, cols], d_ref[:, cols]
        grad = (d.astype(F32) * scale).astype(BF16)
        score_grad = jnp.where(lower, dot(grad, v, NT), 0.0).astype(BF16)
        score_keys = jnp.where(lower, dot(q, k, NT), 0.0).astype(BF16)
        earlier = jnp.where(mine, own_ref[i], other_ref[i]).astype(F32) + before_ref[0, i]
        dq = scale * dot(d, earlier.astype(BF16), NT) + dot(score_grad, k, NN)
        dkey = dot(score_grad, q, TN)
        dval = dot(score_keys, grad, TN)
        if state_ref is not None:
            after = state_ref[i].astype(BF16)
            dkey = dkey + dot(v, after, NT)
            dval = dval + dot(k, after, NN)
        wide[pl.ds(j * PAIR + i, rows, stride=heads), :] = dq
        dk_ref[:, cols] = dkey.astype(BF16)
        dv_ref[:, cols] = dval.astype(BF16)

    @pl.when(j == pl.num_programs(0) - 1)
    def _():
        dq_ref[...] = wide[...].astype(BF16)


def within(chunk, index, q, k, v, d, scale, before, own, other, state, held, heads, dk):
    tokens, width = q.shape
    rows = CHUNK
    tile = PAIR * dk
    half_steps = heads // (2 * PAIR)
    block = pl.BlockSpec((rows, tile), lambda j, s: (chunk, j))
    pair = pl.BlockSpec((PAIR, dk, dk), lambda j, s: (j, 0, 0))
    half_pair = pl.BlockSpec((PAIR, dk, dk), lambda j, s: (lax.rem(j, half_steps), 0, 0))
    in_specs = [
        block,
        block,
        block,
        pl.BlockSpec((rows, tile), lambda j, s: (0, j)),
        pl.BlockSpec((rows, dk), lambda j, s: (chunk, 0)),
        pl.BlockSpec((1, PAIR, dk, dk), lambda j, s: (chunk, j, 0, 0)),
        half_pair,
        half_pair,
    ]
    args = [q, k, v, d, scale, before, own, other]
    kernel = functools.partial(within_kernel, heads, dk)
    if state is not None:
        in_specs.append(pair)
        args.append(state)
    else:
        inner = kernel

        def kernel(*refs):
            inner(*refs[:9], None, *refs[9:])

    aliases = {}
    if held is not None:
        for out, array in enumerate(held):
            aliases[1 + len(args)] = out
            args.append(array)
            in_specs.append(pl.BlockSpec(memory_space=pl.ANY))
    return pl.pallas_call(
        kernel,
        grid_spec=pltpu.PrefetchScalarGridSpec(
            num_scalar_prefetch=1,
            grid=(width // tile,),
            in_specs=in_specs,
            out_specs=[pl.BlockSpec((rows * heads, dk), lambda j, s: (chunk, 0)), block, block],
            scratch_shapes=[pltpu.VMEM((rows * heads, dk), F32)],
        ),
        out_shape=[shape((tokens * heads, dk), BF16)] + [shape((tokens, width), BF16)] * 2,
        input_output_aliases=aliases,
        compiler_params=params(),
        cost_estimate=pl.CostEstimate(
            flops=16 * rows * rows * width, bytes_accessed=14 * rows * width, transcendentals=0
        ),
        name="within",
    )(index, *args)


def finish_kernel(heads, dk, index_ref, k_ref, v_ref, dkp_ref, dvp_ref, own_ref, other_ref, dk_ref, dv_ref, wide_k, wide_v):
    rows = k_ref.shape[0]
    first = index_ref[2] == 0
    half = heads // 2
    for h in range(heads):
        cols = slice(h * dk, (h + 1) * dk)
        own, other = own_ref[h % half], other_ref[h % half]
        after = jnp.where(first, own, other) if h < half else jnp.where(first, other, own)
        wide_k[pl.ds(h, rows, stride=heads), :] = dkp_ref[:, cols].astype(F32) + dot(v_ref[:, cols], after, NT)
        wide_v[pl.ds(h, rows, stride=heads), :] = dvp_ref[:, cols].astype(F32) + dot(k_ref[:, cols], after, NN)
    dk_ref[...] = wide_k[...].astype(BF16)
    dv_ref[...] = wide_v[...].astype(BF16)


def finish(index, k, v, dkp, dvp, own, other, heads, dk):
    tokens, width = k.shape
    rows = 128
    block = pl.BlockSpec((rows, width), lambda i, s: (i, 0))
    part = pl.BlockSpec((heads // 2, dk, dk), lambda i, s: (0, 0, 0))
    out = pl.BlockSpec((rows * heads, dk), lambda i, s: (i, 0))
    return pl.pallas_call(
        functools.partial(finish_kernel, heads, dk),
        grid_spec=pltpu.PrefetchScalarGridSpec(
            num_scalar_prefetch=1,
            grid=(tokens // rows,),
            in_specs=[block] * 4 + [part] * 2,
            out_specs=[out, out],
            scratch_shapes=[pltpu.VMEM((rows * heads, dk), F32)] * 2,
        ),
        out_shape=[shape((tokens * heads, dk), BF16)] * 2,
        compiler_params=params(),
        cost_estimate=pl.CostEstimate(
            flops=4 * tokens * width * dk, bytes_accessed=12 * tokens * width, transcendentals=0
        ),
        name="finish",
    )(index, k, v, dkp, dvp, own, other)


def swap(array, axis, size, bit):
    return lax.ppermute(array, axis, [(i, i ^ bit) for i in range(size)])


def shifted(array, size, step):
    return lax.ppermute(array, "ctx", [(i, i + step) for i in range(size) if 0 <= i + step < size])


def scan_states(keep, send, size, odd, direction):
    came = swap(send, "ctx", size, 1)
    own = keep.astype(F32)
    total = own + came.astype(F32)
    exclusive = jnp.zeros_like(total)
    step = 2
    while step < size:
        got = shifted(total.astype(BF16), size, direction * step).astype(F32)
        exclusive = exclusive + got
        total = total + got
        step *= 2
    later = odd if direction == 1 else jnp.logical_not(odd)
    other = swap((exclusive + jnp.where(later, 0.0, own)).astype(BF16), "ctx", size, 1)
    mine = exclusive + jnp.where(later, came.astype(F32), 0.0)
    return mine.astype(BF16), other


def body(n_ctx, n_head, queries, keys, values, d_layer, out_weight):
    tokens, heads, dk = queries.shape
    n = tokens // CHUNK
    block = lax.axis_index("ctx").astype(jnp.int32)
    place = lax.axis_index("head").astype(jnp.int32)
    odd = (block & 1) == 1
    half = (block & 1).astype(jnp.int32)

    near = n_head // 2
    far = 1
    order = list(range(n))[::-1]
    across = {c: swap(d_layer[c * CHUNK : (c + 1) * CHUNK], "head", n_head, near) for c in order}
    beside = swap(d_layer, "head", n_head, far)
    both = {c: swap(across[c], "head", n_head, far) for c in order}

    position = block * tokens + jnp.arange(tokens, dtype=jnp.int32)
    scale = lax.rsqrt((dk * (position + 1)).astype(F32))
    scale = jnp.broadcast_to(scale[:, None], (tokens, dk))

    flat = (tokens * heads, dk)
    q, k, v, before, keep, send = prepare(
        half[None], queries.reshape(flat), keys.reshape(flat), values.reshape(flat), tokens, heads, dk
    )
    own_prefix, other_prefix = scan_states(keep, send, n_ctx, odd, 1)

    part = early(jnp.stack([place, place ^ far]), d_layer, beside, out_weight)
    index = jnp.stack([place ^ near, place ^ near ^ far, half])
    state = None
    d, after = {}, {}
    for c in order:
        after[c] = state
        result = late(c, c == 0, index, across[c], both[c], out_weight, part, scale, q, state, heads, dk)
        if c == 0:
            d[c], keep, send = result
        else:
            d[c], state = result
    own_suffix, other_suffix = scan_states(keep, send, n_ctx, odd, -1)
    held = None
    for c in order:
        held = within(c, index, q, k, v, d[c], scale, before, own_prefix, other_prefix, after[c], held, heads, dk)
    d_queries, dk_part, dv_part = held
    d_keys, d_values = finish(index, k, v, dk_part, dv_part, own_suffix, other_suffix, heads, dk)
    return tuple(a.reshape(tokens, heads, dk) for a in (d_queries, d_keys, d_values))


def solution(mesh):
    in_specs = (
        P("ctx", "head", None),
        P("ctx", "head", None),
        P("ctx", "head", None),
        P("ctx", "head"),
        P("head", None),
    )
    out_specs = (P("ctx", "head", None), P("ctx", "head", None), P("ctx", "head", None))

    def program(queries, keys, values, d_layer, out_weight):
        return body(mesh.shape["ctx"], mesh.shape["head"], queries, keys, values, d_layer, out_weight)

    return jax.shard_map(program, mesh=mesh, in_specs=in_specs, out_specs=out_specs, check_vma=False)
```

```python
import functools

import jax
import jax.numpy as jnp
from jax import lax
from jax.experimental import pallas as pl
from jax.experimental.pallas import tpu as pltpu
from jax.sharding import PartitionSpec as P

CHUNK = 256
PAIR = 2
F32 = jnp.float32
BF16 = jnp.bfloat16
NT = (((1,), (1,)), ((), ()))
NN = (((1,), (0,)), ((), ()))
TN = (((0,), (0,)), ((), ()))
VMEM_LIMIT = 20 * 1024 * 1024
TOKEN = (8, 128)
FREE = pl.CostEstimate(flops=0, bytes_accessed=0, transcendentals=0)


def dot(a, b, dims):
    return lax.dot_general(a, b, dims, preferred_element_type=F32)


def params():
    return pltpu.CompilerParams(vmem_limit_bytes=VMEM_LIMIT)


def shape(dims, dtype):
    return jax.ShapeDtypeStruct(dims, dtype)


def hbm(*arrays):
    return [pltpu.with_memory_space_constraint(a, pltpu.HBM) for a in arrays]


def prepare_kernel(
    heads, dk, half_ref, q_ref, k_ref, v_ref, qf_ref, kf_ref, vf_ref, qt_ref, vt_ref, before_ref, keep_ref, send_ref, token_ref, wide, acc
):
    step = pl.program_id(0)
    rows = qf_ref.shape[0]

    @pl.when(step == 0)
    def _():
        acc[...] = jnp.zeros_like(acc)
        token_ref[...] = jnp.zeros_like(token_ref)

    before_ref[0] = acc[...]
    for source, target, turned in ((k_ref, kf_ref, None), (v_ref, vf_ref, vt_ref), (q_ref, qf_ref, qt_ref)):
        wide[...] = source[...].astype(F32)
        for h in range(heads):
            cols = slice(h * dk, (h + 1) * dk)
            one = wide[pl.ds(h, rows, stride=heads), :].astype(BF16)
            target[:, cols] = one
            if turned is not None:
                turned[cols, :] = one.T
            if turned is vt_ref:
                acc[h] += dot(vt_ref[cols, :], kf_ref[:, cols], NN)

    @pl.when(step == pl.num_programs(0) - 1)
    def _():
        low, high = acc[: heads // 2].astype(BF16), acc[heads // 2 :].astype(BF16)
        first = half_ref[0] == 0
        keep_ref[...] = jnp.where(first, low, high)
        send_ref[...] = jnp.where(first, high, low)


def prepare(half, q, k, v, tokens, heads, dk):
    n = tokens // CHUNK
    raw = pl.BlockSpec((CHUNK * heads, dk), lambda i, s: (i, 0))
    flat = pl.BlockSpec((CHUNK, heads * dk), lambda i, s: (i, 0))
    turned = pl.BlockSpec((heads * dk, CHUNK), lambda i, s: (0, i))
    part = pl.BlockSpec((heads // 2, dk, dk), lambda i, s: (0, 0, 0))
    width = heads * dk
    return pl.pallas_call(
        functools.partial(prepare_kernel, heads, dk),
        grid_spec=pltpu.PrefetchScalarGridSpec(
            num_scalar_prefetch=1,
            grid=(n,),
            in_specs=[raw] * 3,
            out_specs=[flat] * 3
            + [turned] * 2
            + [pl.BlockSpec((1, heads, dk, dk), lambda i, s: (i, 0, 0, 0)), part, part, pl.BlockSpec(TOKEN, lambda i, s: (0, 0))],
            scratch_shapes=[pltpu.VMEM((CHUNK * heads, dk), F32), pltpu.VMEM((heads, dk, dk), F32)],
        ),
        out_shape=[pltpu.HBM((tokens, width), BF16)] * 3
        + [pltpu.HBM((width, tokens), BF16)] * 2
        + [pltpu.HBM((n, heads, dk, dk), F32)]
        + [shape((heads // 2, dk, dk), BF16)] * 2
        + [shape(TOKEN, F32)],
        compiler_params=params(),
        cost_estimate=FREE,
        name="prepare",
    )(half, *hbm(q, k, v))


def early_kernel(index_ref, a_ref, b_ref, wa_ref, wb_ref, after_ref, out_ref, token_ref):
    token_ref[...] = jnp.zeros_like(token_ref)
    out_ref[...] = dot(a_ref[...], wa_ref[...], NT) + dot(b_ref[...], wb_ref[...], NT)


def early(index, a, b, weight, token):
    tokens, features = a.shape
    width = weight.shape[0]
    tile = 256
    whole = pl.BlockSpec((tokens, features), lambda j, s: (0, 0))
    return pl.pallas_call(
        early_kernel,
        grid_spec=pltpu.PrefetchScalarGridSpec(
            num_scalar_prefetch=1,
            grid=(width // tile,),
            in_specs=[
                whole,
                whole,
                pl.BlockSpec((tile, features), lambda j, s: (j, s[0])),
                pl.BlockSpec((tile, features), lambda j, s: (j, s[1])),
                pl.BlockSpec(memory_space=pl.ANY),
            ],
            out_specs=[pl.BlockSpec((tokens, tile), lambda j, s: (0, j)), pl.BlockSpec(TOKEN, lambda j, s: (0, 0))],
        ),
        out_shape=[pltpu.HBM((tokens, width), F32), shape(TOKEN, F32)],
        compiler_params=params(),
        cost_estimate=FREE,
        name="early",
    )(index, *hbm(a), b, *hbm(weight, weight), token)


def late_kernel(last, first, dk, index_ref, a_ref, b_ref, wa_ref, wb_ref, part_ref, scale_ref, qt_ref, after_ref, *refs):
    j = pl.program_id(0)
    state_ref, refs = (None, refs) if first else (refs[0], refs[1:])
    refs, token_ref, at, bt = refs[:-3], refs[-3], refs[-2], refs[-1]
    d_ref = refs[0]

    @pl.when(j == 0)
    def _():
        token_ref[...] = jnp.zeros_like(token_ref)
        at[...] = a_ref[...].T
        bt[...] = b_ref[...].T

    turned = dot(wa_ref[...], at[...], NN) + dot(wb_ref[...], bt[...], NN)
    low = (part_ref[...] + turned.T).astype(BF16)
    d_ref[...] = low
    states = [None if first else state_ref[0, i] for i in range(PAIR)]
    for c in reversed(range(low.shape[0] // CHUNK)):
        rows = slice(c * CHUNK, (c + 1) * CHUNK)
        for i in range(PAIR):
            cols = slice(i * dk, (i + 1) * dk)
            grad = (low[rows, cols].astype(F32) * scale_ref[rows, :]).astype(BF16)
            state = dot(qt_ref[cols, rows], grad, NN)
            states[i] = state if states[i] is None else states[i] + state
            if not last:
                refs[1][c, i] = states[i]
    if not last:
        return
    keep_ref, send_ref = refs[1:]
    steps = pl.num_programs(0) // 2
    place = lax.rem(j, steps) * PAIR
    mine = (j // steps) == index_ref[2]

    @pl.when(mine)
    def _():
        for i in range(PAIR):
            keep_ref[place + i] = states[i].astype(BF16)

    @pl.when(jnp.logical_not(mine))
    def _():
        for i in range(PAIR):
            send_ref[place + i] = states[i].astype(BF16)


def late(start, last, index, a, b, weight, part, scale, qt, token, state, heads, dk):
    rows, features = a.shape
    width = weight.shape[0]
    tile = PAIR * dk
    m = rows // CHUNK
    here = start // rows
    whole = pl.BlockSpec((rows, features), lambda j, s: (0, 0))
    in_specs = [
        whole,
        whole,
        pl.BlockSpec((tile, features), lambda j, s: (j, s[0])),
        pl.BlockSpec((tile, features), lambda j, s: (j, s[1])),
        pl.BlockSpec((rows, tile), lambda j, s: (here, j)),
        pl.BlockSpec((rows, dk), lambda j, s: (here, 0)),
        pl.BlockSpec((tile, rows), lambda j, s: (j, here)),
        pl.BlockSpec(memory_space=pl.ANY),
    ]
    args = [a, b, *hbm(weight, weight, part), scale, *hbm(qt), token]
    if state is not None:
        in_specs.append(pl.BlockSpec((1, PAIR, dk, dk), lambda j, s: (0, j, 0, 0)))
        args += hbm(state)
    out_specs = [pl.BlockSpec((rows, tile), lambda j, s: (0, j))]
    out_shape = [pltpu.HBM((rows, width), BF16)]
    if last:
        out_specs += [pl.BlockSpec((heads // 2, dk, dk), lambda j, s: (0, 0, 0))] * 2
        out_shape += [shape((heads // 2, dk, dk), BF16)] * 2
    else:
        out_specs.append(pl.BlockSpec((m, PAIR, dk, dk), lambda j, s: (0, j, 0, 0)))
        out_shape.append(pltpu.HBM((m, heads, dk, dk), F32))
    out_specs.append(pl.BlockSpec(TOKEN, lambda j, s: (0, 0)))
    out_shape.append(shape(TOKEN, F32))
    return pl.pallas_call(
        functools.partial(late_kernel, last, state is None, dk),
        grid_spec=pltpu.PrefetchScalarGridSpec(
            num_scalar_prefetch=1,
            grid=(width // tile,),
            in_specs=in_specs,
            out_specs=out_specs,
            scratch_shapes=[pltpu.VMEM((features, rows), BF16)] * 2,
        ),
        out_shape=out_shape,
        compiler_params=params(),
        cost_estimate=FREE,
        name="late",
    )(index, *args)


def within_kernel(
    heads, dk, first, index_ref, q_ref, k_ref, v_ref, qt_ref, vt_ref, d_ref, scale_ref, before_ref, own_ref, other_ref, after_ref, *refs
):
    j = pl.program_id(0)
    dq_ref, dk_ref, dv_ref, token_ref, wide = refs[-5:]
    rows = q_ref.shape[0]
    mine = (j // (pl.num_programs(0) // 2)) == index_ref[2]
    t = lax.broadcasted_iota(jnp.int32, (rows, rows), 0)
    s = lax.broadcasted_iota(jnp.int32, (rows, rows), 1)
    lower = s <= t
    upper = t <= s
    scale = scale_ref[...]
    for i in range(PAIR):
        cols = slice(i * dk, (i + 1) * dk)
        q, k, v, d = q_ref[:, cols], k_ref[:, cols], v_ref[:, cols], d_ref[:, cols]
        grad = (d.astype(F32) * scale).astype(BF16)
        score_grad = jnp.where(lower, dot(grad, vt_ref[cols, :], NN), 0.0).astype(BF16)
        score_grad_t = jnp.where(upper, dot(v, grad, NT), 0.0).astype(BF16)
        score_keys_t = jnp.where(upper, dot(k, qt_ref[cols, :], NN), 0.0).astype(BF16)
        earlier = jnp.where(mine, own_ref[i], other_ref[i]).astype(F32) + before_ref[0, i]
        dq = scale * dot(d, earlier.astype(BF16), NN) + dot(score_grad, k, NN)
        dkey = dot(score_grad_t, q, NN)
        dval = dot(score_keys_t, grad, NN)
        if not first:
            after = refs[0][0, i].astype(BF16)
            dkey = dkey + dot(v, after, NT)
            dval = dval + dot(k, after, NN)
        wide[pl.ds(j * PAIR + i, rows, stride=heads), :] = dq
        dk_ref[:, cols] = dkey.astype(BF16)
        dv_ref[:, cols] = dval.astype(BF16)

    @pl.when(j == pl.num_programs(0) - 1)
    def _():
        dq_ref[...] = wide[...].astype(BF16)
        token_ref[...] = jnp.zeros_like(token_ref)


def within(chunk, index, q, k, v, qt, vt, d, scale, before, own, other, token, at, state, held, heads, dk):
    tokens, width = q.shape
    rows = CHUNK
    tile = PAIR * dk
    half_steps = heads // (2 * PAIR)
    block = pl.BlockSpec((rows, tile), lambda j, s: (chunk, j))
    turned = pl.BlockSpec((tile, rows), lambda j, s: (j, chunk))
    half_pair = pl.BlockSpec((PAIR, dk, dk), lambda j, s: (lax.rem(j, half_steps), 0, 0))
    in_specs = [block] * 3 + [turned] * 2
    in_specs += [
        pl.BlockSpec((rows, tile), lambda j, s: (at, j)),
        pl.BlockSpec((rows, dk), lambda j, s: (chunk, 0)),
        pl.BlockSpec((1, PAIR, dk, dk), lambda j, s: (chunk, j, 0, 0)),
        half_pair,
        half_pair,
        pl.BlockSpec(memory_space=pl.ANY),
    ]
    args = [*hbm(q, k, v, qt, vt, d), scale, *hbm(before), own, other, token]
    if state is not None:
        level = state[1]
        in_specs.append(pl.BlockSpec((1, PAIR, dk, dk), lambda j, s: (level, j, 0, 0)))
        args += hbm(state[0])
    aliases = {}
    if held is not None:
        for out, array in enumerate(held):
            aliases[1 + len(args)] = out
            args += hbm(array)
            in_specs.append(pl.BlockSpec(memory_space=pl.ANY))
    return pl.pallas_call(
        functools.partial(within_kernel, heads, dk, state is None),
        grid_spec=pltpu.PrefetchScalarGridSpec(
            num_scalar_prefetch=1,
            grid=(width // tile,),
            in_specs=in_specs,
            out_specs=[
                pl.BlockSpec((rows * heads, dk), lambda j, s: (chunk, 0)),
                block,
                block,
                pl.BlockSpec(TOKEN, lambda j, s: (0, 0)),
            ],
            scratch_shapes=[pltpu.VMEM((rows * heads, dk), F32)],
        ),
        out_shape=[pltpu.HBM((tokens * heads, dk), BF16)]
        + [pltpu.HBM((tokens, width), BF16)] * 2
        + [shape(TOKEN, F32)],
        input_output_aliases=aliases,
        compiler_params=params(),
        cost_estimate=FREE,
        name="within",
    )(index, *args)


def finish_kernel(
    heads, dk, index_ref, k_ref, v_ref, dkp_ref, dvp_ref, own_ref, other_ref, after_ref, dk_ref, dv_ref, wide_k, wide_v, after, turned
):
    rows = k_ref.shape[0]
    half = heads // 2

    @pl.when(pl.program_id(0) == 0)
    def _():
        first = index_ref[2] == 0
        for h in range(heads):
            own, other = own_ref[h % half], other_ref[h % half]
            one = jnp.where(first, own, other) if h < half else jnp.where(first, other, own)
            after[h] = one
            turned[h] = one.T

    for h in range(heads):
        cols = slice(h * dk, (h + 1) * dk)
        wide_k[pl.ds(h, rows, stride=heads), :] = dkp_ref[:, cols].astype(F32) + dot(v_ref[:, cols], turned[h], NN)
        wide_v[pl.ds(h, rows, stride=heads), :] = dvp_ref[:, cols].astype(F32) + dot(k_ref[:, cols], after[h], NN)
    dk_ref[...] = wide_k[...].astype(BF16)
    dv_ref[...] = wide_v[...].astype(BF16)


def finish(index, k, v, dkp, dvp, own, other, token, heads, dk):
    tokens, width = k.shape
    rows = CHUNK
    block = pl.BlockSpec((rows, width), lambda i, s: (i, 0))
    part = pl.BlockSpec((heads // 2, dk, dk), lambda i, s: (0, 0, 0))
    out = pl.BlockSpec((rows * heads, dk), lambda i, s: (i, 0))
    return pl.pallas_call(
        functools.partial(finish_kernel, heads, dk),
        grid_spec=pltpu.PrefetchScalarGridSpec(
            num_scalar_prefetch=1,
            grid=(tokens // rows,),
            in_specs=[block] * 4 + [part] * 2 + [pl.BlockSpec(memory_space=pl.ANY)],
            out_specs=[out, out],
            scratch_shapes=[pltpu.VMEM((rows * heads, dk), F32)] * 2 + [pltpu.VMEM((heads, dk, dk), BF16)] * 2,
        ),
        out_shape=[shape((tokens * heads, dk), BF16)] * 2,
        compiler_params=params(),
        cost_estimate=FREE,
        name="finish",
    )(index, *hbm(k, v, dkp, dvp), own, other, token)


def swap(array, axis, size, bit):
    return lax.ppermute(array, axis, [(i, i ^ bit) for i in range(size)])


def shifted(array, size, step):
    return lax.ppermute(array, "ctx", [(i, i + step) for i in range(size) if 0 <= i + step < size])


class Order:
    def __init__(self):
        self.token = None

    def tie(self, array):
        array, self.token = lax.optimization_barrier((array, self.token))
        return array


def scan_states(keep, send, size, odd, direction, order):
    came = swap(send, "ctx", size, 1)
    yield None
    own = keep.astype(F32)
    total = own + came.astype(F32)
    exclusive = jnp.zeros_like(total)
    step = 2
    while step < size:
        got = shifted(order.tie(total.astype(BF16)), size, direction * step).astype(F32)
        yield None
        exclusive = exclusive + got
        total = total + got
        step *= 2
    later = odd if direction == 1 else jnp.logical_not(odd)
    low = (exclusive + jnp.where(later, 0.0, own)).astype(BF16)
    other = swap(order.tie(low), "ctx", size, 1)
    mine = exclusive + jnp.where(later, came.astype(F32), 0.0)
    yield mine.astype(BF16), other


def body(n_ctx, n_head, queries, keys, values, d_layer, out_weight):
    tokens, heads, dk = queries.shape
    n = tokens // CHUNK
    block = lax.axis_index("ctx").astype(jnp.int32)
    place = lax.axis_index("head").astype(jnp.int32)
    odd = (block & 1) == 1
    half = (block & 1).astype(jnp.int32)

    near = n_head // 2
    far = 1
    groups = [(n // 2, n - n // 2)] + [(c, 1) for c in reversed(range(n // 2))]
    across = {}
    source = d_layer
    for c, m in groups:
        across[c] = swap(source[c * CHUNK : (c + m) * CHUNK], "head", n_head, near)
        source = lax.optimization_barrier(d_layer) if (c, m) == groups[0] else source
    beside = swap(d_layer, "head", n_head, far)

    position = block * tokens + jnp.arange(tokens, dtype=jnp.int32)
    scale = lax.rsqrt((dk * (position + 1)).astype(F32))
    scale = jnp.broadcast_to(scale[:, None], (tokens, dk))
    index = jnp.stack([place ^ near, place ^ near ^ far, half])

    order = Order()
    flat = (tokens * heads, dk)
    q, k, v, qt, vt, before, keep, send, order.token = prepare(
        half[None], queries.reshape(flat), keys.reshape(flat), values.reshape(flat), tokens, heads, dk
    )
    forward = scan_states(keep, send, n_ctx, odd, 1, order)
    next(forward)
    part, order.token = early(jnp.stack([place, place ^ far]), d_layer, beside, out_weight, order.token)

    prefix = state = held = None
    d, after = {}, {}

    def inner(c):
        nonlocal held
        *held, order.token = within(
            c, index, q, k, v, qt, vt, d[c][0], scale, before, *prefix, order.token, d[c][1], after[c], held, heads, dk
        )

    def outer(c, m):
        nonlocal state, keep, send, prefix
        after[c + m - 1] = None if state is None else (state, 0)
        piece = order.tie(across[c])
        both = swap(piece, "head", n_head, far)
        if prefix is None:
            prefix = next(forward)
        while prefix is None and state is not None:
            prefix = next(forward)
        out = late(c * CHUNK, c == 0, index, piece, both, out_weight, part, scale, qt, order.token, state, heads, dk)
        order.token = out[-1]
        if c == 0:
            keep, send = out[1:3]
        else:
            state = out[1]
        for i in range(m):
            d[c + i] = (out[0], i)
            if i < m - 1:
                after[c + i] = (state, i + 1)

    waiting = []
    for c, m in groups:
        outer(c, m)
        waiting += list(range(c, c + m))[::-1]
        if prefix is None:
            prefix = next(forward)
        elif c != 0:
            while len(waiting) > 1:
                inner(waiting.pop(0))
    backward = scan_states(keep, send, n_ctx, odd, -1, order)
    next(backward)
    suffix = None
    while suffix is None:
        suffix = next(backward)
        if waiting:
            inner(waiting.pop(0))
    while waiting:
        inner(waiting.pop(0))
    d_queries, dk_part, dv_part = held
    d_keys, d_values = finish(index, k, v, dk_part, dv_part, *suffix, order.token, heads, dk)
    return tuple(a.reshape(tokens, heads, dk) for a in (d_queries, d_keys, d_values))


def solution(mesh):
    in_specs = (
        P("ctx", "head", None),
        P("ctx", "head", None),
        P("ctx", "head", None),
        P("ctx", "head"),
        P("head", None),
    )
    out_specs = (P("ctx", "head", None), P("ctx", "head", None), P("ctx", "head", None))

    def program(queries, keys, values, d_layer, out_weight):
        return body(mesh.shape["ctx"], mesh.shape["head"], queries, keys, values, d_layer, out_weight)

    return jax.shard_map(program, mesh=mesh, in_specs=in_specs, out_specs=out_specs, check_vma=False)
```

```python
import functools

import jax
import jax.numpy as jnp
from jax import lax
from jax.experimental import pallas as pl
from jax.experimental.pallas import tpu as pltpu
from jax.sharding import PartitionSpec as P

CHUNK = 256
PAIR = 2
GROUP = 4
F32 = jnp.float32
BF16 = jnp.bfloat16
TOKEN = (8, 128)
NT = (((1,), (1,)), ((), ()))
NN = (((1,), (0,)), ((), ()))
FREE = pl.CostEstimate(flops=0, bytes_accessed=0, transcendentals=0)
VMEM_LIMIT = 14 * 1024 * 1024
WHOLE = pl.BlockSpec(memory_space=pltpu.VMEM)
SCALARS = pl.BlockSpec(memory_space=pltpu.SMEM)
ANYWHERE = pl.BlockSpec(memory_space=pl.ANY)


def dot(a, b, dims):
    return lax.dot_general(a, b, dims, preferred_element_type=F32)


def shape(dims, dtype):
    return jax.ShapeDtypeStruct(dims, dtype)


def outside(*arrays):
    return [pltpu.with_memory_space_constraint(a, pltpu.HBM) for a in arrays]


def part_of(i, size):
    return pl.ds(pl.multiple_of(i * size, size), size)


def call(kernel, name, args, in_specs, out_shape, out_specs, scratch=()):
    return pl.pallas_call(
        kernel,
        in_specs=in_specs,
        out_specs=out_specs,
        out_shape=out_shape,
        scratch_shapes=scratch,
        compiler_params=pltpu.CompilerParams(vmem_limit_bytes=VMEM_LIMIT),
        cost_estimate=FREE,
        name=name,
    )(*args)


def cut_kernel(starts, source, *refs):
    pieces, token_ref, sem = refs[: len(starts)], refs[-2], refs[-1]
    token_ref[...] = jnp.zeros_like(token_ref)
    copies = [
        pltpu.make_async_copy(source.at[pl.ds(start, piece.shape[0])], piece, sem.at[i])
        for i, (start, piece) in enumerate(zip(starts, pieces))
    ]
    for copy in copies:
        copy.start()
    for copy in copies:
        copy.wait()


def cut(d_layer, groups):
    features = d_layer.shape[1]
    return call(
        functools.partial(cut_kernel, [c * CHUNK for c, _ in groups]),
        "cut",
        outside(d_layer),
        [ANYWHERE],
        [shape((m * CHUNK, features), d_layer.dtype) for _, m in groups] + [shape(TOKEN, F32)],
        [WHOLE] * (len(groups) + 1),
        [pltpu.SemaphoreType.DMA((len(groups),))],
    )


def prepare_kernel(
    heads, dk, half_ref, q_ref, k_ref, v_ref, _, qf_ref, kf_ref, vf_ref, qt_ref, vt_ref, before_ref, keep_ref, send_ref, token_ref,
    raw, wides, acc, sem
):
    n = qf_ref.shape[0] // CHUNK

    def load(i, c):
        source = (q_ref, k_ref, v_ref)[i].at[part_of(c, CHUNK * heads)]
        return pltpu.make_async_copy(source, raw.at[i, c], sem.at[i, c])

    for c in range(n):
        for i in range(3):
            load(i, c).start()
    token_ref[...] = jnp.zeros_like(token_ref)
    acc[...] = jnp.zeros_like(acc)

    def one_chunk(c, _):
        rows = part_of(c, CHUNK)
        before_ref[c] = acc[...]
        for i in range(3):
            load(i, c).wait()
            wides[i] = raw[i, c].astype(F32)
        for h in range(heads):
            cols = slice(h * dk, (h + 1) * dk)
            mine = pl.ds(h, CHUNK, stride=heads)
            q, k, v = (wides[i, mine, :].astype(BF16) for i in range(3))
            qf_ref[rows, cols] = q
            kf_ref[rows, cols] = k
            vf_ref[rows, cols] = v
            qt_ref[cols, rows] = q.T
            vt = v.T
            vt_ref[cols, rows] = vt
            acc[h] += dot(vt, k, NN)
        return 0

    lax.fori_loop(0, n, one_chunk, 0)
    low, high = acc[: heads // 2].astype(BF16), acc[heads // 2 :].astype(BF16)
    first = half_ref[0] == 0
    keep_ref[...] = jnp.where(first, low, high)
    send_ref[...] = jnp.where(first, high, low)


def prepare(half, q, k, v, token, tokens, heads, dk):
    n = tokens // CHUNK
    width = heads * dk
    return call(
        functools.partial(prepare_kernel, heads, dk),
        "prepare",
        [half, *outside(q, k, v), token],
        [SCALARS] + [ANYWHERE] * 4,
        [shape((tokens, width), BF16)] * 3
        + [shape((width, tokens), BF16)] * 2
        + [shape((n, heads, dk, dk), F32)]
        + [shape((heads // 2, dk, dk), BF16)] * 2
        + [shape(TOKEN, F32)],
        [WHOLE] * 9,
        [
            pltpu.VMEM((3, n, CHUNK * heads, dk), BF16),
            pltpu.VMEM((3, CHUNK * heads, dk), F32),
            pltpu.VMEM((heads, dk, dk), F32),
            pltpu.SemaphoreType.DMA((3, n)),
        ],
    )


def early_kernel(starts, index_ref, *refs):
    pieces, (b_ref, w_ref, _, out_ref, token_ref) = refs[: len(starts)], refs[len(starts) :]
    token_ref[...] = jnp.zeros_like(token_ref)
    features = b_ref.shape[1]
    first, second = part_of(index_ref[0], features), part_of(index_ref[1], features)

    def one_tile(j, _):
        tile = part_of(j, PAIR * 128)
        wa, wb = w_ref[tile, first].T, w_ref[tile, second].T
        for start, piece in zip(starts, pieces):
            rows = slice(start, start + piece.shape[0])
            out_ref[rows, tile] = dot(piece[...], wa, NN) + dot(b_ref[rows, :], wb, NN)
        return 0

    lax.fori_loop(0, out_ref.shape[1] // (PAIR * 128), one_tile, 0)


def early(index, pieces, starts, b, weight, token):
    tokens = b.shape[0]
    width = weight.shape[0]
    return call(
        functools.partial(early_kernel, starts),
        "early",
        [index, *pieces, b, weight, token],
        [SCALARS] + [WHOLE] * (len(pieces) + 2) + [ANYWHERE],
        [shape((tokens, width), F32), shape(TOKEN, F32)],
        [WHOLE] * 2,
    )


def late_kernel(last, first, start, dk, index_ref, a_ref, b_ref, w_ref, part_ref, scale_ref, qt_ref, _, *refs):
    state_ref, refs = (None, refs) if first else (refs[0], refs[1:])
    refs, token_ref, at, bt = refs[:-3], refs[-3], refs[-2], refs[-1]
    d_ref = refs[0]
    count, features = a_ref.shape
    tile = PAIR * dk
    token_ref[...] = jnp.zeros_like(token_ref)
    at[...] = a_ref[...].T
    bt[...] = b_ref[...].T
    one, two = part_of(index_ref[0], features), part_of(index_ref[1], features)
    steps = d_ref.shape[1] // tile
    here = slice(start, start + count)

    def one_tile(j, _):
        wide = part_of(j, tile)
        turned = dot(w_ref[wide, one], at[...], NN) + dot(w_ref[wide, two], bt[...], NN)
        low = (part_ref[here, wide] + turned.T).astype(BF16)
        d_ref[:, wide] = low
        states = [None if first else state_ref[0, j * PAIR + i] for i in range(PAIR)]
        for c in reversed(range(count // CHUNK)):
            rows = slice(c * CHUNK, (c + 1) * CHUNK)
            there = slice(start + c * CHUNK, start + (c + 1) * CHUNK)
            for i in range(PAIR):
                grad = (low[rows, i * dk : (i + 1) * dk].astype(F32) * scale_ref[there, :]).astype(BF16)
                state = dot(qt_ref[part_of(j * PAIR + i, dk), there], grad, NN)
                states[i] = state if states[i] is None else states[i] + state
                if not last:
                    refs[1][c, j * PAIR + i] = states[i]
        if last:
            keep_ref, send_ref = refs[1:]
            place = lax.rem(j, steps // 2) * PAIR
            mine = (j // (steps // 2)) == index_ref[2]

            @pl.when(mine)
            def _():
                for i in range(PAIR):
                    keep_ref[place + i] = states[i].astype(BF16)

            @pl.when(jnp.logical_not(mine))
            def _():
                for i in range(PAIR):
                    send_ref[place + i] = states[i].astype(BF16)

        return 0

    lax.fori_loop(0, steps, one_tile, 0)


def late(start, last, index, a, b, weight, part, scale, qt, token, state, heads, dk):
    rows, features = a.shape
    width = weight.shape[0]
    args = [index, a, b, weight, part, scale, qt, token]
    in_specs = [SCALARS] + [WHOLE] * 6 + [ANYWHERE]
    if state is not None:
        args.append(state)
        in_specs.append(WHOLE)
    out_shape = [shape((rows, width), BF16)]
    if last:
        out_shape += [shape((heads // 2, dk, dk), BF16)] * 2
    else:
        out_shape.append(shape((rows // CHUNK, heads, dk, dk), F32))
    out_shape.append(shape(TOKEN, F32))
    return call(
        functools.partial(late_kernel, last, state is None, start, dk),
        "late",
        args,
        in_specs,
        out_shape,
        [WHOLE] * len(out_shape),
        [pltpu.VMEM((features, rows), BF16)] * 2,
    )


def within_kernel(
    heads, dk, chunk, at, level, others,
    index_ref, q_ref, k_ref, v_ref, qt_ref, vt_ref, d_ref, scale_ref, before_ref, own_ref, other_ref, _, *refs
):
    state_ref, refs = (None, refs) if level is None else (refs[0], refs[1:])
    earlier_dq, refs = refs[: len(others)], refs[len(others) :]
    dq_ref, dk_ref, dv_ref, token_ref, wide = refs[:5]
    token_ref[...] = jnp.zeros_like(token_ref)
    if others:
        low_ref, sem = refs[5:]
        copies = [
            pltpu.make_async_copy(source, dq_ref.at[pl.ds(c * CHUNK * heads, CHUNK * heads)], sem.at[i])
            for i, (c, source) in enumerate(zip(others, earlier_dq))
        ]
        for copy in copies:
            copy.start()
    rows = slice(chunk * CHUNK, (chunk + 1) * CHUNK)
    there = slice(at * CHUNK, (at + 1) * CHUNK)
    t = lax.broadcasted_iota(jnp.int32, (CHUNK, CHUNK), 0)
    s = lax.broadcasted_iota(jnp.int32, (CHUNK, CHUNK), 1)
    lower = s <= t
    upper = t <= s
    scale = scale_ref[rows, :]
    half = heads // 2

    def some_heads(g, _):
        mine = g * GROUP // half == index_ref[2]
        for i in range(GROUP):
            h = g * GROUP + i
            cols = part_of(h, dk)
            q, k, v, d = q_ref[rows, cols], k_ref[rows, cols], v_ref[rows, cols], d_ref[there, cols]
            grad = (d.astype(F32) * scale).astype(BF16)
            score_grad = jnp.where(lower, dot(grad, vt_ref[cols, rows], NN), 0.0).astype(BF16)
            score_grad_t = jnp.where(upper, dot(v, grad, NT), 0.0).astype(BF16)
            score_keys_t = jnp.where(upper, dot(k, qt_ref[cols, rows], NN), 0.0).astype(BF16)
            place = lax.rem(h, half)
            earlier = jnp.where(mine, own_ref[place], other_ref[place]).astype(F32) + before_ref[chunk, h]
            dq = scale * dot(d, earlier.astype(BF16), NN) + dot(score_grad, k, NN)
            dkey = dot(score_grad_t, q, NN)
            dval = dot(score_keys_t, grad, NN)
            if state_ref is not None:
                after = state_ref[level, h].astype(BF16)
                dkey = dkey + dot(v, after, NT)
                dval = dval + dot(k, after, NN)
            wide[pl.ds(h, CHUNK, stride=heads), :] = dq
            dk_ref[:, cols] = dkey.astype(BF16)
            dv_ref[:, cols] = dval.astype(BF16)
        return 0

    lax.fori_loop(0, heads // GROUP, some_heads, 0)
    if others:
        low_ref[...] = wide[...].astype(BF16)
        last = pltpu.make_async_copy(
            low_ref, dq_ref.at[pl.ds(chunk * CHUNK * heads, CHUNK * heads)], sem.at[len(others)]
        )
        last.start()
        for copy in copies + [last]:
            copy.wait()
    else:
        dq_ref[...] = wide[...].astype(BF16)


def within(chunk, index, q, k, v, qt, vt, d, at, scale, before, own, other, token, state, others, heads, dk):
    tokens, width = q.shape
    args = [index, q, k, v, qt, vt, d, scale, before, own, other, token]
    in_specs = [SCALARS] + [WHOLE] * 10 + [ANYWHERE]
    level = None
    if state is not None:
        level = state[1]
        args.append(state[0])
        in_specs.append(WHOLE)
    args += list(others.values())
    in_specs += [WHOLE] * len(others)
    scratch = [pltpu.VMEM((CHUNK * heads, dk), F32)]
    rows = tokens if others else CHUNK
    if others:
        scratch += [pltpu.VMEM((CHUNK * heads, dk), BF16), pltpu.SemaphoreType.DMA((len(others) + 1,))]
    return call(
        functools.partial(within_kernel, heads, dk, chunk, at, level, list(others)),
        "within",
        args,
        in_specs,
        [shape((rows * heads, dk), BF16)] + [shape((CHUNK, width), BF16)] * 2 + [shape(TOKEN, F32)],
        [ANYWHERE if others else WHOLE] + [WHOLE] * 3,
        scratch,
    )


def finish_kernel(heads, dk, n, index_ref, k_ref, v_ref, own_ref, other_ref, _, *refs):
    dkp, dvp, (dk_ref, dv_ref, wide_k, wide_v, low_k, low_v, sem) = refs[:n], refs[n : 2 * n], refs[2 * n :]
    half = heads // 2
    first = index_ref[2] == 0
    after, turned = [], []
    for h in range(heads):
        own, other = own_ref[h % half], other_ref[h % half]
        one = jnp.where(first, own, other) if h < half else jnp.where(first, other, own)
        after.append(one)
        turned.append(one.T)
    copies = []
    for c in range(n):
        rows = slice(c * CHUNK, (c + 1) * CHUNK)
        for h in range(heads):
            cols = slice(h * dk, (h + 1) * dk)
            mine = pl.ds(h, CHUNK, stride=heads)
            wide_k[mine, :] = dkp[c][:, cols].astype(F32) + dot(v_ref[rows, cols], turned[h], NN)
            wide_v[mine, :] = dvp[c][:, cols].astype(F32) + dot(k_ref[rows, cols], after[h], NN)
        for i, (wide, low, out) in enumerate(((wide_k, low_k, dk_ref), (wide_v, low_v, dv_ref))):
            low[c] = wide[...].astype(BF16)
            copy = pltpu.make_async_copy(low.at[c], out.at[pl.ds(c * CHUNK * heads, CHUNK * heads)], sem.at[i, c])
            copy.start()
            copies.append(copy)
    for copy in copies:
        copy.wait()


def finish(index, k, v, dkp, dvp, own, other, token, heads, dk):
    tokens, width = k.shape
    n = tokens // CHUNK
    raw = (CHUNK * heads, dk)
    return call(
        functools.partial(finish_kernel, heads, dk, n),
        "finish",
        [index, k, v, own, other, token, *dkp, *dvp],
        [SCALARS] + [WHOLE] * 4 + [ANYWHERE] + [WHOLE] * (2 * n),
        [shape((tokens * heads, dk), BF16)] * 2,
        [ANYWHERE] * 2,
        [pltpu.VMEM(raw, F32)] * 2 + [pltpu.VMEM((n, *raw), BF16)] * 2 + [pltpu.SemaphoreType.DMA((2, n))],
    )


def swap(array, axis, size, bit):
    return lax.ppermute(array, axis, [(i, i ^ bit) for i in range(size)])


def shifted(array, size, step):
    return lax.ppermute(array, "ctx", [(i, i + step) for i in range(size) if 0 <= i + step < size])


class Order:
    def __init__(self):
        self.token = None

    def tie(self, array):
        array, self.token = lax.optimization_barrier((array, self.token))
        return array


def scan_states(keep, send, size, odd, direction, order):
    came = swap(send, "ctx", size, 1)
    yield None
    own = keep.astype(F32)
    total = own + came.astype(F32)
    exclusive = jnp.zeros_like(total)
    step = 2
    while step < size:
        got = shifted(order.tie(total.astype(BF16)), size, direction * step).astype(F32)
        yield None
        exclusive = exclusive + got
        total = total + got
        step *= 2
    later = odd if direction == 1 else jnp.logical_not(odd)
    low = (exclusive + jnp.where(later, 0.0, own)).astype(BF16)
    other = swap(order.tie(low), "ctx", size, 1)
    mine = exclusive + jnp.where(later, came.astype(F32), 0.0)
    yield mine.astype(BF16), other


def body(n_ctx, n_head, queries, keys, values, d_layer, out_weight):
    tokens, heads, dk = queries.shape
    n = tokens // CHUNK
    block = lax.axis_index("ctx").astype(jnp.int32)
    place = lax.axis_index("head").astype(jnp.int32)
    odd = (block & 1) == 1
    half = (block & 1).astype(jnp.int32)

    near = n_head // 2
    far = 1
    groups = [(n // 2, n - n // 2)] + [(c, 1) for c in reversed(range(n // 2))]
    order = Order()
    *pieces, order.token = cut(d_layer, groups)
    across = {c: swap(piece, "head", n_head, near) for (c, _), piece in zip(groups, pieces)}
    beside = swap(d_layer, "head", n_head, far)

    position = block * tokens + jnp.arange(tokens, dtype=jnp.int32)
    scale = lax.rsqrt((dk * (position + 1)).astype(F32))
    scale = jnp.broadcast_to(scale[:, None], (tokens, dk))
    index = jnp.stack([place ^ near, place ^ near ^ far, half])

    flat = (tokens * heads, dk)
    q, k, v, qt, vt, before, keep, send, order.token = prepare(
        half[None], queries.reshape(flat), keys.reshape(flat), values.reshape(flat), order.token, tokens, heads, dk
    )
    forward = scan_states(keep, send, n_ctx, odd, 1, order)
    next(forward)
    starts = [c * CHUNK for c, _ in groups]
    part, order.token = early(jnp.stack([place, place ^ far]), pieces, starts, beside, out_weight, order.token)

    prefix = state = None
    d, after, dq, dkp, dvp = {}, {}, {}, {}, {}

    def inner(c):
        dq[c], dkp[c], dvp[c], order.token = within(
            c, index, q, k, v, qt, vt, *d[c], scale, before, *prefix, order.token, after[c], dict(dq) if c == 0 else {}, heads, dk
        )

    def outer(c, m):
        nonlocal state, keep, send, prefix
        after[c + m - 1] = None if state is None else (state, 0)
        piece = order.tie(across[c])
        both = swap(piece, "head", n_head, far)
        if prefix is None:
            prefix = next(forward)
        while prefix is None and state is not None:
            prefix = next(forward)
        out = late(c * CHUNK, c == 0, index, piece, both, out_weight, part, scale, qt, order.token, state, heads, dk)
        order.token = out[-1]
        if c == 0:
            keep, send = out[1:3]
        else:
            state = out[1]
        for i in range(m):
            d[c + i] = (out[0], i)
            if i < m - 1:
                after[c + i] = (state, i + 1)

    waiting = []
    for c, m in groups:
        outer(c, m)
        waiting += list(range(c, c + m))[::-1]
        if prefix is None:
            prefix = next(forward)
        elif c != 0:
            while len(waiting) > 1:
                inner(waiting.pop(0))
    backward = scan_states(keep, send, n_ctx, odd, -1, order)
    next(backward)
    suffix = None
    while suffix is None:
        suffix = next(backward)
        if waiting:
            inner(waiting.pop(0))
    while waiting:
        inner(waiting.pop(0))
    d_keys, d_values = finish(
        index, k, v, [dkp[c] for c in range(n)], [dvp[c] for c in range(n)], *suffix, order.token, heads, dk
    )
    return tuple(a.reshape(tokens, heads, dk) for a in (dq[0], d_keys, d_values))


def solution(mesh):
    in_specs = (
        P("ctx", "head", None),
        P("ctx", "head", None),
        P("ctx", "head", None),
        P("ctx", "head"),
        P("head", None),
    )
    out_specs = (P("ctx", "head", None), P("ctx", "head", None), P("ctx", "head", None))

    def program(queries, keys, values, d_layer, out_weight):
        return body(mesh.shape["ctx"], mesh.shape["head"], queries, keys, values, d_layer, out_weight)

    return jax.shard_map(program, mesh=mesh, in_specs=in_specs, out_specs=out_specs, check_vma=False)
```

```python
import functools

import jax
import jax.numpy as jnp
from jax import lax
from jax.experimental import pallas as pl
from jax.experimental.pallas import tpu as pltpu
from jax.sharding import PartitionSpec as P

CHUNK = 256
PAIR = 2
GROUP = 4
F32 = jnp.float32
BF16 = jnp.bfloat16
TOKEN = (8, 128)
NT = (((1,), (1,)), ((), ()))
NN = (((1,), (0,)), ((), ()))
FREE = pl.CostEstimate(flops=0, bytes_accessed=0, transcendentals=0)
VMEM_LIMIT = 14 * 1024 * 1024
WHOLE = pl.BlockSpec(memory_space=pltpu.VMEM)
ANYWHERE = pl.BlockSpec(memory_space=pl.ANY)


def dot(a, b, dims):
    return lax.dot_general(a, b, dims, preferred_element_type=F32)


def shape(dims, dtype):
    return jax.ShapeDtypeStruct(dims, dtype)


def outside(*arrays):
    return [pltpu.with_memory_space_constraint(a, pltpu.HBM) for a in arrays]


def part_of(i, size):
    return pl.ds(pl.multiple_of(i * size, size), size)


def call(kernel, name, args, in_specs, out_shape, out_specs, scratch=()):
    return pl.pallas_call(
        kernel,
        in_specs=in_specs,
        out_specs=out_specs,
        out_shape=out_shape,
        scratch_shapes=scratch,
        compiler_params=pltpu.CompilerParams(vmem_limit_bytes=VMEM_LIMIT),
        cost_estimate=FREE,
        name=name,
    )(*args)


def cut_kernel(starts, source, *refs):
    pieces, token_ref, sem = refs[: len(starts)], refs[-2], refs[-1]
    token_ref[...] = jnp.zeros_like(token_ref)
    copies = [
        pltpu.make_async_copy(source.at[pl.ds(start, piece.shape[0])], piece, sem.at[i])
        for i, (start, piece) in enumerate(zip(starts, pieces))
    ]
    for copy in copies:
        copy.start()
    for copy in copies:
        copy.wait()


def cut(d_layer, groups):
    features = d_layer.shape[1]
    return call(
        functools.partial(cut_kernel, [c * CHUNK for c, _ in groups]),
        "cut",
        outside(d_layer),
        [ANYWHERE],
        [shape((m * CHUNK, features), d_layer.dtype) for _, m in groups] + [shape(TOKEN, F32)],
        [WHOLE] * (len(groups) + 1),
        [pltpu.SemaphoreType.DMA((len(groups),))],
    )


def prepare_kernel(
    heads, dk, q_ref, k_ref, v_ref, _, qf_ref, kf_ref, vf_ref, qt_ref, vt_ref, before_ref, scale_ref, keep_ref, send_ref, token_ref,
    raw, wides, acc, sem
):
    n = qf_ref.shape[0] // CHUNK

    def load(i, c):
        source = (q_ref, k_ref, v_ref)[i].at[part_of(c, CHUNK * heads)]
        return pltpu.make_async_copy(source, raw.at[i, c], sem.at[i, c])

    for c in range(n):
        for i in range(3):
            load(i, c).start()
    token_ref[...] = jnp.zeros_like(token_ref)
    acc[...] = jnp.zeros_like(acc)
    tokens = scale_ref.shape[0]
    position = lax.axis_index("ctx") * tokens + lax.broadcasted_iota(jnp.int32, scale_ref.shape, 0)
    scale_ref[...] = lax.rsqrt((dk * (position + 1)).astype(F32))

    def one_chunk(c, _):
        rows = part_of(c, CHUNK)
        before_ref[c] = acc[...]
        for i in range(3):
            load(i, c).wait()
            wides[i] = raw[i, c].astype(F32)
        for h in range(heads):
            cols = slice(h * dk, (h + 1) * dk)
            mine = pl.ds(h, CHUNK, stride=heads)
            q, k, v = (wides[i, mine, :].astype(BF16) for i in range(3))
            qf_ref[rows, cols] = q
            kf_ref[rows, cols] = k
            vf_ref[rows, cols] = v
            qt_ref[cols, rows] = q.T
            vt = v.T
            vt_ref[cols, rows] = vt
            acc[h] += dot(vt, k, NN)
        return 0

    lax.fori_loop(0, n, one_chunk, 0)
    low, high = acc[: heads // 2].astype(BF16), acc[heads // 2 :].astype(BF16)
    first = lax.axis_index("ctx") % 2 == 0
    keep_ref[...] = jnp.where(first, low, high)
    send_ref[...] = jnp.where(first, high, low)


def prepare(q, k, v, token, tokens, heads, dk):
    n = tokens // CHUNK
    width = heads * dk
    return call(
        functools.partial(prepare_kernel, heads, dk),
        "prepare",
        [*outside(q, k, v), token],
        [ANYWHERE] * 4,
        [shape((tokens, width), BF16)] * 3
        + [shape((width, tokens), BF16)] * 2
        + [shape((n, heads, dk, dk), F32), shape((tokens, dk), F32)]
        + [shape((heads // 2, dk, dk), BF16)] * 2
        + [shape(TOKEN, F32)],
        [WHOLE] * 10,
        [
            pltpu.VMEM((3, n, CHUNK * heads, dk), BF16),
            pltpu.VMEM((3, CHUNK * heads, dk), F32),
            pltpu.VMEM((heads, dk, dk), F32),
            pltpu.SemaphoreType.DMA((3, n)),
        ],
    )


def early_kernel(starts, *refs):
    pieces, (b_ref, w_ref, _, out_ref, token_ref) = refs[: len(starts)], refs[len(starts) :]
    token_ref[...] = jnp.zeros_like(token_ref)
    features = b_ref.shape[1]
    place = lax.axis_index("head")
    first, second = part_of(place, features), part_of(place ^ 1, features)

    def one_tile(j, _):
        tile = part_of(j, PAIR * 128)
        wa, wb = w_ref[tile, first].T, w_ref[tile, second].T
        for start, piece in zip(starts, pieces):
            rows = slice(start, start + piece.shape[0])
            out_ref[rows, tile] = dot(piece[...], wa, NN) + dot(b_ref[rows, :], wb, NN)
        return 0

    lax.fori_loop(0, out_ref.shape[1] // (PAIR * 128), one_tile, 0)


def early(pieces, starts, b, weight, token):
    tokens = b.shape[0]
    width = weight.shape[0]
    return call(
        functools.partial(early_kernel, starts),
        "early",
        [*pieces, b, weight, token],
        [WHOLE] * (len(pieces) + 2) + [ANYWHERE],
        [shape((tokens, width), F32), shape(TOKEN, F32)],
        [WHOLE] * 2,
    )


def late_kernel(last, first, start, near, dk, a_ref, b_ref, w_ref, part_ref, scale_ref, qt_ref, _, *refs):
    state_ref, refs = (None, refs) if first else (refs[0], refs[1:])
    refs, token_ref, at, bt = refs[:-3], refs[-3], refs[-2], refs[-1]
    d_ref = refs[0]
    count, features = a_ref.shape
    tile = PAIR * dk
    token_ref[...] = jnp.zeros_like(token_ref)
    at[...] = a_ref[...].T
    bt[...] = b_ref[...].T
    place = lax.axis_index("head")
    one, two = part_of(place ^ near, features), part_of(place ^ near ^ 1, features)
    steps = d_ref.shape[1] // tile
    here = slice(start, start + count)

    def one_tile(j, _):
        wide = part_of(j, tile)
        turned = dot(w_ref[wide, one], at[...], NN) + dot(w_ref[wide, two], bt[...], NN)
        low = (part_ref[here, wide] + turned.T).astype(BF16)
        d_ref[:, wide] = low
        states = [None if first else state_ref[0, j * PAIR + i] for i in range(PAIR)]
        for c in reversed(range(count // CHUNK)):
            rows = slice(c * CHUNK, (c + 1) * CHUNK)
            there = slice(start + c * CHUNK, start + (c + 1) * CHUNK)
            for i in range(PAIR):
                grad = (low[rows, i * dk : (i + 1) * dk].astype(F32) * scale_ref[there, :]).astype(BF16)
                state = dot(qt_ref[part_of(j * PAIR + i, dk), there], grad, NN)
                states[i] = state if states[i] is None else states[i] + state
                if not last:
                    refs[1][c, j * PAIR + i] = states[i]
        if last:
            keep_ref, send_ref = refs[1:]
            place = lax.rem(j, steps // 2) * PAIR
            mine = (j // (steps // 2)) == lax.axis_index("ctx") % 2

            @pl.when(mine)
            def _():
                for i in range(PAIR):
                    keep_ref[place + i] = states[i].astype(BF16)

            @pl.when(jnp.logical_not(mine))
            def _():
                for i in range(PAIR):
                    send_ref[place + i] = states[i].astype(BF16)

        return 0

    lax.fori_loop(0, steps, one_tile, 0)


def late(start, last, near, a, b, weight, part, scale, qt, token, state, heads, dk):
    rows, features = a.shape
    width = weight.shape[0]
    args = [a, b, weight, part, scale, qt, token]
    in_specs = [WHOLE] * 6 + [ANYWHERE]
    if state is not None:
        args.append(state)
        in_specs.append(WHOLE)
    out_shape = [shape((rows, width), BF16)]
    if last:
        out_shape += [shape((heads // 2, dk, dk), BF16)] * 2
    else:
        out_shape.append(shape((rows // CHUNK, heads, dk, dk), F32))
    out_shape.append(shape(TOKEN, F32))
    return call(
        functools.partial(late_kernel, last, state is None, start, near, dk),
        "late",
        args,
        in_specs,
        out_shape,
        [WHOLE] * len(out_shape),
        [pltpu.VMEM((features, rows), BF16)] * 2,
    )


def within_kernel(
    heads, dk, chunk, at, level, others,
    q_ref, k_ref, v_ref, qt_ref, vt_ref, d_ref, scale_ref, before_ref, own_ref, other_ref, _, *refs
):
    state_ref, refs = (None, refs) if level is None else (refs[0], refs[1:])
    earlier_dq, refs = refs[: len(others)], refs[len(others) :]
    dq_ref, dk_ref, dv_ref, token_ref, wide = refs[:5]
    token_ref[...] = jnp.zeros_like(token_ref)
    if others:
        low_ref, sem = refs[5:]
        copies = [
            pltpu.make_async_copy(source, dq_ref.at[pl.ds(c * CHUNK * heads, CHUNK * heads)], sem.at[i])
            for i, (c, source) in enumerate(zip(others, earlier_dq))
        ]
        for copy in copies:
            copy.start()
    rows = slice(chunk * CHUNK, (chunk + 1) * CHUNK)
    there = slice(at * CHUNK, (at + 1) * CHUNK)
    t = lax.broadcasted_iota(jnp.int32, (CHUNK, CHUNK), 0)
    s = lax.broadcasted_iota(jnp.int32, (CHUNK, CHUNK), 1)
    lower = s <= t
    upper = t <= s
    scale = scale_ref[rows, :]
    half = heads // 2

    def some_heads(g, _):
        mine = g * GROUP // half == lax.axis_index("ctx") % 2
        for i in range(GROUP):
            h = g * GROUP + i
            cols = part_of(h, dk)
            q, k, v, d = q_ref[rows, cols], k_ref[rows, cols], v_ref[rows, cols], d_ref[there, cols]
            grad = (d.astype(F32) * scale).astype(BF16)
            score_grad = jnp.where(lower, dot(grad, vt_ref[cols, rows], NN), 0.0).astype(BF16)
            score_grad_t = jnp.where(upper, dot(v, grad, NT), 0.0).astype(BF16)
            score_keys_t = jnp.where(upper, dot(k, qt_ref[cols, rows], NN), 0.0).astype(BF16)
            place = lax.rem(h, half)
            earlier = jnp.where(mine, own_ref[place], other_ref[place]).astype(F32) + before_ref[chunk, h]
            dq = scale * dot(d, earlier.astype(BF16), NN) + dot(score_grad, k, NN)
            dkey = dot(score_grad_t, q, NN)
            dval = dot(score_keys_t, grad, NN)
            if state_ref is not None:
                after = state_ref[level, h].astype(BF16)
                dkey = dkey + dot(v, after, NT)
                dval = dval + dot(k, after, NN)
            wide[pl.ds(h, CHUNK, stride=heads), :] = dq
            dk_ref[:, cols] = dkey.astype(BF16)
            dv_ref[:, cols] = dval.astype(BF16)
        return 0

    lax.fori_loop(0, heads // GROUP, some_heads, 0)
    if others:
        low_ref[...] = wide[...].astype(BF16)
        last = pltpu.make_async_copy(
            low_ref, dq_ref.at[pl.ds(chunk * CHUNK * heads, CHUNK * heads)], sem.at[len(others)]
        )
        last.start()
        for copy in copies + [last]:
            copy.wait()
    else:
        dq_ref[...] = wide[...].astype(BF16)


def within(chunk, q, k, v, qt, vt, d, at, scale, before, own, other, token, state, others, heads, dk):
    tokens, width = q.shape
    args = [q, k, v, qt, vt, d, scale, before, own, other, token]
    in_specs = [WHOLE] * 10 + [ANYWHERE]
    level = None
    if state is not None:
        level = state[1]
        args.append(state[0])
        in_specs.append(WHOLE)
    args += list(others.values())
    in_specs += [WHOLE] * len(others)
    scratch = [pltpu.VMEM((CHUNK * heads, dk), F32)]
    rows = tokens if others else CHUNK
    if others:
        scratch += [pltpu.VMEM((CHUNK * heads, dk), BF16), pltpu.SemaphoreType.DMA((len(others) + 1,))]
    return call(
        functools.partial(within_kernel, heads, dk, chunk, at, level, list(others)),
        "within",
        args,
        in_specs,
        [shape((rows * heads, dk), BF16)] + [shape((CHUNK, width), BF16)] * 2 + [shape(TOKEN, F32)],
        [ANYWHERE if others else WHOLE] + [WHOLE] * 3,
        scratch,
    )


def finish_kernel(heads, dk, n, k_ref, v_ref, own_ref, other_ref, _, *refs):
    dkp, dvp, (dk_ref, dv_ref, wide_k, wide_v, low_k, low_v, sem) = refs[:n], refs[n : 2 * n], refs[2 * n :]
    half = heads // 2
    first = lax.axis_index("ctx") % 2 == 0
    after, turned = [], []
    for h in range(heads):
        own, other = own_ref[h % half], other_ref[h % half]
        one = jnp.where(first, own, other) if h < half else jnp.where(first, other, own)
        after.append(one)
        turned.append(one.T)
    copies = []
    for c in range(n):
        rows = slice(c * CHUNK, (c + 1) * CHUNK)
        for h in range(heads):
            cols = slice(h * dk, (h + 1) * dk)
            mine = pl.ds(h, CHUNK, stride=heads)
            wide_k[mine, :] = dkp[c][:, cols].astype(F32) + dot(v_ref[rows, cols], turned[h], NN)
            wide_v[mine, :] = dvp[c][:, cols].astype(F32) + dot(k_ref[rows, cols], after[h], NN)
        for i, (wide, low, out) in enumerate(((wide_k, low_k, dk_ref), (wide_v, low_v, dv_ref))):
            low[c] = wide[...].astype(BF16)
            copy = pltpu.make_async_copy(low.at[c], out.at[pl.ds(c * CHUNK * heads, CHUNK * heads)], sem.at[i, c])
            copy.start()
            copies.append(copy)
    for copy in copies:
        copy.wait()


def finish(k, v, dkp, dvp, own, other, token, heads, dk):
    tokens, width = k.shape
    n = tokens // CHUNK
    raw = (CHUNK * heads, dk)
    return call(
        functools.partial(finish_kernel, heads, dk, n),
        "finish",
        [k, v, own, other, token, *dkp, *dvp],
        [WHOLE] * 4 + [ANYWHERE] + [WHOLE] * (2 * n),
        [shape((tokens * heads, dk), BF16)] * 2,
        [ANYWHERE] * 2,
        [pltpu.VMEM(raw, F32)] * 2 + [pltpu.VMEM((n, *raw), BF16)] * 2 + [pltpu.SemaphoreType.DMA((2, n))],
    )


def swap(array, axis, size, bit):
    return lax.ppermute(array, axis, [(i, i ^ bit) for i in range(size)])


def shifted(array, size, step):
    return lax.ppermute(array, "ctx", [(i, i + step) for i in range(size) if 0 <= i + step < size])


class Order:
    def __init__(self):
        self.token = None

    def tie(self, array):
        array, self.token = lax.optimization_barrier((array, self.token))
        return array


def total_kernel(*refs):
    *terms, out = refs
    total = terms[0][...].astype(F32)
    for term in terms[1:]:
        total = total + term[...].astype(F32)
    out[...] = total.astype(BF16)


def ends_kernel(later_is_odd, own, came, *refs):
    *got, give, mine = refs
    exclusive = got[0][...].astype(F32)
    for term in got[1:]:
        exclusive = exclusive + term[...].astype(F32)
    later = (lax.axis_index("ctx") % 2 == 1) == later_is_odd
    give[...] = jnp.where(later, exclusive, exclusive + own[...].astype(F32)).astype(BF16)
    mine[...] = jnp.where(later, exclusive + came[...].astype(F32), exclusive).astype(BF16)


def scan_states(keep, send, size, direction, order):
    terms = [keep, swap(send, "ctx", size, 1)]
    yield None
    like = shape(keep.shape, BF16)
    step = 2
    while step < size:
        total = call(total_kernel, "total", terms, [WHOLE] * len(terms), like, WHOLE)
        terms.append(shifted(order.tie(total), size, direction * step))
        yield None
        step *= 2
    kernel = functools.partial(ends_kernel, direction == 1)
    give, mine = call(kernel, "ends", terms, [WHOLE] * len(terms), [like] * 2, [WHOLE] * 2)
    yield mine, swap(order.tie(give), "ctx", size, 1)


def body(n_ctx, n_head, queries, keys, values, d_layer, out_weight):
    tokens, heads, dk = queries.shape
    n = tokens // CHUNK
    near = n_head // 2
    far = 1
    groups = [(n // 2, n - n // 2)] + [(c, 1) for c in reversed(range(n // 2))]
    order = Order()
    *pieces, order.token = cut(d_layer, groups)
    across = {c: swap(piece, "head", n_head, near) for (c, _), piece in zip(groups, pieces)}
    beside = swap(d_layer, "head", n_head, far)

    flat = (tokens * heads, dk)
    q, k, v, qt, vt, before, scale, keep, send, order.token = prepare(
        queries.reshape(flat), keys.reshape(flat), values.reshape(flat), order.token, tokens, heads, dk
    )
    forward = scan_states(keep, send, n_ctx, 1, order)
    next(forward)
    starts = [c * CHUNK for c, _ in groups]
    part, order.token = early(pieces, starts, beside, out_weight, order.token)

    prefix = state = None
    d, after, dq, dkp, dvp = {}, {}, {}, {}, {}

    def inner(c):
        dq[c], dkp[c], dvp[c], order.token = within(
            c, q, k, v, qt, vt, *d[c], scale, before, *prefix, order.token, after[c], dict(dq) if c == 0 else {}, heads, dk
        )

    def outer(c, m):
        nonlocal state, keep, send, prefix
        after[c + m - 1] = None if state is None else (state, 0)
        piece = order.tie(across[c])
        both = swap(piece, "head", n_head, far)
        if prefix is None:
            prefix = next(forward)
        while prefix is None and state is not None:
            prefix = next(forward)
        out = late(c * CHUNK, c == 0, near, piece, both, out_weight, part, scale, qt, order.token, state, heads, dk)
        order.token = out[-1]
        if c == 0:
            keep, send = out[1:3]
        else:
            state = out[1]
        for i in range(m):
            d[c + i] = (out[0], i)
            if i < m - 1:
                after[c + i] = (state, i + 1)

    waiting = []
    for c, m in groups:
        outer(c, m)
        waiting += list(range(c, c + m))[::-1]
        if prefix is None:
            prefix = next(forward)
        elif c != 0:
            while len(waiting) > 1:
                inner(waiting.pop(0))
    backward = scan_states(keep, send, n_ctx, -1, order)
    next(backward)
    suffix = None
    while suffix is None:
        suffix = next(backward)
        if waiting:
            inner(waiting.pop(0))
    while waiting:
        inner(waiting.pop(0))
    d_keys, d_values = finish(
        k, v, [dkp[c] for c in range(n)], [dvp[c] for c in range(n)], *suffix, order.token, heads, dk
    )
    return tuple(a.reshape(tokens, heads, dk) for a in (dq[0], d_keys, d_values))


def solution(mesh):
    in_specs = (
        P("ctx", "head", None),
        P("ctx", "head", None),
        P("ctx", "head", None),
        P("ctx", "head"),
        P("head", None),
    )
    out_specs = (P("ctx", "head", None), P("ctx", "head", None), P("ctx", "head", None))

    def program(queries, keys, values, d_layer, out_weight):
        return body(mesh.shape["ctx"], mesh.shape["head"], queries, keys, values, d_layer, out_weight)

    return jax.shard_map(program, mesh=mesh, in_specs=in_specs, out_specs=out_specs, check_vma=False)
```

```python
import functools

import jax
import jax.numpy as jnp
from jax import lax
from jax.experimental import pallas as pl
from jax.experimental.pallas import tpu as pltpu
from jax.sharding import PartitionSpec as P

CHUNK = 256
PAIR = 2
GROUP = 4
F32 = jnp.float32
BF16 = jnp.bfloat16
TOKEN = (8, 128)
NT = (((1,), (1,)), ((), ()))
NN = (((1,), (0,)), ((), ()))
FREE = pl.CostEstimate(flops=0, bytes_accessed=0, transcendentals=0)
VMEM_LIMIT = 14 * 1024 * 1024
WHOLE = pl.BlockSpec(memory_space=pltpu.VMEM)
ANYWHERE = pl.BlockSpec(memory_space=pl.ANY)


def dot(a, b, dims):
    return lax.dot_general(a, b, dims, preferred_element_type=F32)


def shape(dims, dtype):
    return jax.ShapeDtypeStruct(dims, dtype)


def outside(*arrays):
    return [pltpu.with_memory_space_constraint(a, pltpu.HBM) for a in arrays]


def part_of(i, size):
    return pl.ds(pl.multiple_of(i * size, size), size)


def call(kernel, name, args, in_specs, out_shape, out_specs, scratch=()):
    return pl.pallas_call(
        kernel,
        in_specs=in_specs,
        out_specs=out_specs,
        out_shape=out_shape,
        scratch_shapes=scratch,
        compiler_params=pltpu.CompilerParams(vmem_limit_bytes=VMEM_LIMIT),
        cost_estimate=FREE,
        name=name,
    )(*args)


def cut_kernel(starts, source, *refs):
    pieces, token_ref, sem = refs[: len(starts)], refs[-2], refs[-1]
    token_ref[...] = jnp.zeros_like(token_ref)
    copies = [
        pltpu.make_async_copy(source.at[pl.ds(start, piece.shape[0])], piece, sem.at[i])
        for i, (start, piece) in enumerate(zip(starts, pieces))
    ]
    for copy in copies:
        copy.start()
    for copy in copies:
        copy.wait()


def cut(d_layer, groups):
    features = d_layer.shape[1]
    return call(
        functools.partial(cut_kernel, [c * CHUNK for c, _ in groups]),
        "cut",
        outside(d_layer),
        [ANYWHERE],
        [shape((m * CHUNK, features), d_layer.dtype) for _, m in groups] + [shape(TOKEN, F32)],
        [WHOLE] * (len(groups) + 1),
        [pltpu.SemaphoreType.DMA((len(groups),))],
    )


def prepare_kernel(
    heads, dk, q_ref, k_ref, v_ref, _, qf_ref, kf_ref, vf_ref, qt_ref, vt_ref, before_ref, scale_ref, state_ref, token_ref,
    raw, wides, acc, sem
):
    n = qf_ref.shape[0] // CHUNK

    def load(i, c):
        source = (q_ref, k_ref, v_ref)[i].at[part_of(c, CHUNK * heads)]
        return pltpu.make_async_copy(source, raw.at[i, c], sem.at[i, c])

    for c in range(n):
        for i in range(3):
            load(i, c).start()
    token_ref[...] = jnp.zeros_like(token_ref)
    acc[...] = jnp.zeros_like(acc)
    tokens = scale_ref.shape[0]
    position = lax.axis_index("ctx") * tokens + lax.broadcasted_iota(jnp.int32, scale_ref.shape, 0)
    scale_ref[...] = lax.rsqrt((dk * (position + 1)).astype(F32))

    def one_chunk(c, _):
        rows = part_of(c, CHUNK)
        before_ref[c] = acc[...]
        for i in range(3):
            load(i, c).wait()
            wides[i] = raw[i, c].astype(F32)
        for h in range(heads):
            cols = slice(h * dk, (h + 1) * dk)
            mine = pl.ds(h, CHUNK, stride=heads)
            q, k, v = (wides[i, mine, :].astype(BF16) for i in range(3))
            qf_ref[rows, cols] = q
            kf_ref[rows, cols] = k
            vf_ref[rows, cols] = v
            qt_ref[cols, rows] = q.T
            vt = v.T
            vt_ref[cols, rows] = vt
            acc[h] += dot(vt, k, NN)
        return 0

    lax.fori_loop(0, n, one_chunk, 0)
    state_ref[...] = acc[...].astype(BF16)


def prepare(q, k, v, token, tokens, heads, dk):
    n = tokens // CHUNK
    width = heads * dk
    return call(
        functools.partial(prepare_kernel, heads, dk),
        "prepare",
        [*outside(q, k, v), token],
        [ANYWHERE] * 4,
        [shape((tokens, width), BF16)] * 3
        + [shape((width, tokens), BF16)] * 2
        + [shape((n, heads, dk, dk), F32), shape((tokens, dk), F32)]
        + [shape((heads, dk, dk), BF16), shape(TOKEN, F32)],
        [WHOLE] * 9,
        [
            pltpu.VMEM((3, n, CHUNK * heads, dk), BF16),
            pltpu.VMEM((3, CHUNK * heads, dk), F32),
            pltpu.VMEM((heads, dk, dk), F32),
            pltpu.SemaphoreType.DMA((3, n)),
        ],
    )


def early_kernel(starts, *refs):
    pieces, (b_ref, w_ref, _, out_ref, token_ref) = refs[: len(starts)], refs[len(starts) :]
    token_ref[...] = jnp.zeros_like(token_ref)
    features = b_ref.shape[1]
    place = lax.axis_index("head")
    first, second = part_of(place, features), part_of(place ^ 1, features)

    def one_tile(j, _):
        tile = part_of(j, PAIR * 128)
        wa, wb = w_ref[tile, first].T, w_ref[tile, second].T
        for start, piece in zip(starts, pieces):
            rows = slice(start, start + piece.shape[0])
            out_ref[rows, tile] = dot(piece[...], wa, NN) + dot(b_ref[rows, :], wb, NN)
        return 0

    lax.fori_loop(0, out_ref.shape[1] // (PAIR * 128), one_tile, 0)


def early(pieces, starts, b, weight, token):
    tokens = b.shape[0]
    width = weight.shape[0]
    return call(
        functools.partial(early_kernel, starts),
        "early",
        [*pieces, b, weight, token],
        [WHOLE] * (len(pieces) + 2) + [ANYWHERE],
        [shape((tokens, width), F32), shape(TOKEN, F32)],
        [WHOLE] * 2,
    )


def late_kernel(last, first, start, near, dk, a_ref, b_ref, w_ref, part_ref, scale_ref, qt_ref, _, *refs):
    state_ref, refs = (None, refs) if first else (refs[0], refs[1:])
    refs, token_ref, at, bt = refs[:-3], refs[-3], refs[-2], refs[-1]
    d_ref = refs[0]
    count, features = a_ref.shape
    tile = PAIR * dk
    token_ref[...] = jnp.zeros_like(token_ref)
    at[...] = a_ref[...].T
    bt[...] = b_ref[...].T
    place = lax.axis_index("head")
    one, two = part_of(place ^ near, features), part_of(place ^ near ^ 1, features)
    steps = d_ref.shape[1] // tile
    here = slice(start, start + count)

    def one_tile(j, _):
        wide = part_of(j, tile)
        turned = dot(w_ref[wide, one], at[...], NN) + dot(w_ref[wide, two], bt[...], NN)
        low = (part_ref[here, wide] + turned.T).astype(BF16)
        d_ref[:, wide] = low
        states = [None if first else state_ref[0, j * PAIR + i] for i in range(PAIR)]
        for c in reversed(range(count // CHUNK)):
            rows = slice(c * CHUNK, (c + 1) * CHUNK)
            there = slice(start + c * CHUNK, start + (c + 1) * CHUNK)
            for i in range(PAIR):
                grad = (low[rows, i * dk : (i + 1) * dk].astype(F32) * scale_ref[there, :]).astype(BF16)
                state = dot(qt_ref[part_of(j * PAIR + i, dk), there], grad, NN)
                states[i] = state if states[i] is None else states[i] + state
                if not last:
                    refs[1][c, j * PAIR + i] = states[i]
        if last:
            for i in range(PAIR):
                refs[1][j * PAIR + i] = states[i].astype(BF16)
        return 0

    lax.fori_loop(0, steps, one_tile, 0)


def late(start, last, near, a, b, weight, part, scale, qt, token, state, heads, dk):
    rows, features = a.shape
    width = weight.shape[0]
    args = [a, b, weight, part, scale, qt, token]
    in_specs = [WHOLE] * 6 + [ANYWHERE]
    if state is not None:
        args.append(state)
        in_specs.append(WHOLE)
    out_shape = [shape((rows, width), BF16)]
    if last:
        out_shape.append(shape((heads, dk, dk), BF16))
    else:
        out_shape.append(shape((rows // CHUNK, heads, dk, dk), F32))
    out_shape.append(shape(TOKEN, F32))
    return call(
        functools.partial(late_kernel, last, state is None, start, near, dk),
        "late",
        args,
        in_specs,
        out_shape,
        [WHOLE] * len(out_shape),
        [pltpu.VMEM((features, rows), BF16)] * 2,
    )


def within_kernel(
    heads, dk, chunk, at, level, others,
    q_ref, k_ref, v_ref, qt_ref, vt_ref, d_ref, scale_ref, before_ref, prefix_ref, _, *refs
):
    state_ref, refs = (None, refs) if level is None else (refs[0], refs[1:])
    earlier_dq, refs = refs[: len(others)], refs[len(others) :]
    dq_ref, dk_ref, dv_ref, token_ref, wide = refs[:5]
    token_ref[...] = jnp.zeros_like(token_ref)
    if others:
        low_ref, sem = refs[5:]
        copies = [
            pltpu.make_async_copy(source, dq_ref.at[pl.ds(c * CHUNK * heads, CHUNK * heads)], sem.at[i])
            for i, (c, source) in enumerate(zip(others, earlier_dq))
        ]
        for copy in copies:
            copy.start()
    rows = slice(chunk * CHUNK, (chunk + 1) * CHUNK)
    there = slice(at * CHUNK, (at + 1) * CHUNK)
    t = lax.broadcasted_iota(jnp.int32, (CHUNK, CHUNK), 0)
    s = lax.broadcasted_iota(jnp.int32, (CHUNK, CHUNK), 1)
    lower = s <= t
    upper = t <= s
    scale = scale_ref[rows, :]

    def some_heads(g, _):
        for i in range(GROUP):
            h = g * GROUP + i
            cols = part_of(h, dk)
            q, k, v, d = q_ref[rows, cols], k_ref[rows, cols], v_ref[rows, cols], d_ref[there, cols]
            grad = (d.astype(F32) * scale).astype(BF16)
            score_grad = jnp.where(lower, dot(grad, vt_ref[cols, rows], NN), 0.0).astype(BF16)
            score_grad_t = jnp.where(upper, dot(v, grad, NT), 0.0).astype(BF16)
            score_keys_t = jnp.where(upper, dot(k, qt_ref[cols, rows], NN), 0.0).astype(BF16)
            earlier = prefix_ref[h].astype(F32) + before_ref[chunk, h]
            dq = scale * dot(d, earlier.astype(BF16), NN) + dot(score_grad, k, NN)
            dkey = dot(score_grad_t, q, NN)
            dval = dot(score_keys_t, grad, NN)
            if state_ref is not None:
                after = state_ref[level, h].astype(BF16)
                dkey = dkey + dot(v, after, NT)
                dval = dval + dot(k, after, NN)
            wide[pl.ds(h, CHUNK, stride=heads), :] = dq
            dk_ref[:, cols] = dkey.astype(BF16)
            dv_ref[:, cols] = dval.astype(BF16)
        return 0

    lax.fori_loop(0, heads // GROUP, some_heads, 0)
    if others:
        low_ref[...] = wide[...].astype(BF16)
        last = pltpu.make_async_copy(
            low_ref, dq_ref.at[pl.ds(chunk * CHUNK * heads, CHUNK * heads)], sem.at[len(others)]
        )
        last.start()
        for copy in copies + [last]:
            copy.wait()
    else:
        dq_ref[...] = wide[...].astype(BF16)


def within(chunk, q, k, v, qt, vt, d, at, scale, before, prefix, token, state, others, heads, dk):
    tokens, width = q.shape
    args = [q, k, v, qt, vt, d, scale, before, prefix, token]
    in_specs = [WHOLE] * 9 + [ANYWHERE]
    level = None
    if state is not None:
        level = state[1]
        args.append(state[0])
        in_specs.append(WHOLE)
    args += list(others.values())
    in_specs += [WHOLE] * len(others)
    scratch = [pltpu.VMEM((CHUNK * heads, dk), F32)]
    rows = tokens if others else CHUNK
    if others:
        scratch += [pltpu.VMEM((CHUNK * heads, dk), BF16), pltpu.SemaphoreType.DMA((len(others) + 1,))]
    return call(
        functools.partial(within_kernel, heads, dk, chunk, at, level, list(others)),
        "within",
        args,
        in_specs,
        [shape((rows * heads, dk), BF16)] + [shape((CHUNK, width), BF16)] * 2 + [shape(TOKEN, F32)],
        [ANYWHERE if others else WHOLE] + [WHOLE] * 3,
        scratch,
    )


def finish_kernel(heads, dk, n, k_ref, v_ref, suffix_ref, _, *refs):
    dkp, dvp, (dk_ref, dv_ref, wide_k, wide_v, low_k, low_v, sem) = refs[:n], refs[n : 2 * n], refs[2 * n :]
    after = [suffix_ref[h] for h in range(heads)]
    turned = [one.T for one in after]
    copies = []
    for c in range(n):
        rows = slice(c * CHUNK, (c + 1) * CHUNK)
        for h in range(heads):
            cols = slice(h * dk, (h + 1) * dk)
            mine = pl.ds(h, CHUNK, stride=heads)
            wide_k[mine, :] = dkp[c][:, cols].astype(F32) + dot(v_ref[rows, cols], turned[h], NN)
            wide_v[mine, :] = dvp[c][:, cols].astype(F32) + dot(k_ref[rows, cols], after[h], NN)
        for i, (wide, low, out) in enumerate(((wide_k, low_k, dk_ref), (wide_v, low_v, dv_ref))):
            low[c] = wide[...].astype(BF16)
            copy = pltpu.make_async_copy(low.at[c], out.at[pl.ds(c * CHUNK * heads, CHUNK * heads)], sem.at[i, c])
            copy.start()
            copies.append(copy)
    for copy in copies:
        copy.wait()


def finish(k, v, dkp, dvp, suffix, token, heads, dk):
    tokens, width = k.shape
    n = tokens // CHUNK
    raw = (CHUNK * heads, dk)
    return call(
        functools.partial(finish_kernel, heads, dk, n),
        "finish",
        [k, v, suffix, token, *dkp, *dvp],
        [WHOLE] * 3 + [ANYWHERE] + [WHOLE] * (2 * n),
        [shape((tokens * heads, dk), BF16)] * 2,
        [ANYWHERE] * 2,
        [pltpu.VMEM(raw, F32)] * 2 + [pltpu.VMEM((n, *raw), BF16)] * 2 + [pltpu.SemaphoreType.DMA((2, n))],
    )


def swap(array, axis, size, bit):
    return lax.ppermute(array, axis, [(i, i ^ bit) for i in range(size)])


def shifted(array, size, step):
    return lax.ppermute(array, "ctx", [(i, i + step) for i in range(size) if 0 <= i + step < size])


class Order:
    def __init__(self):
        self.token = None

    def tie(self, array):
        array, self.token = lax.optimization_barrier((array, self.token))
        return array


def sums_kernel(direction, states_ref, out_ref):
    size = states_ref.shape[0]
    order = range(size) if direction == 1 else range(size - 1, -1, -1)
    total = jnp.zeros(states_ref.shape[1:], F32)
    for i in order:
        out_ref[i] = total.astype(BF16)
        total = total + states_ref[i].astype(F32)


def exchange(array):
    return lax.all_to_all(array, "ctx", 0, 0, tiled=True)


def scan_states(state, size, direction, order):
    heads, dk, width = state.shape
    parts = exchange(state.reshape(size, heads * dk // size, width))
    yield None
    sums = call(
        functools.partial(sums_kernel, direction), "sums", [parts], [WHOLE], shape(parts.shape, BF16), WHOLE
    )
    yield exchange(order.tie(sums)).reshape(state.shape)


def body(n_ctx, n_head, queries, keys, values, d_layer, out_weight):
    tokens, heads, dk = queries.shape
    n = tokens // CHUNK
    near = n_head // 2
    far = 1
    groups = [(n // 2, n - n // 2)] + [(c, 1) for c in reversed(range(n // 2))]
    order = Order()
    *pieces, order.token = cut(d_layer, groups)
    across = {c: swap(piece, "head", n_head, near) for (c, _), piece in zip(groups, pieces)}
    beside = swap(d_layer, "head", n_head, far)

    flat = (tokens * heads, dk)
    q, k, v, qt, vt, before, scale, key_state, order.token = prepare(
        queries.reshape(flat), keys.reshape(flat), values.reshape(flat), order.token, tokens, heads, dk
    )
    forward = scan_states(key_state, n_ctx, 1, order)
    next(forward)
    starts = [c * CHUNK for c, _ in groups]
    part, order.token = early(pieces, starts, beside, out_weight, order.token)

    prefix = next(forward)
    state = None
    d, after, dq, dkp, dvp = {}, {}, {}, {}, {}

    def inner(c):
        dq[c], dkp[c], dvp[c], order.token = within(
            c, q, k, v, qt, vt, *d[c], scale, before, prefix, order.token, after[c], dict(dq) if c == 0 else {}, heads, dk
        )

    def outer(c, m):
        nonlocal state
        after[c + m - 1] = None if state is None else (state, 0)
        piece = order.tie(across[c])
        both = swap(piece, "head", n_head, far)
        out = late(c * CHUNK, c == 0, near, piece, both, out_weight, part, scale, qt, order.token, state, heads, dk)
        order.token = out[-1]
        state = out[1]
        for i in range(m):
            d[c + i] = (out[0], i)
            if i < m - 1:
                after[c + i] = (state, i + 1)

    waiting = []
    for c, m in groups:
        outer(c, m)
        waiting += list(range(c, c + m))[::-1]
        while c != 0 and waiting:
            inner(waiting.pop(0))
    backward = scan_states(state, n_ctx, -1, order)
    next(backward)
    while waiting:
        inner(waiting.pop(0))
    suffix = next(backward)
    d_keys, d_values = finish(
        k, v, [dkp[c] for c in range(n)], [dvp[c] for c in range(n)], suffix, order.token, heads, dk
    )
    return tuple(a.reshape(tokens, heads, dk) for a in (dq[0], d_keys, d_values))


def solution(mesh):
    in_specs = (
        P("ctx", "head", None),
        P("ctx", "head", None),
        P("ctx", "head", None),
        P("ctx", "head"),
        P("head", None),
    )
    out_specs = (P("ctx", "head", None), P("ctx", "head", None), P("ctx", "head", None))

    def program(queries, keys, values, d_layer, out_weight):
        return body(mesh.shape["ctx"], mesh.shape["head"], queries, keys, values, d_layer, out_weight)

    return jax.shard_map(program, mesh=mesh, in_specs=in_specs, out_specs=out_specs, check_vma=False)
```

```python
import functools

import jax
import jax.numpy as jnp
from jax import lax
from jax.experimental import pallas as pl
from jax.experimental.pallas import tpu as pltpu
from jax.sharding import PartitionSpec as P

CHUNK = 256
PAIR = 2
F32 = jnp.float32
BF16 = jnp.bfloat16
TOKEN = (8, 128)
NT = (((1,), (1,)), ((), ()))
NN = (((1,), (0,)), ((), ()))
FREE = pl.CostEstimate(flops=0, bytes_accessed=0, transcendentals=0)
VMEM_LIMIT = 14 * 1024 * 1024
WHOLE = pl.BlockSpec(memory_space=pltpu.VMEM)
ANYWHERE = pl.BlockSpec(memory_space=pl.ANY)


def dot(a, b, dims):
    return lax.dot_general(a, b, dims, preferred_element_type=F32)


def shape(dims, dtype):
    return jax.ShapeDtypeStruct(dims, dtype)


def outside(*arrays):
    return [pltpu.with_memory_space_constraint(a, pltpu.HBM) for a in arrays]


def part_of(i, size):
    return pl.ds(pl.multiple_of(i * size, size), size)


def call(kernel, name, args, in_specs, out_shape, out_specs, scratch=()):
    return pl.pallas_call(
        kernel,
        in_specs=in_specs,
        out_specs=out_specs,
        out_shape=out_shape,
        scratch_shapes=scratch,
        compiler_params=pltpu.CompilerParams(vmem_limit_bytes=VMEM_LIMIT),
        cost_estimate=FREE,
        name=name,
    )(*args)


def cut_kernel(starts, source, *refs):
    pieces, token_ref, sem = refs[: len(starts)], refs[-2], refs[-1]
    token_ref[...] = jnp.zeros_like(token_ref)
    copies = [
        pltpu.make_async_copy(source.at[pl.ds(start, piece.shape[0])], piece, sem.at[i])
        for i, (start, piece) in enumerate(zip(starts, pieces))
    ]
    for copy in copies:
        copy.start()
    for copy in copies:
        copy.wait()


def cut(d_layer, groups):
    features = d_layer.shape[1]
    return call(
        functools.partial(cut_kernel, [c * CHUNK for c, _ in groups]),
        "cut",
        outside(d_layer),
        [ANYWHERE],
        [shape((m * CHUNK, features), d_layer.dtype) for _, m in groups] + [shape(TOKEN, F32)],
        [WHOLE] * (len(groups) + 1),
        [pltpu.SemaphoreType.DMA((len(groups),))],
    )


def prepare_kernel(
    heads, dk, q_ref, k_ref, v_ref, _, qf_ref, kf_ref, vf_ref, qt_ref, vt_ref, before_ref, scale_ref, keep_ref, send_ref, token_ref,
    raw, wides, acc, sem
):
    n = qf_ref.shape[0] // CHUNK

    def load(i, c):
        source = (q_ref, k_ref, v_ref)[i].at[part_of(c, CHUNK * heads)]
        return pltpu.make_async_copy(source, raw.at[i, c], sem.at[i, c])

    for c in range(n):
        for i in range(3):
            load(i, c).start()
    token_ref[...] = jnp.zeros_like(token_ref)
    acc[...] = jnp.zeros_like(acc)
    tokens = scale_ref.shape[0]
    position = lax.axis_index("ctx") * tokens + lax.broadcasted_iota(jnp.int32, scale_ref.shape, 0)
    scale_ref[...] = lax.rsqrt((dk * (position + 1)).astype(F32))

    def one_chunk(c, _):
        rows = part_of(c, CHUNK)
        before_ref[c] = acc[...]
        for i in range(3):
            load(i, c).wait()
            wides[i] = raw[i, c].astype(F32)
        for h in range(heads):
            cols = slice(h * dk, (h + 1) * dk)
            mine = pl.ds(h, CHUNK, stride=heads)
            q, k, v = (wides[i, mine, :].astype(BF16) for i in range(3))
            qf_ref[rows, cols] = q
            kf_ref[rows, cols] = k
            vf_ref[rows, cols] = v
            qt_ref[cols, rows] = q.T
            vt = v.T
            vt_ref[cols, rows] = vt
            acc[h] += dot(vt, k, NN)
        return 0

    lax.fori_loop(0, n, one_chunk, 0)
    low, high = acc[: heads // 2].astype(BF16), acc[heads // 2 :].astype(BF16)
    first = lax.axis_index("ctx") % 2 == 0
    keep_ref[...] = jnp.where(first, low, high)
    send_ref[...] = jnp.where(first, high, low)


def prepare(q, k, v, token, tokens, heads, dk):
    n = tokens // CHUNK
    width = heads * dk
    return call(
        functools.partial(prepare_kernel, heads, dk),
        "prepare",
        [*outside(q, k, v), token],
        [ANYWHERE] * 4,
        [shape((tokens, width), BF16)] * 3
        + [shape((width, tokens), BF16)] * 2
        + [shape((n, heads, dk, dk), F32), shape((tokens, dk), F32)]
        + [shape((heads // 2, dk, dk), BF16)] * 2
        + [shape(TOKEN, F32)],
        [WHOLE] * 10,
        [
            pltpu.VMEM((3, n, CHUNK * heads, dk), BF16),
            pltpu.VMEM((3, CHUNK * heads, dk), F32),
            pltpu.VMEM((heads, dk, dk), F32),
            pltpu.SemaphoreType.DMA((3, n)),
        ],
    )


def early_kernel(starts, *refs):
    pieces, (b_ref, w_ref, _, out_ref, token_ref) = refs[: len(starts)], refs[len(starts) :]
    token_ref[...] = jnp.zeros_like(token_ref)
    features = b_ref.shape[1]
    place = lax.axis_index("head")
    first, second = part_of(place, features), part_of(place ^ 1, features)

    def one_tile(j, _):
        tile = part_of(j, PAIR * 128)
        wa, wb = w_ref[tile, first].T, w_ref[tile, second].T
        for start, piece in zip(starts, pieces):
            rows = slice(start, start + piece.shape[0])
            out_ref[rows, tile] = dot(piece[...], wa, NN) + dot(b_ref[rows, :], wb, NN)
        return 0

    lax.fori_loop(0, out_ref.shape[1] // (PAIR * 128), one_tile, 0)


def early(pieces, starts, b, weight, token):
    tokens = b.shape[0]
    width = weight.shape[0]
    return call(
        functools.partial(early_kernel, starts),
        "early",
        [*pieces, b, weight, token],
        [WHOLE] * (len(pieces) + 2) + [ANYWHERE],
        [shape((tokens, width), F32), shape(TOKEN, F32)],
        [WHOLE] * 2,
    )


def late_kernel(half, first, start, near, dk, a_ref, b_ref, w_ref, part_ref, scale_ref, qt_ref, _, *refs):
    state_ref, refs = (None, refs) if first else (refs[0], refs[1:])
    d_ref, out_ref, token_ref = refs[:3]
    tile = PAIR * dk
    token_ref[...] = jnp.zeros_like(token_ref)
    if half == 0:
        at, bt = a_ref, b_ref
    else:
        at, bt = refs[3:]
        at[...] = a_ref[...].T
        bt[...] = b_ref[...].T
    features, count = at.shape
    place = lax.axis_index("head")
    one, two = part_of(place ^ near, features), part_of(place ^ near ^ 1, features)
    steps = d_ref.shape[1] // tile
    here = slice(start, start + count)
    base = 0 if half is None else steps * (lax.axis_index("ctx") % 2 ^ half)

    def one_tile(local, _):
        j = base + local
        wide = part_of(j, tile)
        turned = dot(w_ref[wide, one], at[...], NN) + dot(w_ref[wide, two], bt[...], NN)
        low = (part_ref[here, wide] + turned.T).astype(BF16)
        d_ref[:, part_of(local, tile)] = low
        states = [None if first else state_ref[0, j * PAIR + i] for i in range(PAIR)]
        for c in reversed(range(count // CHUNK)):
            rows = slice(c * CHUNK, (c + 1) * CHUNK)
            there = slice(start + c * CHUNK, start + (c + 1) * CHUNK)
            for i in range(PAIR):
                grad = (low[rows, i * dk : (i + 1) * dk].astype(F32) * scale_ref[there, :]).astype(BF16)
                state = dot(qt_ref[part_of(j * PAIR + i, dk), there], grad, NN)
                states[i] = state if states[i] is None else states[i] + state
                if half is None:
                    out_ref[c, j * PAIR + i] = states[i]
        if half is not None:
            for i in range(PAIR):
                out_ref[local * PAIR + i] = states[i].astype(BF16)
        return 0

    lax.fori_loop(0, steps, one_tile, 0)


def late(start, half, near, a, b, weight, part, scale, qt, token, state, heads, dk):
    features, rows = a.shape if half == 0 else a.shape[::-1]
    width = weight.shape[0]
    args = [a, b, weight, part, scale, qt, token]
    in_specs = [WHOLE] * 6 + [ANYWHERE]
    if state is not None:
        args.append(state)
        in_specs.append(WHOLE)
    if half is None:
        out_shape = [shape((rows, width), BF16), shape((rows // CHUNK, heads, dk, dk), F32), shape(TOKEN, F32)]
    else:
        out_shape = [shape((rows, width // 2), BF16), shape((heads // 2, dk, dk), BF16), shape(TOKEN, F32)]
    turned = [] if half == 0 else [(features, rows)] * 2
    scratch = [pltpu.VMEM(dims, BF16) for dims in turned] if half is None else []
    if half == 1:
        out_shape += [shape(dims, BF16) for dims in turned]
    return call(
        functools.partial(late_kernel, half, state is None, start, near, dk),
        "late",
        args,
        in_specs,
        out_shape,
        [WHOLE] * len(out_shape),
        scratch,
    )


def within_kernel(
    heads, dk, chunk, at, level, others,
    q_ref, k_ref, v_ref, qt_ref, vt_ref, d_ref, also_ref, scale_ref, before_ref, own_ref, other_ref, _, *refs
):
    state_ref, refs = (None, refs) if level is None else (refs[0], refs[1:])
    earlier_dq, refs = refs[: len(others)], refs[len(others) :]
    dq_ref, dk_ref, dv_ref, token_ref, wide = refs[:5]
    token_ref[...] = jnp.zeros_like(token_ref)
    if others:
        low_ref, sem = refs[5:]
        copies = [
            pltpu.make_async_copy(source, dq_ref.at[pl.ds(c * CHUNK * heads, CHUNK * heads)], sem.at[i])
            for i, (c, source) in enumerate(zip(others, earlier_dq))
        ]
        for copy in copies:
            copy.start()
    rows = slice(chunk * CHUNK, (chunk + 1) * CHUNK)
    there = None if at is None else slice(at * CHUNK, (at + 1) * CHUNK)
    t = lax.broadcasted_iota(jnp.int32, (CHUNK, CHUNK), 0)
    s = lax.broadcasted_iota(jnp.int32, (CHUNK, CHUNK), 1)
    lower = s <= t
    upper = t <= s
    scale = scale_ref[rows, :]
    half = heads // 2

    for g, prefix_ref in enumerate((own_ref, other_ref)):
        for i in range(half):
            h = (lax.axis_index("ctx") % 2 ^ g) * half + i
            cols = part_of(h, dk)
            q, k, v = q_ref[rows, cols], k_ref[rows, cols], v_ref[rows, cols]
            if at is None:
                d = (d_ref, also_ref)[g][:, i * dk : (i + 1) * dk]
            else:
                d = d_ref[there, cols]
            grad = (d.astype(F32) * scale).astype(BF16)
            score_grad = jnp.where(lower, dot(grad, vt_ref[cols, rows], NN), 0.0).astype(BF16)
            score_grad_t = jnp.where(upper, dot(v, grad, NT), 0.0).astype(BF16)
            score_keys_t = jnp.where(upper, dot(k, qt_ref[cols, rows], NN), 0.0).astype(BF16)
            earlier = prefix_ref[i].astype(F32) + before_ref[chunk, h]
            dq = scale * dot(d, earlier.astype(BF16), NN) + dot(score_grad, k, NN)
            dkey = dot(score_grad_t, q, NN)
            dval = dot(score_keys_t, grad, NN)
            if state_ref is not None:
                after = state_ref[level, h].astype(BF16)
                dkey = dkey + dot(v, after, NT)
                dval = dval + dot(k, after, NN)
            wide[pl.ds(h, CHUNK, stride=heads), :] = dq
            dk_ref[:, cols] = dkey.astype(BF16)
            dv_ref[:, cols] = dval.astype(BF16)
    if others:
        low_ref[...] = wide[...].astype(BF16)
        last = pltpu.make_async_copy(
            low_ref, dq_ref.at[pl.ds(chunk * CHUNK * heads, CHUNK * heads)], sem.at[len(others)]
        )
        last.start()
        for copy in copies + [last]:
            copy.wait()
    else:
        dq_ref[...] = wide[...].astype(BF16)


def within(chunk, q, k, v, qt, vt, d, also, at, scale, before, own, other, token, state, others, heads, dk):
    tokens, width = q.shape
    args = [q, k, v, qt, vt, d, also, scale, before, own, other, token]
    in_specs = [WHOLE] * 11 + [ANYWHERE]
    level = None
    if state is not None:
        level = state[1]
        args.append(state[0])
        in_specs.append(WHOLE)
    args += list(others.values())
    in_specs += [WHOLE] * len(others)
    scratch = [pltpu.VMEM((CHUNK * heads, dk), F32)]
    rows = tokens if others else CHUNK
    if others:
        scratch += [pltpu.VMEM((CHUNK * heads, dk), BF16), pltpu.SemaphoreType.DMA((len(others) + 1,))]
    return call(
        functools.partial(within_kernel, heads, dk, chunk, at, level, list(others)),
        "within",
        args,
        in_specs,
        [shape((rows * heads, dk), BF16)] + [shape((CHUNK, width), BF16)] * 2 + [shape(TOKEN, F32)],
        [ANYWHERE if others else WHOLE] + [WHOLE] * 3,
        scratch,
    )


def finish_kernel(heads, dk, n, k_ref, v_ref, own_ref, other_ref, _, *refs):
    dkp, dvp, (dk_ref, dv_ref, wide_k, wide_v, low_k, low_v, sem) = refs[:n], refs[n : 2 * n], refs[2 * n :]
    half = heads // 2
    first = lax.axis_index("ctx") % 2 == 0
    after, turned = [], []
    for h in range(heads):
        own, other = own_ref[h % half], other_ref[h % half]
        one = jnp.where(first, own, other) if h < half else jnp.where(first, other, own)
        after.append(one)
        turned.append(one.T)
    copies = []
    for c in range(n):
        rows = slice(c * CHUNK, (c + 1) * CHUNK)
        for h in range(heads):
            cols = slice(h * dk, (h + 1) * dk)
            mine = pl.ds(h, CHUNK, stride=heads)
            wide_k[mine, :] = dkp[c][:, cols].astype(F32) + dot(v_ref[rows, cols], turned[h], NN)
            wide_v[mine, :] = dvp[c][:, cols].astype(F32) + dot(k_ref[rows, cols], after[h], NN)
        for i, (wide, low, out) in enumerate(((wide_k, low_k, dk_ref), (wide_v, low_v, dv_ref))):
            low[c] = wide[...].astype(BF16)
            copy = pltpu.make_async_copy(low.at[c], out.at[pl.ds(c * CHUNK * heads, CHUNK * heads)], sem.at[i, c])
            copy.start()
            copies.append(copy)
    for copy in copies:
        copy.wait()


def finish(k, v, dkp, dvp, own, other, token, heads, dk):
    tokens, width = k.shape
    n = tokens // CHUNK
    raw = (CHUNK * heads, dk)
    return call(
        functools.partial(finish_kernel, heads, dk, n),
        "finish",
        [k, v, own, other, token, *dkp, *dvp],
        [WHOLE] * 4 + [ANYWHERE] + [WHOLE] * (2 * n),
        [shape((tokens * heads, dk), BF16)] * 2,
        [ANYWHERE] * 2,
        [pltpu.VMEM(raw, F32)] * 2 + [pltpu.VMEM((n, *raw), BF16)] * 2 + [pltpu.SemaphoreType.DMA((2, n))],
    )


def swap(array, axis, size, bit):
    return lax.ppermute(array, axis, [(i, i ^ bit) for i in range(size)])


def shifted(array, size, step):
    return lax.ppermute(array, "ctx", [(i, i + step) for i in range(size) if 0 <= i + step < size])


class Order:
    def __init__(self):
        self.token = None

    def tie(self, array):
        array, self.token = lax.optimization_barrier((array, self.token))
        return array


def total_kernel(*refs):
    *terms, out = refs
    total = terms[0][...].astype(F32)
    for term in terms[1:]:
        total = total + term[...].astype(F32)
    out[...] = total.astype(BF16)


def ends_kernel(later_is_odd, own, came, *refs):
    *got, give, mine = refs
    exclusive = got[0][...].astype(F32)
    for term in got[1:]:
        exclusive = exclusive + term[...].astype(F32)
    later = (lax.axis_index("ctx") % 2 == 1) == later_is_odd
    give[...] = jnp.where(later, exclusive, exclusive + own[...].astype(F32)).astype(BF16)
    mine[...] = jnp.where(later, exclusive + came[...].astype(F32), exclusive).astype(BF16)


def scan_states(keep, send, size, direction, order):
    terms = [keep, swap(send, "ctx", size, 1)]
    yield None
    like = shape(keep.shape, BF16)
    step = 2
    while step < size:
        total = call(total_kernel, "total", terms, [WHOLE] * len(terms), like, WHOLE)
        terms.append(shifted(order.tie(total), size, direction * step))
        yield None
        step *= 2
    kernel = functools.partial(ends_kernel, direction == 1)
    give, mine = call(kernel, "ends", terms, [WHOLE] * len(terms), [like] * 2, [WHOLE] * 2)
    yield mine, swap(order.tie(give), "ctx", size, 1)


def body(n_ctx, n_head, queries, keys, values, d_layer, out_weight):
    tokens, heads, dk = queries.shape
    n = tokens // CHUNK
    near = n_head // 2
    far = 1
    groups = [(1, n - 1), (0, 1)]
    order = Order()
    *pieces, order.token = cut(d_layer, groups)
    across = {c: swap(piece, "head", n_head, near) for (c, _), piece in zip(groups, pieces)}
    beside = swap(d_layer, "head", n_head, far)

    flat = (tokens * heads, dk)
    q, k, v, qt, vt, before, scale, keep, send, order.token = prepare(
        queries.reshape(flat), keys.reshape(flat), values.reshape(flat), order.token, tokens, heads, dk
    )
    forward = scan_states(keep, send, n_ctx, 1, order)
    next(forward)
    starts = [c * CHUNK for c, _ in groups]
    part, order.token = early(pieces, starts, beside, out_weight, order.token)

    prefix = None
    while prefix is None:
        prefix = next(forward)
    d, after, dq, dkp, dvp = {}, {}, {}, {}, {}

    def inner(c):
        others = dict(dq) if c == 0 else {}
        dq[c], dkp[c], dvp[c], order.token = within(
            c, q, k, v, qt, vt, *d[c], scale, before, *prefix, order.token, after[c], others, heads, dk
        )

    state = None
    for c, m in groups[:-1]:
        after[c + m - 1] = None if state is None else (state, 0)
        piece = order.tie(across[c])
        both = swap(piece, "head", n_head, far)
        low, state, order.token = late(
            c * CHUNK, None, near, piece, both, out_weight, part, scale, qt, order.token, state, heads, dk
        )
        for i in range(m):
            d[c + i] = (low, low, i)
            if i < m - 1:
                after[c + i] = (state, i + 1)
        for i in reversed(range(m)):
            if c + i > 1:
                inner(c + i)
    after[0] = (state, 0)
    piece = order.tie(across[0])
    both = swap(piece, "head", n_head, far)
    low_send, send, order.token, *turned = late(
        0, 1, near, piece, both, out_weight, part, scale, qt, order.token, state, heads, dk
    )
    low_keep, keep, order.token = late(
        0, 0, near, *turned, out_weight, part, scale, qt, order.token, state, heads, dk
    )
    d[0] = (low_keep, low_send, None)
    backward = scan_states(keep, send, n_ctx, -1, order)
    next(backward)
    waiting = [1, 0]
    suffix = None
    while suffix is None:
        suffix = next(backward)
        if waiting:
            inner(waiting.pop(0))
    d_keys, d_values = finish(
        k, v, [dkp[c] for c in range(n)], [dvp[c] for c in range(n)], *suffix, order.token, heads, dk
    )
    return tuple(a.reshape(tokens, heads, dk) for a in (dq[0], d_keys, d_values))


def solution(mesh):
    in_specs = (
        P("ctx", "head", None),
        P("ctx", "head", None),
        P("ctx", "head", None),
        P("ctx", "head"),
        P("head", None),
    )
    out_specs = (P("ctx", "head", None), P("ctx", "head", None), P("ctx", "head", None))

    def program(queries, keys, values, d_layer, out_weight):
        return body(mesh.shape["ctx"], mesh.shape["head"], queries, keys, values, d_layer, out_weight)

    return jax.shard_map(program, mesh=mesh, in_specs=in_specs, out_specs=out_specs, check_vma=False)
```

```python
import functools

import jax
import jax.numpy as jnp
from jax import lax
from jax.experimental import pallas as pl
from jax.experimental.pallas import tpu as pltpu
from jax.sharding import PartitionSpec as P

CHUNK = 256
PAIR = 2
F32 = jnp.float32
BF16 = jnp.bfloat16
TOKEN = (8, 128)
NT = (((1,), (1,)), ((), ()))
NN = (((1,), (0,)), ((), ()))
FREE = pl.CostEstimate(flops=0, bytes_accessed=0, transcendentals=0)
VMEM_LIMIT = 14 * 1024 * 1024
WHOLE = pl.BlockSpec(memory_space=pltpu.VMEM)
ANYWHERE = pl.BlockSpec(memory_space=pl.ANY)


def dot(a, b, dims):
    return lax.dot_general(a, b, dims, preferred_element_type=F32)


def shape(dims, dtype):
    return jax.ShapeDtypeStruct(dims, dtype)


def outside(*arrays):
    return [pltpu.with_memory_space_constraint(a, pltpu.HBM) for a in arrays]


def part_of(i, size):
    return slice(i * size, (i + 1) * size) if isinstance(i, int) else pl.ds(pl.multiple_of(i * size, size), size)


def call(kernel, name, args, in_specs, out_shape, out_specs, scratch=()):
    return pl.pallas_call(
        kernel,
        in_specs=in_specs,
        out_specs=out_specs,
        out_shape=out_shape,
        scratch_shapes=scratch,
        compiler_params=pltpu.CompilerParams(vmem_limit_bytes=VMEM_LIMIT),
        cost_estimate=FREE,
        name=name,
    )(*args)


def cut_kernel(starts, source, *refs):
    pieces, token_ref, sem = refs[: len(starts)], refs[-2], refs[-1]
    token_ref[...] = jnp.zeros_like(token_ref)
    copies = [
        pltpu.make_async_copy(source.at[pl.ds(start, piece.shape[0])], piece, sem.at[i])
        for i, (start, piece) in enumerate(zip(starts, pieces))
    ]
    for copy in copies:
        copy.start()
    for copy in copies:
        copy.wait()


def cut(d_layer, groups):
    features = d_layer.shape[1]
    return call(
        functools.partial(cut_kernel, [c * CHUNK for c, _ in groups]),
        "cut",
        outside(d_layer),
        [ANYWHERE],
        [shape((m * CHUNK, features), d_layer.dtype) for _, m in groups] + [shape(TOKEN, F32)],
        [WHOLE] * (len(groups) + 1),
        [pltpu.SemaphoreType.DMA((len(groups),))],
    )


def prepare_kernel(
    heads, dk, q_ref, k_ref, v_ref, _, qf_ref, kf_ref, vf_ref, qt_ref, vt_ref, before_ref, scale_ref, keep_ref, send_ref, token_ref,
    raw, wides, acc, sem
):
    n = qf_ref.shape[0] // CHUNK

    def load(i, c):
        source = (q_ref, k_ref, v_ref)[i].at[part_of(c, CHUNK * heads)]
        return pltpu.make_async_copy(source, raw.at[i, c], sem.at[i, c])

    for c in range(n):
        for i in range(3):
            load(i, c).start()
    token_ref[...] = jnp.zeros_like(token_ref)
    acc[...] = jnp.zeros_like(acc)
    tokens = scale_ref.shape[0]
    position = lax.axis_index("ctx") * tokens + lax.broadcasted_iota(jnp.int32, scale_ref.shape, 0)
    scale_ref[...] = lax.rsqrt((dk * (position + 1)).astype(F32))

    def one_chunk(c, _):
        rows = part_of(c, CHUNK)
        before_ref[c] = acc[...]
        for i in range(3):
            load(i, c).wait()
            wides[i] = raw[i, c].astype(F32)
        for h in range(heads):
            cols = slice(h * dk, (h + 1) * dk)
            mine = pl.ds(h, CHUNK, stride=heads)
            q, k, v = (wides[i, mine, :].astype(BF16) for i in range(3))
            qf_ref[rows, cols] = q
            kf_ref[rows, cols] = k
            vf_ref[rows, cols] = v
            qt_ref[cols, rows] = q.T
            vt = v.T
            vt_ref[cols, rows] = vt
            acc[h] += dot(vt, k, NN)
        return 0

    lax.fori_loop(0, n, one_chunk, 0)
    low, high = acc[: heads // 2].astype(BF16), acc[heads // 2 :].astype(BF16)
    first = lax.axis_index("ctx") % 2 == 0
    keep_ref[...] = jnp.where(first, low, high)
    send_ref[...] = jnp.where(first, high, low)


def prepare(q, k, v, token, tokens, heads, dk):
    n = tokens // CHUNK
    width = heads * dk
    return call(
        functools.partial(prepare_kernel, heads, dk),
        "prepare",
        [*outside(q, k, v), token],
        [ANYWHERE] * 4,
        [shape((tokens, width), BF16)] * 3
        + [shape((width, tokens), BF16)] * 2
        + [shape((n, heads, dk, dk), F32), shape((tokens, dk), F32)]
        + [shape((heads // 2, dk, dk), BF16)] * 2
        + [shape(TOKEN, F32)],
        [WHOLE] * 10,
        [
            pltpu.VMEM((3, n, CHUNK * heads, dk), BF16),
            pltpu.VMEM((3, CHUNK * heads, dk), F32),
            pltpu.VMEM((heads, dk, dk), F32),
            pltpu.SemaphoreType.DMA((3, n)),
        ],
    )


def early_kernel(starts, *refs):
    pieces, (b_ref, w_ref, _, out_ref, token_ref) = refs[: len(starts)], refs[len(starts) :]
    token_ref[...] = jnp.zeros_like(token_ref)
    features = b_ref.shape[1]
    place = lax.axis_index("head")
    first, second = part_of(place, features), part_of(place ^ 1, features)

    def one_tile(j, _):
        tile = part_of(j, PAIR * 128)
        wa, wb = w_ref[tile, first].T, w_ref[tile, second].T
        for start, piece in zip(starts, pieces):
            rows = slice(start, start + piece.shape[0])
            out_ref[rows, tile] = dot(piece[...], wa, NN) + dot(b_ref[rows, :], wb, NN)
        return 0

    lax.fori_loop(0, out_ref.shape[1] // (PAIR * 128), one_tile, 0)


def early(pieces, starts, b, weight, token):
    tokens = b.shape[0]
    width = weight.shape[0]
    return call(
        functools.partial(early_kernel, starts),
        "early",
        [*pieces, b, weight, token],
        [WHOLE] * (len(pieces) + 2) + [ANYWHERE],
        [shape((tokens, width), F32), shape(TOKEN, F32)],
        [WHOLE] * 2,
    )


def late_kernel(half, first, start, near, dk, a_ref, b_ref, w_ref, part_ref, scale_ref, qt_ref, _, *refs):
    state_ref, refs = (None, refs) if first else (refs[0], refs[1:])
    d_ref, token_ref = refs[:2]
    tile = PAIR * dk
    steps = d_ref.shape[1] // tile
    outs, refs = (refs[2:3], refs[3:]) if half is None else (refs[2 : 2 + steps], refs[2 + steps :])
    token_ref[...] = jnp.zeros_like(token_ref)
    if half == 0:
        at, bt = a_ref, b_ref
    else:
        at, bt = refs
        at[...] = a_ref[...].T
        bt[...] = b_ref[...].T
    features, count = at.shape
    place = lax.axis_index("head")
    one, two = part_of(place ^ near, features), part_of(place ^ near ^ 1, features)
    here = slice(start, start + count)
    base = 0 if half is None else steps * (lax.axis_index("ctx") % 2 ^ half)

    def one_tile(local, _):
        j = base + local
        wide = part_of(j, tile)
        turned = dot(w_ref[wide, one], at[...], NN) + dot(w_ref[wide, two], bt[...], NN)
        low = (part_ref[here, wide] + turned.T).astype(BF16)
        d_ref[:, part_of(local, tile)] = low
        states = [None if first else state_ref[0, j * PAIR + i] for i in range(PAIR)]
        for c in reversed(range(count // CHUNK)):
            rows = slice(c * CHUNK, (c + 1) * CHUNK)
            there = slice(start + c * CHUNK, start + (c + 1) * CHUNK)
            for i in range(PAIR):
                grad = (low[rows, i * dk : (i + 1) * dk].astype(F32) * scale_ref[there, :]).astype(BF16)
                state = dot(qt_ref[part_of(j * PAIR + i, dk), there], grad, NN)
                states[i] = state if states[i] is None else states[i] + state
                if half is None:
                    outs[0][c, j * PAIR + i] = states[i]
        if half is not None:
            for i in range(PAIR):
                outs[local][i] = states[i].astype(BF16)
        return 0

    if half is None:
        lax.fori_loop(0, steps, one_tile, 0)
    else:
        for local in range(steps):
            one_tile(local, 0)


def late(start, half, near, a, b, weight, part, scale, qt, token, state, heads, dk):
    features, rows = a.shape if half == 0 else a.shape[::-1]
    width = weight.shape[0]
    args = [a, b, weight, part, scale, qt, token]
    in_specs = [WHOLE] * 6 + [ANYWHERE]
    if state is not None:
        args.append(state)
        in_specs.append(WHOLE)
    if half is None:
        out_shape = [shape((rows, width), BF16), shape(TOKEN, F32), shape((rows // CHUNK, heads, dk, dk), F32)]
    else:
        out_shape = [shape((rows, width // 2), BF16), shape(TOKEN, F32)]
        out_shape += [shape((PAIR, dk, dk), BF16)] * (heads // 2 // PAIR)
    turned = [] if half == 0 else [(features, rows)] * 2
    scratch = [pltpu.VMEM(dims, BF16) for dims in turned] if half is None else []
    if half == 1:
        out_shape += [shape(dims, BF16) for dims in turned]
    return call(
        functools.partial(late_kernel, half, state is None, start, near, dk),
        "late",
        args,
        in_specs,
        out_shape,
        [WHOLE] * len(out_shape),
        scratch,
    )


def within_kernel(
    heads, dk, chunk, at, level, others,
    q_ref, k_ref, v_ref, qt_ref, vt_ref, d_ref, also_ref, scale_ref, before_ref, own_ref, other_ref, _, *refs
):
    state_ref, refs = (None, refs) if level is None else (refs[0], refs[1:])
    earlier_dq, refs = refs[: len(others)], refs[len(others) :]
    dq_ref, dk_ref, dv_ref, token_ref, wide = refs[:5]
    token_ref[...] = jnp.zeros_like(token_ref)
    if others:
        low_ref, sem = refs[5:]
        copies = [
            pltpu.make_async_copy(source, dq_ref.at[pl.ds(c * CHUNK * heads, CHUNK * heads)], sem.at[i])
            for i, (c, source) in enumerate(zip(others, earlier_dq))
        ]
        for copy in copies:
            copy.start()
    rows = slice(chunk * CHUNK, (chunk + 1) * CHUNK)
    there = None if at is None else slice(at * CHUNK, (at + 1) * CHUNK)
    t = lax.broadcasted_iota(jnp.int32, (CHUNK, CHUNK), 0)
    s = lax.broadcasted_iota(jnp.int32, (CHUNK, CHUNK), 1)
    lower = s <= t
    upper = t <= s
    scale = scale_ref[rows, :]
    half = heads // 2

    for g, prefix_ref in enumerate((own_ref, other_ref)):
        for i in range(half):
            h = (lax.axis_index("ctx") % 2 ^ g) * half + i
            cols = part_of(h, dk)
            q, k, v = q_ref[rows, cols], k_ref[rows, cols], v_ref[rows, cols]
            if at is None:
                d = (d_ref, also_ref)[g][:, i * dk : (i + 1) * dk]
            else:
                d = d_ref[there, cols]
            grad = (d.astype(F32) * scale).astype(BF16)
            score_grad = jnp.where(lower, dot(grad, vt_ref[cols, rows], NN), 0.0).astype(BF16)
            score_grad_t = jnp.where(upper, dot(v, grad, NT), 0.0).astype(BF16)
            score_keys_t = jnp.where(upper, dot(k, qt_ref[cols, rows], NN), 0.0).astype(BF16)
            earlier = prefix_ref[i].astype(F32) + before_ref[chunk, h]
            dq = scale * dot(d, earlier.astype(BF16), NN) + dot(score_grad, k, NN)
            dkey = dot(score_grad_t, q, NN)
            dval = dot(score_keys_t, grad, NN)
            if state_ref is not None:
                after = state_ref[level, h].astype(BF16)
                dkey = dkey + dot(v, after, NT)
                dval = dval + dot(k, after, NN)
            wide[pl.ds(h, CHUNK, stride=heads), :] = dq
            dk_ref[:, cols] = dkey.astype(BF16)
            dv_ref[:, cols] = dval.astype(BF16)
    if others:
        low_ref[...] = wide[...].astype(BF16)
        last = pltpu.make_async_copy(
            low_ref, dq_ref.at[pl.ds(chunk * CHUNK * heads, CHUNK * heads)], sem.at[len(others)]
        )
        last.start()
        for copy in copies + [last]:
            copy.wait()
    else:
        dq_ref[...] = wide[...].astype(BF16)


def within(chunk, q, k, v, qt, vt, d, also, at, scale, before, own, other, token, state, others, heads, dk):
    tokens, width = q.shape
    args = [q, k, v, qt, vt, d, also, scale, before, own, other, token]
    in_specs = [WHOLE] * 11 + [ANYWHERE]
    level = None
    if state is not None:
        level = state[1]
        args.append(state[0])
        in_specs.append(WHOLE)
    args += list(others.values())
    in_specs += [WHOLE] * len(others)
    scratch = [pltpu.VMEM((CHUNK * heads, dk), F32)]
    rows = tokens if others else CHUNK
    if others:
        scratch += [pltpu.VMEM((CHUNK * heads, dk), BF16), pltpu.SemaphoreType.DMA((len(others) + 1,))]
    return call(
        functools.partial(within_kernel, heads, dk, chunk, at, level, list(others)),
        "within",
        args,
        in_specs,
        [shape((rows * heads, dk), BF16)] + [shape((CHUNK, width), BF16)] * 2 + [shape(TOKEN, F32)],
        [ANYWHERE if others else WHOLE] + [WHOLE] * 3,
        scratch,
    )


def finish_kernel(heads, dk, n, parts, k_ref, v_ref, _, *refs):
    own, other, refs = refs[:parts], refs[parts : 2 * parts], refs[2 * parts :]
    dkp, dvp, (dk_ref, dv_ref, after, turned, wide_k, wide_v, low_k, low_v, sem) = refs[:n], refs[n : 2 * n], refs[2 * n :]
    first = lax.axis_index("ctx") % 2 == 0
    after[...] = jnp.zeros_like(after)
    turned[...] = jnp.zeros_like(turned)
    for p in range(parts):
        for i in range(PAIR):
            mine, its = own[p][i], other[p][i]
            cols = slice(i * dk, (i + 1) * dk)
            for place, one in ((p, jnp.where(first, mine, its)), (parts + p, jnp.where(first, its, mine))):
                after[place, cols, cols] = one
                turned[place, cols, cols] = one.T
    copies = []
    for c in range(n):
        rows = slice(c * CHUNK, (c + 1) * CHUNK)
        for p in range(heads // PAIR):
            cols = slice(p * PAIR * dk, (p + 1) * PAIR * dk)
            full_k = dkp[c][:, cols].astype(F32) + dot(v_ref[rows, cols], turned[p], NN)
            full_v = dvp[c][:, cols].astype(F32) + dot(k_ref[rows, cols], after[p], NN)
            for i in range(PAIR):
                mine = pl.ds(p * PAIR + i, CHUNK, stride=heads)
                wide_k[mine, :] = full_k[:, i * dk : (i + 1) * dk]
                wide_v[mine, :] = full_v[:, i * dk : (i + 1) * dk]
        for i, (wide, low, out) in enumerate(((wide_k, low_k, dk_ref), (wide_v, low_v, dv_ref))):
            low[c] = wide[...].astype(BF16)
            copy = pltpu.make_async_copy(low.at[c], out.at[pl.ds(c * CHUNK * heads, CHUNK * heads)], sem.at[i, c])
            copy.start()
            copies.append(copy)
    for copy in copies:
        copy.wait()


def finish(k, v, dkp, dvp, own, other, token, heads, dk):
    tokens, width = k.shape
    n = tokens // CHUNK
    raw = (CHUNK * heads, dk)
    return call(
        functools.partial(finish_kernel, heads, dk, n, len(own)),
        "finish",
        [k, v, token, *own, *other, *dkp, *dvp],
        [WHOLE] * 2 + [ANYWHERE] + [WHOLE] * (2 * len(own) + 2 * n),
        [shape((tokens * heads, dk), BF16)] * 2,
        [ANYWHERE] * 2,
        [pltpu.VMEM((heads // PAIR, PAIR * dk, PAIR * dk), BF16)] * 2
        + [pltpu.VMEM(raw, F32)] * 2
        + [pltpu.VMEM((n, *raw), BF16)] * 2
        + [pltpu.SemaphoreType.DMA((2, n))],
    )


def swap(array, axis, size, bit):
    return lax.ppermute(array, axis, [(i, i ^ bit) for i in range(size)])


def shifted(array, size, step):
    return lax.ppermute(array, "ctx", [(i, i + step) for i in range(size) if 0 <= i + step < size])


class Order:
    def __init__(self):
        self.token = None

    def tie(self, array):
        array, self.token = lax.optimization_barrier((array, self.token))
        return array


def total_kernel(*refs):
    *terms, out = refs
    total = terms[0][...].astype(F32)
    for term in terms[1:]:
        total = total + term[...].astype(F32)
    out[...] = total.astype(BF16)


def ends_kernel(later_is_odd, own, came, *refs):
    *got, give, mine = refs
    exclusive = got[0][...].astype(F32)
    for term in got[1:]:
        exclusive = exclusive + term[...].astype(F32)
    later = (lax.axis_index("ctx") % 2 == 1) == later_is_odd
    give[...] = jnp.where(later, exclusive, exclusive + own[...].astype(F32)).astype(BF16)
    mine[...] = jnp.where(later, exclusive + came[...].astype(F32), exclusive).astype(BF16)


def scan_states(keep, send, size, direction, order):
    terms = [[own, swap(away, "ctx", size, 1)] for own, away in zip(keep, send)]
    yield None
    like = shape(keep[0].shape, BF16)
    step = 2
    while step < size:
        for part in terms:
            total = call(total_kernel, "total", part, [WHOLE] * len(part), like, WHOLE)
            part.append(shifted(order.tie(total), size, direction * step))
        yield None
        step *= 2
    kernel = functools.partial(ends_kernel, direction == 1)
    mine, other = [], []
    for part in terms:
        give, own = call(kernel, "ends", part, [WHOLE] * len(part), [like] * 2, [WHOLE] * 2)
        mine.append(own)
        other.append(swap(order.tie(give), "ctx", size, 1))
    yield mine, other


def body(n_ctx, n_head, queries, keys, values, d_layer, out_weight):
    tokens, heads, dk = queries.shape
    n = tokens // CHUNK
    near = n_head // 2
    far = 1
    groups = [(1, n - 1), (0, 1)]
    order = Order()
    *pieces, order.token = cut(d_layer, groups)
    across = {c: swap(piece, "head", n_head, near) for (c, _), piece in zip(groups, pieces)}
    beside = swap(d_layer, "head", n_head, far)

    flat = (tokens * heads, dk)
    q, k, v, qt, vt, before, scale, keep, send, order.token = prepare(
        queries.reshape(flat), keys.reshape(flat), values.reshape(flat), order.token, tokens, heads, dk
    )
    forward = scan_states([keep], [send], n_ctx, 1, order)
    next(forward)
    starts = [c * CHUNK for c, _ in groups]
    part, order.token = early(pieces, starts, beside, out_weight, order.token)

    prefix = None
    while prefix is None:
        prefix = next(forward)
    prefix = [prefix[0][0], order.tie(prefix[1][0])]
    d, after, dq, dkp, dvp = {}, {}, {}, {}, {}

    def inner(c):
        others = dict(dq) if c == 0 else {}
        dq[c], dkp[c], dvp[c], order.token = within(
            c, q, k, v, qt, vt, *d[c], scale, before, *prefix, order.token, after[c], others, heads, dk
        )

    state = None
    for c, m in groups[:-1]:
        after[c + m - 1] = None if state is None else (state, 0)
        piece = order.tie(across[c])
        both = swap(piece, "head", n_head, far)
        low, order.token, state = late(
            c * CHUNK, None, near, piece, both, out_weight, part, scale, qt, order.token, state, heads, dk
        )
        for i in range(m):
            d[c + i] = (low, low, i)
            if i < m - 1:
                after[c + i] = (state, i + 1)
        for i in reversed(range(m)):
            if c + i > 1:
                inner(c + i)
    after[0] = (state, 0)
    piece = order.tie(across[0])
    both = swap(piece, "head", n_head, far)
    low_send, order.token, *send = late(
        0, 1, near, piece, both, out_weight, part, scale, qt, order.token, state, heads, dk
    )
    *send, turned_a, turned_b = send
    low_keep, order.token, *keep = late(
        0, 0, near, turned_a, turned_b, out_weight, part, scale, qt, order.token, state, heads, dk
    )
    d[0] = (low_keep, low_send, None)
    backward = scan_states(keep, send, n_ctx, -1, order)
    next(backward)
    waiting = [1, 0]
    suffix = None
    while suffix is None:
        suffix = next(backward)
        if waiting:
            inner(waiting.pop(0))
    d_keys, d_values = finish(
        k, v, [dkp[c] for c in range(n)], [dvp[c] for c in range(n)], *suffix, order.token, heads, dk
    )
    return tuple(a.reshape(tokens, heads, dk) for a in (dq[0], d_keys, d_values))


def solution(mesh):
    in_specs = (
        P("ctx", "head", None),
        P("ctx", "head", None),
        P("ctx", "head", None),
        P("ctx", "head"),
        P("head", None),
    )
    out_specs = (P("ctx", "head", None), P("ctx", "head", None), P("ctx", "head", None))

    def program(queries, keys, values, d_layer, out_weight):
        return body(mesh.shape["ctx"], mesh.shape["head"], queries, keys, values, d_layer, out_weight)

    return jax.shard_map(program, mesh=mesh, in_specs=in_specs, out_specs=out_specs, check_vma=False)
```

```python
import functools

import jax
import jax.numpy as jnp
from jax import lax
from jax.experimental import pallas as pl
from jax.experimental.pallas import tpu as pltpu
from jax.sharding import PartitionSpec as P

CHUNK = 256
PAIR = 2
F32 = jnp.float32
BF16 = jnp.bfloat16
TOKEN = (8, 128)
NT = (((1,), (1,)), ((), ()))
NN = (((1,), (0,)), ((), ()))
FREE = pl.CostEstimate(flops=0, bytes_accessed=0, transcendentals=0)
VMEM_LIMIT = 14 * 1024 * 1024
WHOLE = pl.BlockSpec(memory_space=pltpu.VMEM)
ANYWHERE = pl.BlockSpec(memory_space=pl.ANY)


def dot(a, b, dims):
    return lax.dot_general(a, b, dims, preferred_element_type=F32)


def shape(dims, dtype):
    return jax.ShapeDtypeStruct(dims, dtype)


def outside(*arrays):
    return [pltpu.with_memory_space_constraint(a, pltpu.HBM) for a in arrays]


def part_of(i, size):
    return slice(i * size, (i + 1) * size) if isinstance(i, int) else pl.ds(pl.multiple_of(i * size, size), size)


def call(kernel, name, args, in_specs, out_shape, out_specs, scratch=(), aliases=None):
    return pl.pallas_call(
        kernel,
        in_specs=in_specs,
        out_specs=out_specs,
        out_shape=out_shape,
        scratch_shapes=scratch,
        input_output_aliases=aliases or {},
        compiler_params=pltpu.CompilerParams(vmem_limit_bytes=VMEM_LIMIT),
        cost_estimate=FREE,
        name=name,
    )(*args)


def cut_kernel(starts, source, *refs):
    pieces, token_ref, sem = refs[: len(starts)], refs[-2], refs[-1]
    token_ref[...] = jnp.zeros_like(token_ref)
    copies = [
        pltpu.make_async_copy(source.at[pl.ds(start, piece.shape[0])], piece, sem.at[i])
        for i, (start, piece) in enumerate(zip(starts, pieces))
    ]
    for copy in copies:
        copy.start()
    for copy in copies:
        copy.wait()


def cut(d_layer, groups):
    features = d_layer.shape[1]
    return call(
        functools.partial(cut_kernel, [c * CHUNK for c, _ in groups]),
        "cut",
        outside(d_layer),
        [ANYWHERE],
        [shape((m * CHUNK, features), d_layer.dtype) for _, m in groups] + [shape(TOKEN, F32)],
        [WHOLE] * (len(groups) + 1),
        [pltpu.SemaphoreType.DMA((len(groups),))],
    )


def prepare_kernel(
    heads, dk, q_ref, k_ref, v_ref, _, qf_ref, kf_ref, vf_ref, qt_ref, vt_ref, before_ref, scale_ref, keep_ref, send_ref, token_ref,
    raw, wides, acc, sem
):
    n = qf_ref.shape[0] // CHUNK

    def load(i, c):
        source = (q_ref, k_ref, v_ref)[i].at[part_of(c, CHUNK * heads)]
        return pltpu.make_async_copy(source, raw.at[i, c], sem.at[i, c])

    for c in range(n):
        for i in range(3):
            load(i, c).start()
    token_ref[...] = jnp.zeros_like(token_ref)
    acc[...] = jnp.zeros_like(acc)
    tokens = scale_ref.shape[0]
    position = lax.axis_index("ctx") * tokens + lax.broadcasted_iota(jnp.int32, scale_ref.shape, 0)
    scale_ref[...] = lax.rsqrt((dk * (position + 1)).astype(F32))

    def one_chunk(c, _):
        rows = part_of(c, CHUNK)
        before_ref[c] = acc[...]
        for i in range(3):
            load(i, c).wait()
            wides[i] = raw[i, c].astype(F32)
        for h in range(heads):
            cols = slice(h * dk, (h + 1) * dk)
            mine = pl.ds(h, CHUNK, stride=heads)
            q, k, v = (wides[i, mine, :].astype(BF16) for i in range(3))
            qf_ref[rows, cols] = q
            kf_ref[rows, cols] = k
            vf_ref[rows, cols] = v
            qt_ref[cols, rows] = q.T
            vt = v.T
            vt_ref[cols, rows] = vt
            acc[h] += dot(vt, k, NN)
        return 0

    lax.fori_loop(0, n, one_chunk, 0)
    low, high = acc[: heads // 2].astype(BF16), acc[heads // 2 :].astype(BF16)
    first = lax.axis_index("ctx") % 2 == 0
    keep_ref[...] = jnp.where(first, low, high)
    send_ref[...] = jnp.where(first, high, low)


def prepare(q, k, v, token, tokens, heads, dk):
    n = tokens // CHUNK
    width = heads * dk
    return call(
        functools.partial(prepare_kernel, heads, dk),
        "prepare",
        [*outside(q, k, v), token],
        [ANYWHERE] * 4,
        [shape((tokens, width), BF16)] * 3
        + [shape((width, tokens), BF16)] * 2
        + [shape((n, heads, dk, dk), F32), shape((tokens, dk), F32)]
        + [shape((heads // 2, dk, dk), BF16)] * 2
        + [shape(TOKEN, F32)],
        [WHOLE] * 10,
        [
            pltpu.VMEM((3, n, CHUNK * heads, dk), BF16),
            pltpu.VMEM((3, CHUNK * heads, dk), F32),
            pltpu.VMEM((heads, dk, dk), F32),
            pltpu.SemaphoreType.DMA((3, n)),
        ],
    )


def early_kernel(starts, *refs):
    pieces, (b_ref, w_ref, _, out_ref, token_ref) = refs[: len(starts)], refs[len(starts) :]
    token_ref[...] = jnp.zeros_like(token_ref)
    features = b_ref.shape[1]
    place = lax.axis_index("head")
    first, second = part_of(place, features), part_of(place ^ 1, features)

    def one_tile(j, _):
        tile = part_of(j, PAIR * 128)
        wa, wb = w_ref[tile, first].T, w_ref[tile, second].T
        for start, piece in zip(starts, pieces):
            rows = slice(start, start + piece.shape[0])
            out_ref[rows, tile] = dot(piece[...], wa, NN) + dot(b_ref[rows, :], wb, NN)
        return 0

    lax.fori_loop(0, out_ref.shape[1] // (PAIR * 128), one_tile, 0)


def early(pieces, starts, b, weight, token):
    tokens = b.shape[0]
    width = weight.shape[0]
    return call(
        functools.partial(early_kernel, starts),
        "early",
        [*pieces, b, weight, token],
        [WHOLE] * (len(pieces) + 2) + [ANYWHERE],
        [shape((tokens, width), F32), shape(TOKEN, F32)],
        [WHOLE] * 2,
    )


def late_kernel(half, first, start, near, dk, b_ref, w_ref, part_ref, scale_ref, qt_ref, _, *refs):
    a_ref, refs = (refs[0], refs[1:]) if half is None else (None, refs)
    state_ref, refs = (None, refs) if first else (refs[0], refs[1:])
    d_ref, token_ref = refs[:2]
    tile = PAIR * dk
    steps = d_ref.shape[1] // tile
    out_ref, refs = refs[2], refs[3:]
    token_ref[...] = jnp.zeros_like(token_ref)
    if half is None:
        at, bt = refs
        at[...] = a_ref[...].T
        bt[...] = b_ref[...].T
    elif half == 1:
        (bt,) = refs
        bt[...] = b_ref[...].T
    else:
        bt = b_ref
    features, count = bt.shape
    place = lax.axis_index("head")
    one, two = part_of(place ^ near, features), part_of(place ^ near ^ 1, features)
    here = slice(start, start + count)
    base = 0 if half is None else steps * (lax.axis_index("ctx") % 2 ^ half)

    def one_tile(local, _):
        j = base + local
        wide = part_of(j, tile)
        turned = dot(w_ref[wide, two], bt[...], NN)
        if half is None:
            turned = turned + dot(w_ref[wide, one], at[...], NN)
        low = (part_ref[here if half is None else slice(0, count), wide] + turned.T).astype(BF16)
        d_ref[:, part_of(local, tile)] = low
        states = [None if first else state_ref[0, j * PAIR + i] for i in range(PAIR)]
        for c in reversed(range(count // CHUNK)):
            rows = slice(c * CHUNK, (c + 1) * CHUNK)
            there = slice(start + c * CHUNK, start + (c + 1) * CHUNK)
            for i in range(PAIR):
                grad = (low[rows, i * dk : (i + 1) * dk].astype(F32) * scale_ref[there, :]).astype(BF16)
                state = dot(qt_ref[part_of(j * PAIR + i, dk), there], grad, NN)
                states[i] = state if states[i] is None else states[i] + state
                if half is None:
                    out_ref[c, j * PAIR + i] = states[i]
        if half is not None:
            for i in range(PAIR):
                out_ref[local * PAIR + i] = states[i].astype(BF16)
        return 0

    if half is None:
        lax.fori_loop(0, steps, one_tile, 0)
    else:
        for local in range(steps):
            one_tile(local, 0)


def middle_kernel(start, near, a_ref, w_ref, part_ref, _, out_ref, token_ref, at):
    token_ref[...] = jnp.zeros_like(token_ref)
    at[...] = a_ref[...].T
    features, count = at.shape
    one = part_of(lax.axis_index("head") ^ near, features)
    tile = PAIR * 128
    for j in range(out_ref.shape[1] // tile):
        wide = slice(j * tile, (j + 1) * tile)
        out_ref[:, wide] = part_ref[start : start + count, wide] + dot(w_ref[wide, one], at[...], NN).T


def middle(start, near, a, weight, part, token):
    return call(
        functools.partial(middle_kernel, start, near),
        "middle",
        [a, weight, part, token],
        [WHOLE] * 3 + [ANYWHERE],
        [shape((a.shape[0], part.shape[1]), F32), shape(TOKEN, F32)],
        [WHOLE] * 2,
        [pltpu.VMEM(a.shape[::-1], BF16)],
    )


def late(start, half, near, a, b, weight, part, scale, qt, token, state, heads, dk):
    features, rows = b.shape if half == 0 else b.shape[::-1]
    width = weight.shape[0]
    args = [b, weight, part, scale, qt, token]
    in_specs = [WHOLE] * 5 + [ANYWHERE]
    if half is None:
        args.append(a)
        in_specs.append(WHOLE)
    if state is not None:
        args.append(state)
        in_specs.append(WHOLE)
    if half is None:
        out_shape = [shape((rows, width), BF16), shape(TOKEN, F32), shape((rows // CHUNK, heads, dk, dk), F32)]
    else:
        out_shape = [shape((rows, width // 2), BF16), shape(TOKEN, F32)]
        out_shape.append(shape((heads // 2, dk, dk), BF16))
    scratch = [pltpu.VMEM((features, rows), BF16)] * 2 if half is None else []
    if half == 1:
        out_shape.append(shape((features, rows), BF16))
    return call(
        functools.partial(late_kernel, half, state is None, start, near, dk),
        "late",
        args,
        in_specs,
        out_shape,
        [WHOLE] * len(out_shape),
        scratch,
    )


def within_kernel(
    heads, dk, chunk, at, level, others,
    q_ref, k_ref, v_ref, qt_ref, vt_ref, d_ref, also_ref, scale_ref, before_ref, own_ref, other_ref, _, *refs
):
    state_ref, refs = (None, refs) if level is None else (refs[0], refs[1:])
    earlier_dq, refs = refs[: len(others)], refs[len(others) :]
    dq_ref, dk_ref, dv_ref, token_ref, wide = refs[:5]
    token_ref[...] = jnp.zeros_like(token_ref)
    if others:
        low_ref, sem = refs[5:]
        copies = [
            pltpu.make_async_copy(source, dq_ref.at[pl.ds(c * CHUNK * heads, CHUNK * heads)], sem.at[i])
            for i, (c, source) in enumerate(zip(others, earlier_dq))
        ]
        for copy in copies:
            copy.start()
    rows = slice(chunk * CHUNK, (chunk + 1) * CHUNK)
    there = None if at is None else slice(at * CHUNK, (at + 1) * CHUNK)
    t = lax.broadcasted_iota(jnp.int32, (CHUNK, CHUNK), 0)
    s = lax.broadcasted_iota(jnp.int32, (CHUNK, CHUNK), 1)
    lower = s <= t
    upper = t <= s
    scale = scale_ref[rows, :]
    half = heads // 2

    for g, prefix_ref in enumerate((own_ref, other_ref)):
        for i in range(half):
            h = (lax.axis_index("ctx") % 2 ^ g) * half + i
            cols = part_of(h, dk)
            q, k, v = q_ref[rows, cols], k_ref[rows, cols], v_ref[rows, cols]
            if at is None:
                d = (d_ref, also_ref)[g][:, i * dk : (i + 1) * dk]
            else:
                d = d_ref[there, cols]
            grad = (d.astype(F32) * scale).astype(BF16)
            score_grad = jnp.where(lower, dot(grad, vt_ref[cols, rows], NN), 0.0).astype(BF16)
            score_grad_t = jnp.where(upper, dot(v, grad, NT), 0.0).astype(BF16)
            score_keys_t = jnp.where(upper, dot(k, qt_ref[cols, rows], NN), 0.0).astype(BF16)
            earlier = prefix_ref[i].astype(F32) + before_ref[chunk, h]
            dq = scale * dot(d, earlier.astype(BF16), NN) + dot(score_grad, k, NN)
            dkey = dot(score_grad_t, q, NN)
            dval = dot(score_keys_t, grad, NN)
            if state_ref is not None:
                after = state_ref[level, h].astype(BF16)
                dkey = dkey + dot(v, after, NT)
                dval = dval + dot(k, after, NN)
            wide[pl.ds(h, CHUNK, stride=heads), :] = dq
            dk_ref[:, cols] = dkey.astype(BF16)
            dv_ref[:, cols] = dval.astype(BF16)
    if others:
        low_ref[...] = wide[...].astype(BF16)
        last = pltpu.make_async_copy(
            low_ref, dq_ref.at[pl.ds(chunk * CHUNK * heads, CHUNK * heads)], sem.at[len(others)]
        )
        last.start()
        for copy in copies + [last]:
            copy.wait()
    else:
        dq_ref[...] = wide[...].astype(BF16)


def within(chunk, q, k, v, qt, vt, d, also, at, scale, before, own, other, token, state, others, heads, dk):
    tokens, width = q.shape
    args = [q, k, v, qt, vt, d, also, scale, before, own, other, token]
    in_specs = [WHOLE] * 11 + [ANYWHERE]
    level = None
    if state is not None:
        level = state[1]
        args.append(state[0])
        in_specs.append(WHOLE)
    args += list(others.values())
    in_specs += [WHOLE] * len(others)
    scratch = [pltpu.VMEM((CHUNK * heads, dk), F32)]
    rows = tokens if others else CHUNK
    if others:
        scratch += [pltpu.VMEM((CHUNK * heads, dk), BF16), pltpu.SemaphoreType.DMA((len(others) + 1,))]
    return call(
        functools.partial(within_kernel, heads, dk, chunk, at, level, list(others)),
        "within",
        args,
        in_specs,
        [shape((rows * heads, dk), BF16)] + [shape((CHUNK, width), BF16)] * 2 + [shape(TOKEN, F32)],
        [ANYWHERE if others else WHOLE] + [WHOLE] * 3,
        scratch,
    )


def finish_kernel(heads, dk, n, last, k_ref, v_ref, suffix_ref, _, *refs):
    half = heads // 2
    dkp, dvp, refs = refs[:n], refs[n : 2 * n], refs[2 * n :]
    if last:
        dk_ref, dv_ref, wide_k, wide_v, after, turned, low_k, low_v, sem = refs[2:]
    else:
        wide_k, wide_v, token_ref, after, turned = refs
        token_ref[...] = jnp.zeros_like(token_ref)
    base = half * (lax.axis_index("ctx") % 2 ^ last)
    after[...] = jnp.zeros_like(after)
    turned[...] = jnp.zeros_like(turned)
    for h in range(half):
        cols = slice(h % PAIR * dk, (h % PAIR + 1) * dk)
        after[h // PAIR, cols, cols] = suffix_ref[h]
        turned[h // PAIR, cols, cols] = suffix_ref[h].T
    copies = []
    for c in range(n):
        rows = slice(c * CHUNK, (c + 1) * CHUNK)
        for p in range(half // PAIR):
            cols = part_of(base // PAIR + p, PAIR * dk)
            full_k = dkp[c][:, cols].astype(F32) + dot(v_ref[rows, cols], turned[p], NN)
            full_v = dvp[c][:, cols].astype(F32) + dot(k_ref[rows, cols], after[p], NN)
            for i in range(PAIR):
                mine = pl.ds(c * CHUNK * heads + base + p * PAIR + i, CHUNK, stride=heads)
                wide_k[mine, :] = full_k[:, i * dk : (i + 1) * dk]
                wide_v[mine, :] = full_v[:, i * dk : (i + 1) * dk]
        if last:
            raw = slice(c * CHUNK * heads, (c + 1) * CHUNK * heads)
            for i, (wide, low, out) in enumerate(((wide_k, low_k, dk_ref), (wide_v, low_v, dv_ref))):
                low[c] = wide[raw, :].astype(BF16)
                copy = pltpu.make_async_copy(low.at[c], out.at[pl.ds(c * CHUNK * heads, CHUNK * heads)], sem.at[i, c])
                copy.start()
                copies.append(copy)
    for copy in copies:
        copy.wait()


def finish(k, v, dkp, dvp, suffix, token, held, heads, dk):
    tokens, width = k.shape
    n = tokens // CHUNK
    last = held is not None
    raw = (tokens * heads, dk)
    args = [k, v, suffix, token, *dkp, *dvp]
    in_specs = [WHOLE] * 3 + [ANYWHERE] + [WHOLE] * (2 * n)
    out_shape = [shape(raw, F32)] * 2
    out_specs = [WHOLE] * 2
    scratch = [pltpu.VMEM((heads // 2 // PAIR, PAIR * dk, PAIR * dk), BF16)] * 2
    aliases = {}
    if last:
        aliases = {len(args): 2, len(args) + 1: 3}
        args += held
        in_specs += [WHOLE] * 2
        out_shape = [shape(raw, BF16)] * 2 + out_shape
        out_specs = [ANYWHERE] * 2 + out_specs
        scratch += [pltpu.VMEM((n, CHUNK * heads, dk), BF16)] * 2 + [pltpu.SemaphoreType.DMA((2, n))]
    else:
        out_shape.append(shape(TOKEN, F32))
        out_specs.append(WHOLE)
    kernel = functools.partial(finish_kernel, heads, dk, n, int(last))
    return call(kernel, "finish", args, in_specs, out_shape, out_specs, scratch, aliases)


def swap(array, axis, size, bit):
    return lax.ppermute(array, axis, [(i, i ^ bit) for i in range(size)])


def shifted(array, size, step):
    return lax.ppermute(array, "ctx", [(i, i + step) for i in range(size) if 0 <= i + step < size])


class Order:
    def __init__(self):
        self.token = None

    def tie(self, array):
        array, self.token = lax.optimization_barrier((array, self.token))
        return array


def total_kernel(*refs):
    *terms, out = refs
    total = terms[0][...].astype(F32)
    for term in terms[1:]:
        total = total + term[...].astype(F32)
    out[...] = total.astype(BF16)


def ends_kernel(later_is_odd, own, came, *refs):
    *got, give, mine = refs
    exclusive = got[0][...].astype(F32)
    for term in got[1:]:
        exclusive = exclusive + term[...].astype(F32)
    later = (lax.axis_index("ctx") % 2 == 1) == later_is_odd
    give[...] = jnp.where(later, exclusive, exclusive + own[...].astype(F32)).astype(BF16)
    mine[...] = jnp.where(later, exclusive + came[...].astype(F32), exclusive).astype(BF16)


def scan_states(keep, send, size, direction, order):
    terms = [[own, swap(away, "ctx", size, 1)] for own, away in zip(keep, send)]
    yield None
    like = shape(keep[0].shape, BF16)
    step = 2
    while step < size:
        for part in terms:
            total = call(total_kernel, "total", part, [WHOLE] * len(part), like, WHOLE)
            part.append(shifted(order.tie(total), size, direction * step))
        yield None
        step *= 2
    kernel = functools.partial(ends_kernel, direction == 1)
    mine, other = [], []
    for part in terms:
        give, own = call(kernel, "ends", part, [WHOLE] * len(part), [like] * 2, [WHOLE] * 2)
        mine.append(own)
        other.append(swap(order.tie(give), "ctx", size, 1))
    yield mine, other


def body(n_ctx, n_head, queries, keys, values, d_layer, out_weight):
    tokens, heads, dk = queries.shape
    n = tokens // CHUNK
    near = n_head // 2
    far = 1
    groups = [(1, n - 1), (0, 1)]
    order = Order()
    *pieces, order.token = cut(d_layer, groups)
    across = {c: swap(piece, "head", n_head, near) for (c, _), piece in zip(groups, pieces)}
    beside = swap(d_layer, "head", n_head, far)

    flat = (tokens * heads, dk)
    q, k, v, qt, vt, before, scale, keep, send, order.token = prepare(
        queries.reshape(flat), keys.reshape(flat), values.reshape(flat), order.token, tokens, heads, dk
    )
    forward = scan_states([keep], [send], n_ctx, 1, order)
    next(forward)
    starts = [c * CHUNK for c, _ in groups]
    part, order.token = early(pieces, starts, beside, out_weight, order.token)

    prefix = None
    while prefix is None:
        prefix = next(forward)
    prefix = [prefix[0][0], prefix[1][0]]
    d, after, dq, dkp, dvp = {}, {}, {}, {}, {}

    def inner(c):
        others = dict(dq) if c == 0 else {}
        dq[c], dkp[c], dvp[c], order.token = within(
            c, q, k, v, qt, vt, *d[c], scale, before, *prefix, order.token, after[c], others, heads, dk
        )

    state = None
    for c, m in groups[:-1]:
        after[c + m - 1] = None if state is None else (state, 0)
        piece = order.tie(across[c])
        both = swap(piece, "head", n_head, far)
        low, order.token, state = late(
            c * CHUNK, None, near, piece, both, out_weight, part, scale, qt, order.token, state, heads, dk
        )
        for i in range(m):
            d[c + i] = (low, low, i)
            if i < m - 1:
                after[c + i] = (state, i + 1)
        for i in reversed(range(m)):
            if c + i > 2:
                inner(c + i)
    after[0] = (state, 0)
    piece = order.tie(across[0])
    both = swap(piece, "head", n_head, far)
    part, order.token = middle(0, near, piece, out_weight, part, order.token)
    low_send, order.token, send, turned = late(
        0, 1, near, None, both, out_weight, part, scale, qt, order.token, state, heads, dk
    )
    low_keep, order.token, keep = late(
        0, 0, near, None, turned, out_weight, part, scale, qt, order.token, state, heads, dk
    )
    d[0] = (low_keep, low_send, None)
    backward = scan_states([keep], [send], n_ctx, -1, order)
    next(backward)
    plan = [[c for c in range(n) if c > 1 and c not in dq], [1, 0]]
    suffix = None
    while suffix is None:
        suffix = next(backward)
        for c in plan.pop(0) if plan else []:
            inner(c)
    parts = [[dkp[c] for c in range(n)], [dvp[c] for c in range(n)]]
    *held, order.token = finish(k, v, *parts, suffix[0][0], order.token, None, heads, dk)
    d_keys, d_values, *_ = finish(k, v, *parts, suffix[1][0], order.token, held, heads, dk)
    return tuple(a.reshape(tokens, heads, dk) for a in (dq[0], d_keys, d_values))


def solution(mesh):
    in_specs = (
        P("ctx", "head", None),
        P("ctx", "head", None),
        P("ctx", "head", None),
        P("ctx", "head"),
        P("head", None),
    )
    out_specs = (P("ctx", "head", None), P("ctx", "head", None), P("ctx", "head", None))

    def program(queries, keys, values, d_layer, out_weight):
        return body(mesh.shape["ctx"], mesh.shape["head"], queries, keys, values, d_layer, out_weight)

    return jax.shard_map(program, mesh=mesh, in_specs=in_specs, out_specs=out_specs, check_vma=False)
```

```python
import functools

import jax
import jax.numpy as jnp
from jax import lax
from jax.experimental import pallas as pl
from jax.experimental.pallas import tpu as pltpu
from jax.sharding import PartitionSpec as P

CHUNK = 256
PAIR = 2
F32 = jnp.float32
BF16 = jnp.bfloat16
TOKEN = (8, 128)
NT = (((1,), (1,)), ((), ()))
NN = (((1,), (0,)), ((), ()))
FREE = pl.CostEstimate(flops=0, bytes_accessed=0, transcendentals=0)
VMEM_LIMIT = 14 * 1024 * 1024
WHOLE = pl.BlockSpec(memory_space=pltpu.VMEM)
ANYWHERE = pl.BlockSpec(memory_space=pl.ANY)


def dot(a, b, dims):
    return lax.dot_general(a, b, dims, preferred_element_type=F32)


def shape(dims, dtype):
    return jax.ShapeDtypeStruct(dims, dtype)


def outside(*arrays):
    return [pltpu.with_memory_space_constraint(a, pltpu.HBM) for a in arrays]


def part_of(i, size):
    return slice(i * size, (i + 1) * size) if isinstance(i, int) else pl.ds(pl.multiple_of(i * size, size), size)


def call(kernel, name, args, in_specs, out_shape, out_specs, scratch=(), aliases=None):
    return pl.pallas_call(
        kernel,
        in_specs=in_specs,
        out_specs=out_specs,
        out_shape=out_shape,
        scratch_shapes=scratch,
        input_output_aliases=aliases or {},
        compiler_params=pltpu.CompilerParams(vmem_limit_bytes=VMEM_LIMIT),
        cost_estimate=FREE,
        name=name,
    )(*args)


def cut_kernel(starts, source, *refs):
    pieces, token_ref, sem = refs[: len(starts)], refs[-2], refs[-1]
    token_ref[...] = jnp.zeros_like(token_ref)
    copies = [
        pltpu.make_async_copy(source.at[pl.ds(start, piece.shape[0])], piece, sem.at[i])
        for i, (start, piece) in enumerate(zip(starts, pieces))
    ]
    for copy in copies:
        copy.start()
    for copy in copies:
        copy.wait()


def cut(d_layer, groups):
    features = d_layer.shape[1]
    return call(
        functools.partial(cut_kernel, [c * CHUNK for c, _ in groups]),
        "cut",
        outside(d_layer),
        [ANYWHERE],
        [shape((m * CHUNK, features), d_layer.dtype) for _, m in groups] + [shape(TOKEN, F32)],
        [WHOLE] * (len(groups) + 1),
        [pltpu.SemaphoreType.DMA((len(groups),))],
    )


def prepare_kernel(
    heads, dk, q_ref, k_ref, v_ref, _, qf_ref, kf_ref, vf_ref, qt_ref, vt_ref, before_ref, scale_ref, keep_ref, send_ref, token_ref,
    raw, wides, acc, sem
):
    n = qf_ref.shape[0] // CHUNK

    def load(i, c):
        source = (q_ref, k_ref, v_ref)[i].at[part_of(c, CHUNK * heads)]
        return pltpu.make_async_copy(source, raw.at[i, c], sem.at[i, c])

    for c in range(n):
        for i in range(3):
            load(i, c).start()
    token_ref[...] = jnp.zeros_like(token_ref)
    acc[...] = jnp.zeros_like(acc)
    tokens = scale_ref.shape[0]
    position = lax.axis_index("ctx") * tokens + lax.broadcasted_iota(jnp.int32, scale_ref.shape, 0)
    scale_ref[...] = lax.rsqrt((dk * (position + 1)).astype(F32))

    def one_chunk(c, _):
        rows = part_of(c, CHUNK)
        before_ref[c] = acc[...]
        for i in range(3):
            load(i, c).wait()
            wides[i] = raw[i, c].astype(F32)
        for h in range(heads):
            cols = slice(h * dk, (h + 1) * dk)
            mine = pl.ds(h, CHUNK, stride=heads)
            q, k, v = (wides[i, mine, :].astype(BF16) for i in range(3))
            qf_ref[rows, cols] = q
            kf_ref[rows, cols] = k
            vf_ref[rows, cols] = v
            qt_ref[cols, rows] = q.T
            vt = v.T
            vt_ref[cols, rows] = vt
            acc[h] += dot(vt, k, NN)
        return 0

    lax.fori_loop(0, n, one_chunk, 0)
    low, high = acc[: heads // 2].astype(BF16), acc[heads // 2 :].astype(BF16)
    first = lax.axis_index("ctx") % 2 == 0
    keep_ref[...] = jnp.where(first, low, high)
    send_ref[...] = jnp.where(first, high, low)


def prepare(q, k, v, token, tokens, heads, dk):
    n = tokens // CHUNK
    width = heads * dk
    return call(
        functools.partial(prepare_kernel, heads, dk),
        "prepare",
        [*outside(q, k, v), token],
        [ANYWHERE] * 4,
        [shape((tokens, width), BF16)] * 3
        + [shape((width, tokens), BF16)] * 2
        + [shape((n, heads, dk, dk), F32), shape((tokens, dk), F32)]
        + [shape((heads // 2, dk, dk), BF16)] * 2
        + [shape(TOKEN, F32)],
        [WHOLE] * 10,
        [
            pltpu.VMEM((3, n, CHUNK * heads, dk), BF16),
            pltpu.VMEM((3, CHUNK * heads, dk), F32),
            pltpu.VMEM((heads, dk, dk), F32),
            pltpu.SemaphoreType.DMA((3, n)),
        ],
    )


def early_kernel(starts, *refs):
    pieces, (b_ref, w_ref, _, out_ref, token_ref) = refs[: len(starts)], refs[len(starts) :]
    token_ref[...] = jnp.zeros_like(token_ref)
    features = b_ref.shape[1]
    place = lax.axis_index("head")
    first, second = part_of(place, features), part_of(place ^ 1, features)

    def one_tile(j, _):
        tile = part_of(j, PAIR * 128)
        wa, wb = w_ref[tile, first].T, w_ref[tile, second].T
        for start, piece in zip(starts, pieces):
            rows = slice(start, start + piece.shape[0])
            out_ref[rows, tile] = dot(piece[...], wa, NN) + dot(b_ref[rows, :], wb, NN)
        return 0

    lax.fori_loop(0, out_ref.shape[1] // (PAIR * 128), one_tile, 0)


def early(pieces, starts, b, weight, token):
    tokens = b.shape[0]
    width = weight.shape[0]
    return call(
        functools.partial(early_kernel, starts),
        "early",
        [*pieces, b, weight, token],
        [WHOLE] * (len(pieces) + 2) + [ANYWHERE],
        [shape((tokens, width), F32), shape(TOKEN, F32)],
        [WHOLE] * 2,
    )


def late_kernel(half, first, start, near, dk, b_ref, w_ref, part_ref, scale_ref, qt_ref, _, *refs):
    a_ref, refs = (refs[0], refs[1:]) if half is None else (None, refs)
    state_ref, refs = (None, refs) if first else (refs[0], refs[1:])
    d_ref, token_ref = refs[:2]
    tile = PAIR * dk
    steps = d_ref.shape[1] // tile
    out_ref, refs = refs[2], refs[3:]
    token_ref[...] = jnp.zeros_like(token_ref)
    if half is None:
        at, bt = refs
        at[...] = a_ref[...].T
        bt[...] = b_ref[...].T
    elif half == 1:
        (bt,) = refs
        bt[...] = b_ref[...].T
    else:
        bt = b_ref
    features, count = bt.shape
    place = lax.axis_index("head")
    one, two = part_of(place ^ near, features), part_of(place ^ near ^ 1, features)
    here = slice(start, start + count)
    base = 0 if half is None else steps * (lax.axis_index("ctx") % 2 ^ half)

    def one_tile(local, _):
        j = base + local
        wide = part_of(j, tile)
        turned = dot(w_ref[wide, two], bt[...], NN)
        if half is None:
            turned = turned + dot(w_ref[wide, one], at[...], NN)
        low = (part_ref[here if half is None else slice(0, count), wide] + turned.T).astype(BF16)
        d_ref[:, part_of(local, tile)] = low
        states = [None if first else state_ref[0, j * PAIR + i] for i in range(PAIR)]
        for c in reversed(range(count // CHUNK)):
            rows = slice(c * CHUNK, (c + 1) * CHUNK)
            there = slice(start + c * CHUNK, start + (c + 1) * CHUNK)
            for i in range(PAIR):
                grad = (low[rows, i * dk : (i + 1) * dk].astype(F32) * scale_ref[there, :]).astype(BF16)
                state = dot(qt_ref[part_of(j * PAIR + i, dk), there], grad, NN)
                states[i] = state if states[i] is None else states[i] + state
                if half is None:
                    out_ref[c, j * PAIR + i] = states[i]
        if half is not None:
            for i in range(PAIR):
                out_ref[local * PAIR + i] = states[i].astype(BF16)
        return 0

    if half is None:
        lax.fori_loop(0, steps, one_tile, 0)
    else:
        for local in range(steps):
            one_tile(local, 0)


def middle_kernel(start, near, a_ref, w_ref, part_ref, _, out_ref, token_ref, at):
    token_ref[...] = jnp.zeros_like(token_ref)
    at[...] = a_ref[...].T
    features, count = at.shape
    one = part_of(lax.axis_index("head") ^ near, features)
    tile = PAIR * 128
    for j in range(out_ref.shape[1] // tile):
        wide = slice(j * tile, (j + 1) * tile)
        out_ref[:, wide] = part_ref[start : start + count, wide] + dot(w_ref[wide, one], at[...], NN).T


def middle(start, near, a, weight, part, token):
    return call(
        functools.partial(middle_kernel, start, near),
        "middle",
        [a, weight, part, token],
        [WHOLE] * 3 + [ANYWHERE],
        [shape((a.shape[0], part.shape[1]), F32), shape(TOKEN, F32)],
        [WHOLE] * 2,
        [pltpu.VMEM(a.shape[::-1], BF16)],
    )


def late(start, half, near, a, b, weight, part, scale, qt, token, state, heads, dk):
    features, rows = b.shape if half == 0 else b.shape[::-1]
    width = weight.shape[0]
    args = [b, weight, part, scale, qt, token]
    in_specs = [WHOLE] * 5 + [ANYWHERE]
    if half is None:
        args.append(a)
        in_specs.append(WHOLE)
    if state is not None:
        args.append(state)
        in_specs.append(WHOLE)
    if half is None:
        out_shape = [shape((rows, width), BF16), shape(TOKEN, F32), shape((rows // CHUNK, heads, dk, dk), F32)]
    else:
        out_shape = [shape((rows, width // 2), BF16), shape(TOKEN, F32)]
        out_shape.append(shape((heads // 2, dk, dk), BF16))
    scratch = [pltpu.VMEM((features, rows), BF16)] * 2 if half is None else []
    if half == 1:
        out_shape.append(shape((features, rows), BF16))
    return call(
        functools.partial(late_kernel, half, state is None, start, near, dk),
        "late",
        args,
        in_specs,
        out_shape,
        [WHOLE] * len(out_shape),
        scratch,
    )


def within_kernel(
    heads, dk, chunk, at, level, others,
    q_ref, k_ref, v_ref, qt_ref, vt_ref, d_ref, also_ref, scale_ref, before_ref, own_ref, other_ref, _, *refs
):
    state_ref, refs = (None, refs) if level is None else (refs[0], refs[1:])
    earlier_dq, refs = refs[: len(others)], refs[len(others) :]
    dq_ref, dk_ref, dv_ref, token_ref, wide = refs[:5]
    token_ref[...] = jnp.zeros_like(token_ref)
    if others:
        low_ref, sem = refs[5:]
        copies = [
            pltpu.make_async_copy(source, dq_ref.at[pl.ds(c * CHUNK * heads, CHUNK * heads)], sem.at[i])
            for i, (c, source) in enumerate(zip(others, earlier_dq))
        ]
        for copy in copies:
            copy.start()
    rows = slice(chunk * CHUNK, (chunk + 1) * CHUNK)
    there = None if at is None else slice(at * CHUNK, (at + 1) * CHUNK)
    t = lax.broadcasted_iota(jnp.int32, (CHUNK, CHUNK), 0)
    s = lax.broadcasted_iota(jnp.int32, (CHUNK, CHUNK), 1)
    lower = s <= t
    upper = t <= s
    scale = scale_ref[rows, :]
    half = heads // 2

    for g, prefix_ref in enumerate((own_ref, other_ref)):
        for i in range(half):
            h = (lax.axis_index("ctx") % 2 ^ g) * half + i
            cols = part_of(h, dk)
            q, k, v = q_ref[rows, cols], k_ref[rows, cols], v_ref[rows, cols]
            if at is None:
                d = (d_ref, also_ref)[g][:, i * dk : (i + 1) * dk]
            else:
                d = d_ref[there, cols]
            grad = (d.astype(F32) * scale).astype(BF16)
            score_grad = jnp.where(lower, dot(grad, vt_ref[cols, rows], NN), 0.0).astype(BF16)
            score_grad_t = jnp.where(upper, dot(v, grad, NT), 0.0).astype(BF16)
            score_keys_t = jnp.where(upper, dot(k, qt_ref[cols, rows], NN), 0.0).astype(BF16)
            earlier = prefix_ref[i].astype(F32) + before_ref[chunk, h]
            dq = scale * dot(d, earlier.astype(BF16), NN) + dot(score_grad, k, NN)
            dkey = dot(score_grad_t, q, NN)
            dval = dot(score_keys_t, grad, NN)
            if state_ref is not None:
                after = state_ref[level, h].astype(BF16)
                dkey = dkey + dot(v, after, NT)
                dval = dval + dot(k, after, NN)
            wide[pl.ds(h, CHUNK, stride=heads), :] = dq
            dk_ref[:, cols] = dkey.astype(BF16)
            dv_ref[:, cols] = dval.astype(BF16)
    if others:
        low_ref[...] = wide[...].astype(BF16)
        last = pltpu.make_async_copy(
            low_ref, dq_ref.at[pl.ds(chunk * CHUNK * heads, CHUNK * heads)], sem.at[len(others)]
        )
        last.start()
        for copy in copies + [last]:
            copy.wait()
    else:
        dq_ref[...] = wide[...].astype(BF16)


def within(chunk, q, k, v, qt, vt, d, also, at, scale, before, own, other, token, state, others, heads, dk):
    tokens, width = q.shape
    args = [q, k, v, qt, vt, d, also, scale, before, own, other, token]
    in_specs = [WHOLE] * 11 + [ANYWHERE]
    level = None
    if state is not None:
        level = state[1]
        args.append(state[0])
        in_specs.append(WHOLE)
    args += list(others.values())
    in_specs += [WHOLE] * len(others)
    scratch = [pltpu.VMEM((CHUNK * heads, dk), F32)]
    rows = tokens if others else CHUNK
    if others:
        scratch += [pltpu.VMEM((CHUNK * heads, dk), BF16), pltpu.SemaphoreType.DMA((len(others) + 1,))]
    return call(
        functools.partial(within_kernel, heads, dk, chunk, at, level, list(others)),
        "within",
        args,
        in_specs,
        [shape((rows * heads, dk), BF16)] + [shape((CHUNK, width), BF16)] * 2 + [shape(TOKEN, F32)],
        [ANYWHERE if others else WHOLE] + [WHOLE] * 3,
        scratch,
    )


def finish_kernel(heads, dk, n, last, k_ref, v_ref, suffix_ref, _, *refs):
    half = heads // 2
    dkp, dvp, refs = refs[:n], refs[n : 2 * n], refs[2 * n :]
    if last:
        dk_ref, dv_ref, wide_k, wide_v, after, turned, low_k, low_v, sem = refs[2:]
    else:
        wide_k, wide_v, token_ref, after, turned = refs
        token_ref[...] = jnp.zeros_like(token_ref)
    base = half * (lax.axis_index("ctx") % 2 ^ last)
    after[...] = jnp.zeros_like(after)
    turned[...] = jnp.zeros_like(turned)
    for h in range(half):
        cols = slice(h % PAIR * dk, (h % PAIR + 1) * dk)
        after[h // PAIR, cols, cols] = suffix_ref[h]
        turned[h // PAIR, cols, cols] = suffix_ref[h].T
    copies = []
    for c in range(n):
        rows = slice(c * CHUNK, (c + 1) * CHUNK)
        for p in range(half // PAIR):
            cols = part_of(base // PAIR + p, PAIR * dk)
            full_k = dkp[c][:, cols].astype(F32) + dot(v_ref[rows, cols], turned[p], NN)
            full_v = dvp[c][:, cols].astype(F32) + dot(k_ref[rows, cols], after[p], NN)
            for i in range(PAIR):
                mine = pl.ds(c * CHUNK * heads + base + p * PAIR + i, CHUNK, stride=heads)
                wide_k[mine, :] = full_k[:, i * dk : (i + 1) * dk]
                wide_v[mine, :] = full_v[:, i * dk : (i + 1) * dk]
        if last:
            raw = slice(c * CHUNK * heads, (c + 1) * CHUNK * heads)
            for i, (wide, low, out) in enumerate(((wide_k, low_k, dk_ref), (wide_v, low_v, dv_ref))):
                low[c] = wide[raw, :].astype(BF16)
                copy = pltpu.make_async_copy(low.at[c], out.at[pl.ds(c * CHUNK * heads, CHUNK * heads)], sem.at[i, c])
                copy.start()
                copies.append(copy)
    for copy in copies:
        copy.wait()


def finish(k, v, dkp, dvp, suffix, token, held, heads, dk):
    tokens, width = k.shape
    n = tokens // CHUNK
    last = held is not None
    raw = (tokens * heads, dk)
    args = [k, v, suffix, token, *dkp, *dvp]
    in_specs = [WHOLE] * 3 + [ANYWHERE] + [WHOLE] * (2 * n)
    out_shape = [shape(raw, F32)] * 2
    out_specs = [WHOLE] * 2
    scratch = [pltpu.VMEM((heads // 2 // PAIR, PAIR * dk, PAIR * dk), BF16)] * 2
    aliases = {}
    if last:
        aliases = {len(args): 2, len(args) + 1: 3}
        args += held
        in_specs += [WHOLE] * 2
        out_shape = [shape(raw, BF16)] * 2 + out_shape
        out_specs = [ANYWHERE] * 2 + out_specs
        scratch += [pltpu.VMEM((n, CHUNK * heads, dk), BF16)] * 2 + [pltpu.SemaphoreType.DMA((2, n))]
    else:
        out_shape.append(shape(TOKEN, F32))
        out_specs.append(WHOLE)
    kernel = functools.partial(finish_kernel, heads, dk, n, int(last))
    return call(kernel, "finish", args, in_specs, out_shape, out_specs, scratch, aliases)


def swap(array, axis, size, bit):
    return lax.ppermute(array, axis, [(i, i ^ bit) for i in range(size)])


def shifted(array, size, step, pair=None):
    moves = [(i, i + step) for i in range(size) if 0 <= i + step < size]
    return lax.ppermute(array, "ctx", [(i, j) for i, j in moves if pair is None or j // 2 == pair])


class Order:
    def __init__(self):
        self.token = None

    def tie(self, array):
        array, self.token = lax.optimization_barrier((array, self.token))
        return array


def total_kernel(*refs):
    *terms, out = refs
    total = terms[0][...].astype(F32)
    for term in terms[1:]:
        total = total + term[...].astype(F32)
    out[...] = total.astype(BF16)


def ends_kernel(later_is_odd, own, came, *refs):
    *got, give, mine = refs
    exclusive = got[0][...].astype(F32)
    for term in got[1:]:
        exclusive = exclusive + term[...].astype(F32)
    later = (lax.axis_index("ctx") % 2 == 1) == later_is_odd
    give[...] = jnp.where(later, exclusive, exclusive + own[...].astype(F32)).astype(BF16)
    mine[...] = jnp.where(later, exclusive + came[...].astype(F32), exclusive).astype(BF16)


def scan_states(keep, send, size, direction, order):
    terms = [[own, swap(away, "ctx", size, 1)] for own, away in zip(keep, send)]
    yield None
    like = shape(keep[0].shape, BF16)
    step = 2
    if size == 8:
        third, fourth = (2, 3) if direction == 1 else (1, 0)
        for part in terms:
            total = order.tie(call(total_kernel, "total", part, [WHOLE] * 2, like, WHOLE))
            part.append(shifted(total, size, direction * 2))
            part.append(shifted(total, size, direction * 4, third))
        yield None
        for part in terms:
            total = call(total_kernel, "total", part[2:], [WHOLE] * 2, like, WHOLE)
            part.append(shifted(order.tie(total), size, direction * 2, fourth))
        yield None
        step = size
    while step < size:
        for part in terms:
            total = call(total_kernel, "total", part, [WHOLE] * len(part), like, WHOLE)
            part.append(shifted(order.tie(total), size, direction * step))
        yield None
        step *= 2
    kernel = functools.partial(ends_kernel, direction == 1)
    mine, other = [], []
    for part in terms:
        give, own = call(kernel, "ends", part, [WHOLE] * len(part), [like] * 2, [WHOLE] * 2)
        mine.append(own)
        other.append(swap(order.tie(give), "ctx", size, 1))
    yield mine, other


def body(n_ctx, n_head, queries, keys, values, d_layer, out_weight):
    tokens, heads, dk = queries.shape
    n = tokens // CHUNK
    near = n_head // 2
    far = 1
    groups = [(1, n - 1), (0, 1)]
    order = Order()
    *pieces, order.token = cut(d_layer, groups)
    across = {c: swap(piece, "head", n_head, near) for (c, _), piece in zip(groups, pieces)}
    beside = swap(order.tie(d_layer), "head", n_head, far)

    flat = (tokens * heads, dk)
    q, k, v, qt, vt, before, scale, keep, send, order.token = prepare(
        queries.reshape(flat), keys.reshape(flat), values.reshape(flat), order.token, tokens, heads, dk
    )
    forward = scan_states([keep], [send], n_ctx, 1, order)
    next(forward)
    starts = [c * CHUNK for c, _ in groups]
    part, order.token = early(pieces, starts, beside, out_weight, order.token)

    prefix = None
    while prefix is None:
        prefix = next(forward)
    prefix = [prefix[0][0], prefix[1][0]]
    d, after, dq, dkp, dvp = {}, {}, {}, {}, {}

    def inner(c):
        others = dict(dq) if c == 0 else {}
        dq[c], dkp[c], dvp[c], order.token = within(
            c, q, k, v, qt, vt, *d[c], scale, before, *prefix, order.token, after[c], others, heads, dk
        )

    state = None
    for c, m in groups[:-1]:
        after[c + m - 1] = None if state is None else (state, 0)
        piece = order.tie(across[c])
        both = swap(piece, "head", n_head, far)
        low, order.token, state = late(
            c * CHUNK, None, near, piece, both, out_weight, part, scale, qt, order.token, state, heads, dk
        )
        for i in range(m):
            d[c + i] = (low, low, i)
            if i < m - 1:
                after[c + i] = (state, i + 1)
        for i in reversed(range(m)):
            if c + i > 2:
                inner(c + i)
    after[0] = (state, 0)
    piece = order.tie(across[0])
    both = swap(piece, "head", n_head, far)
    part, order.token = middle(0, near, piece, out_weight, part, order.token)
    low_send, order.token, send, turned = late(
        0, 1, near, None, both, out_weight, part, scale, qt, order.token, state, heads, dk
    )
    low_keep, order.token, keep = late(
        0, 0, near, None, turned, out_weight, part, scale, qt, order.token, state, heads, dk
    )
    d[0] = (low_keep, low_send, None)
    backward = scan_states([keep], [send], n_ctx, -1, order)
    next(backward)
    plan = [[c for c in reversed(range(1, n)) if c not in dq], [0]]
    suffix = None
    while suffix is None:
        suffix = next(backward)
        for c in plan.pop(0) if plan else []:
            inner(c)
    parts = [[dkp[c] for c in range(n)], [dvp[c] for c in range(n)]]
    *held, order.token = finish(k, v, *parts, suffix[0][0], order.token, None, heads, dk)
    d_keys, d_values, *_ = finish(k, v, *parts, suffix[1][0], order.token, held, heads, dk)
    return tuple(a.reshape(tokens, heads, dk) for a in (dq[0], d_keys, d_values))


def solution(mesh):
    in_specs = (
        P("ctx", "head", None),
        P("ctx", "head", None),
        P("ctx", "head", None),
        P("ctx", "head"),
        P("head", None),
    )
    out_specs = (P("ctx", "head", None), P("ctx", "head", None), P("ctx", "head", None))

    def program(queries, keys, values, d_layer, out_weight):
        return body(mesh.shape["ctx"], mesh.shape["head"], queries, keys, values, d_layer, out_weight)

    return jax.shard_map(program, mesh=mesh, in_specs=in_specs, out_specs=out_specs, check_vma=False)
```

```python
import functools

import jax
import jax.numpy as jnp
from jax import lax
from jax.experimental import pallas as pl
from jax.experimental.pallas import tpu as pltpu
from jax.sharding import PartitionSpec as P

CHUNK = 256
PAIR = 2
F32 = jnp.float32
BF16 = jnp.bfloat16
TOKEN = (8, 128)
NT = (((1,), (1,)), ((), ()))
NN = (((1,), (0,)), ((), ()))
FREE = pl.CostEstimate(flops=0, bytes_accessed=0, transcendentals=0)
VMEM_LIMIT = 14 * 1024 * 1024
WHOLE = pl.BlockSpec(memory_space=pltpu.VMEM)
ANYWHERE = pl.BlockSpec(memory_space=pl.ANY)


def dot(a, b, dims):
    return lax.dot_general(a, b, dims, preferred_element_type=F32)


def shape(dims, dtype):
    return jax.ShapeDtypeStruct(dims, dtype)


def outside(*arrays):
    return [pltpu.with_memory_space_constraint(a, pltpu.HBM) for a in arrays]


def part_of(i, size):
    return slice(i * size, (i + 1) * size) if isinstance(i, int) else pl.ds(pl.multiple_of(i * size, size), size)


def call(kernel, name, args, in_specs, out_shape, out_specs, scratch=(), aliases=None):
    return pl.pallas_call(
        kernel,
        in_specs=in_specs,
        out_specs=out_specs,
        out_shape=out_shape,
        scratch_shapes=scratch,
        input_output_aliases=aliases or {},
        compiler_params=pltpu.CompilerParams(vmem_limit_bytes=VMEM_LIMIT),
        cost_estimate=FREE,
        name=name,
    )(*args)


def cut_kernel(starts, source, *refs):
    pieces, token_ref, sem = refs[: len(starts)], refs[-2], refs[-1]
    token_ref[...] = jnp.zeros_like(token_ref)
    copies = []
    for start, piece in zip(starts, pieces):
        for row in range(0, piece.shape[0], CHUNK // 2):
            rows = pl.ds(start + row, CHUNK // 2)
            copies.append(
                pltpu.make_async_copy(source.at[rows], piece.at[pl.ds(row, CHUNK // 2)], sem.at[len(copies)])
            )
    for copy in copies:
        copy.start()
    for copy in copies:
        copy.wait()


def cut(d_layer, groups):
    features = d_layer.shape[1]
    return call(
        functools.partial(cut_kernel, [c * CHUNK for c, _ in groups]),
        "cut",
        outside(d_layer),
        [ANYWHERE],
        [shape((m * CHUNK, features), d_layer.dtype) for _, m in groups] + [shape(TOKEN, F32)],
        [WHOLE] * (len(groups) + 1),
        [pltpu.SemaphoreType.DMA((d_layer.shape[0] // (CHUNK // 2),))],
    )


def prepare_kernel(
    heads, dk, q_ref, k_ref, v_ref, _, qf_ref, kf_ref, vf_ref, qt_ref, vt_ref, before_ref, scale_ref, keep_ref, send_ref, token_ref,
    raw, wides, acc, sem
):
    n = qf_ref.shape[0] // CHUNK

    def load(i, c):
        source = (q_ref, k_ref, v_ref)[i].at[part_of(c, CHUNK * heads)]
        return pltpu.make_async_copy(source, raw.at[i, c], sem.at[i, c])

    for c in range(n):
        for i in range(3):
            load(i, c).start()
    token_ref[...] = jnp.zeros_like(token_ref)
    acc[...] = jnp.zeros_like(acc)
    tokens = scale_ref.shape[0]
    position = lax.axis_index("ctx") * tokens + lax.broadcasted_iota(jnp.int32, scale_ref.shape, 0)
    scale_ref[...] = lax.rsqrt((dk * (position + 1)).astype(F32))

    def one_chunk(c, _):
        rows = part_of(c, CHUNK)
        before_ref[c] = acc[...]
        for i in range(3):
            load(i, c).wait()
            wides[i] = raw[i, c].astype(F32)
        for h in range(heads):
            cols = slice(h * dk, (h + 1) * dk)
            mine = pl.ds(h, CHUNK, stride=heads)
            q, k, v = (wides[i, mine, :].astype(BF16) for i in range(3))
            qf_ref[rows, cols] = q
            kf_ref[rows, cols] = k
            vf_ref[rows, cols] = v
            qt_ref[cols, rows] = q.T
            vt = v.T
            vt_ref[cols, rows] = vt
            acc[h] += dot(vt, k, NN)
        return 0

    lax.fori_loop(0, n, one_chunk, 0)
    low, high = acc[: heads // 2].astype(BF16), acc[heads // 2 :].astype(BF16)
    first = lax.axis_index("ctx") % 2 == 0
    keep_ref[...] = jnp.where(first, low, high)
    send_ref[...] = jnp.where(first, high, low)


def prepare(q, k, v, token, tokens, heads, dk):
    n = tokens // CHUNK
    width = heads * dk
    return call(
        functools.partial(prepare_kernel, heads, dk),
        "prepare",
        [*outside(q, k, v), token],
        [ANYWHERE] * 4,
        [shape((tokens, width), BF16)] * 3
        + [shape((width, tokens), BF16)] * 2
        + [shape((n, heads, dk, dk), F32), shape((tokens, dk), F32)]
        + [shape((heads // 2, dk, dk), BF16)] * 2
        + [shape(TOKEN, F32)],
        [WHOLE] * 10,
        [
            pltpu.VMEM((3, n, CHUNK * heads, dk), BF16),
            pltpu.VMEM((3, CHUNK * heads, dk), F32),
            pltpu.VMEM((heads, dk, dk), F32),
            pltpu.SemaphoreType.DMA((3, n)),
        ],
    )


def early_kernel(starts, *refs):
    pieces, (b_ref, w_ref, _, out_ref, token_ref) = refs[: len(starts)], refs[len(starts) :]
    token_ref[...] = jnp.zeros_like(token_ref)
    features = b_ref.shape[1]
    place = lax.axis_index("head")
    first, second = part_of(place, features), part_of(place ^ 1, features)

    def one_tile(j, _):
        tile = part_of(j, PAIR * 128)
        wa, wb = w_ref[tile, first].T, w_ref[tile, second].T
        for start, piece in zip(starts, pieces):
            rows = slice(start, start + piece.shape[0])
            out_ref[rows, tile] = dot(piece[...], wa, NN) + dot(b_ref[rows, :], wb, NN)
        return 0

    lax.fori_loop(0, out_ref.shape[1] // (PAIR * 128), one_tile, 0)


def early(pieces, starts, b, weight, token):
    tokens = b.shape[0]
    width = weight.shape[0]
    return call(
        functools.partial(early_kernel, starts),
        "early",
        [*pieces, b, weight, token],
        [WHOLE] * (len(pieces) + 2) + [ANYWHERE],
        [shape((tokens, width), F32), shape(TOKEN, F32)],
        [WHOLE] * 2,
    )


def late_kernel(half, first, start, near, dk, b_ref, w_ref, part_ref, scale_ref, qt_ref, _, *refs):
    a_ref, refs = (refs[0], refs[1:]) if half is None else (None, refs)
    state_ref, refs = (None, refs) if first else (refs[0], refs[1:])
    d_ref, token_ref = refs[:2]
    tile = PAIR * dk
    steps = d_ref.shape[1] // tile
    out_ref, refs = refs[2], refs[3:]
    token_ref[...] = jnp.zeros_like(token_ref)
    if half is None:
        at, bt = refs
        at[...] = a_ref[...].T
        bt[...] = b_ref[...].T
    elif half == 1:
        (bt,) = refs
        bt[...] = b_ref[...].T
    else:
        bt = b_ref
    features, count = bt.shape
    place = lax.axis_index("head")
    one, two = part_of(place ^ near, features), part_of(place ^ near ^ 1, features)
    here = slice(start, start + count)
    base = 0 if half is None else steps * (lax.axis_index("ctx") % 2 ^ half)

    def one_tile(local, _):
        j = base + local
        wide = part_of(j, tile)
        turned = dot(w_ref[wide, two], bt[...], NN)
        if half is None:
            turned = turned + dot(w_ref[wide, one], at[...], NN)
        low = (part_ref[here if half is None else slice(0, count), wide] + turned.T).astype(BF16)
        d_ref[:, part_of(local, tile)] = low
        states = [None if first else state_ref[0, j * PAIR + i] for i in range(PAIR)]
        for c in reversed(range(count // CHUNK)):
            rows = slice(c * CHUNK, (c + 1) * CHUNK)
            there = slice(start + c * CHUNK, start + (c + 1) * CHUNK)
            for i in range(PAIR):
                grad = (low[rows, i * dk : (i + 1) * dk].astype(F32) * scale_ref[there, :]).astype(BF16)
                state = dot(qt_ref[part_of(j * PAIR + i, dk), there], grad, NN)
                states[i] = state if states[i] is None else states[i] + state
                if half is None:
                    out_ref[c, j * PAIR + i] = states[i]
        if half is not None:
            for i in range(PAIR):
                out_ref[local * PAIR + i] = states[i].astype(BF16)
        return 0

    if half is None:
        lax.fori_loop(0, steps, one_tile, 0)
    else:
        for local in range(steps):
            one_tile(local, 0)


def middle_kernel(start, near, a_ref, w_ref, part_ref, _, out_ref, token_ref, at):
    token_ref[...] = jnp.zeros_like(token_ref)
    at[...] = a_ref[...].T
    features, count = at.shape
    one = part_of(lax.axis_index("head") ^ near, features)
    tile = PAIR * 128
    for j in range(out_ref.shape[1] // tile):
        wide = slice(j * tile, (j + 1) * tile)
        out_ref[:, wide] = part_ref[start : start + count, wide] + dot(w_ref[wide, one], at[...], NN).T


def middle(start, near, a, weight, part, token):
    return call(
        functools.partial(middle_kernel, start, near),
        "middle",
        [a, weight, part, token],
        [WHOLE] * 3 + [ANYWHERE],
        [shape((a.shape[0], part.shape[1]), F32), shape(TOKEN, F32)],
        [WHOLE] * 2,
        [pltpu.VMEM(a.shape[::-1], BF16)],
    )


def late(start, half, near, a, b, weight, part, scale, qt, token, state, heads, dk):
    features, rows = b.shape if half == 0 else b.shape[::-1]
    width = weight.shape[0]
    args = [b, weight, part, scale, qt, token]
    in_specs = [WHOLE] * 5 + [ANYWHERE]
    if half is None:
        args.append(a)
        in_specs.append(WHOLE)
    if state is not None:
        args.append(state)
        in_specs.append(WHOLE)
    if half is None:
        out_shape = [shape((rows, width), BF16), shape(TOKEN, F32), shape((rows // CHUNK, heads, dk, dk), F32)]
    else:
        out_shape = [shape((rows, width // 2), BF16), shape(TOKEN, F32)]
        out_shape.append(shape((heads // 2, dk, dk), BF16))
    scratch = [pltpu.VMEM((features, rows), BF16)] * 2 if half is None else []
    if half == 1:
        out_shape.append(shape((features, rows), BF16))
    return call(
        functools.partial(late_kernel, half, state is None, start, near, dk),
        "late",
        args,
        in_specs,
        out_shape,
        [WHOLE] * len(out_shape),
        scratch,
    )


def within_kernel(
    heads, dk, chunk, at, level, others,
    q_ref, k_ref, v_ref, qt_ref, vt_ref, d_ref, also_ref, scale_ref, before_ref, own_ref, other_ref, _, *refs
):
    state_ref, refs = (None, refs) if level is None else (refs[0], refs[1:])
    earlier_dq, refs = refs[: len(others)], refs[len(others) :]
    dq_ref, dk_ref, dv_ref, token_ref, wide = refs[:5]
    token_ref[...] = jnp.zeros_like(token_ref)
    if others:
        low_ref, sem = refs[5:]
        copies = [
            pltpu.make_async_copy(source, dq_ref.at[pl.ds(c * CHUNK * heads, CHUNK * heads)], sem.at[i])
            for i, (c, source) in enumerate(zip(others, earlier_dq))
        ]
        for copy in copies:
            copy.start()
    rows = slice(chunk * CHUNK, (chunk + 1) * CHUNK)
    there = None if at is None else slice(at * CHUNK, (at + 1) * CHUNK)
    t = lax.broadcasted_iota(jnp.int32, (CHUNK, CHUNK), 0)
    s = lax.broadcasted_iota(jnp.int32, (CHUNK, CHUNK), 1)
    lower = s <= t
    upper = t <= s
    scale = scale_ref[rows, :]
    half = heads // 2

    for g, prefix_ref in enumerate((own_ref, other_ref)):
        for i in range(half):
            h = (lax.axis_index("ctx") % 2 ^ g) * half + i
            cols = part_of(h, dk)
            q, k, v = q_ref[rows, cols], k_ref[rows, cols], v_ref[rows, cols]
            if at is None:
                d = (d_ref, also_ref)[g][:, i * dk : (i + 1) * dk]
            else:
                d = d_ref[there, cols]
            grad = (d.astype(F32) * scale).astype(BF16)
            score_grad = jnp.where(lower, dot(grad, vt_ref[cols, rows], NN), 0.0).astype(BF16)
            score_grad_t = jnp.where(upper, dot(v, grad, NT), 0.0).astype(BF16)
            score_keys_t = jnp.where(upper, dot(k, qt_ref[cols, rows], NN), 0.0).astype(BF16)
            earlier = prefix_ref[i].astype(F32) + before_ref[chunk, h]
            dq = scale * dot(d, earlier.astype(BF16), NN) + dot(score_grad, k, NN)
            dkey = dot(score_grad_t, q, NN)
            dval = dot(score_keys_t, grad, NN)
            if state_ref is not None:
                after = state_ref[level, h].astype(BF16)
                dkey = dkey + dot(v, after, NT)
                dval = dval + dot(k, after, NN)
            wide[pl.ds(h, CHUNK, stride=heads), :] = dq
            dk_ref[:, cols] = dkey.astype(BF16)
            dv_ref[:, cols] = dval.astype(BF16)
    if others:
        low_ref[...] = wide[...].astype(BF16)
        last = pltpu.make_async_copy(
            low_ref, dq_ref.at[pl.ds(chunk * CHUNK * heads, CHUNK * heads)], sem.at[len(others)]
        )
        last.start()
        for copy in copies + [last]:
            copy.wait()
    else:
        dq_ref[...] = wide[...].astype(BF16)


def within(chunk, q, k, v, qt, vt, d, also, at, scale, before, own, other, token, state, others, heads, dk):
    tokens, width = q.shape
    args = [q, k, v, qt, vt, d, also, scale, before, own, other, token]
    in_specs = [WHOLE] * 11 + [ANYWHERE]
    level = None
    if state is not None:
        level = state[1]
        args.append(state[0])
        in_specs.append(WHOLE)
    args += list(others.values())
    in_specs += [WHOLE] * len(others)
    scratch = [pltpu.VMEM((CHUNK * heads, dk), F32)]
    rows = tokens if others else CHUNK
    if others:
        scratch += [pltpu.VMEM((CHUNK * heads, dk), BF16), pltpu.SemaphoreType.DMA((len(others) + 1,))]
    return call(
        functools.partial(within_kernel, heads, dk, chunk, at, level, list(others)),
        "within",
        args,
        in_specs,
        [shape((rows * heads, dk), BF16)] + [shape((CHUNK, width), BF16)] * 2 + [shape(TOKEN, F32)],
        [ANYWHERE if others else WHOLE] + [WHOLE] * 3,
        scratch,
    )


def finish_kernel(heads, dk, n, last, k_ref, v_ref, suffix_ref, _, *refs):
    half = heads // 2
    dkp, dvp, refs = refs[:n], refs[n : 2 * n], refs[2 * n :]
    if last:
        dk_ref, dv_ref, wide_k, wide_v, after, turned, low_k, low_v, sem = refs[2:]
    else:
        wide_k, wide_v, token_ref, after, turned = refs
        token_ref[...] = jnp.zeros_like(token_ref)
    base = half * (lax.axis_index("ctx") % 2 ^ last)
    after[...] = jnp.zeros_like(after)
    turned[...] = jnp.zeros_like(turned)
    for h in range(half):
        cols = slice(h % PAIR * dk, (h % PAIR + 1) * dk)
        after[h // PAIR, cols, cols] = suffix_ref[h]
        turned[h // PAIR, cols, cols] = suffix_ref[h].T
    copies = []
    step = CHUNK // 2
    for c in range(2 * n):
        rows = slice(c * step, (c + 1) * step)
        local = slice(c % 2 * step, (c % 2 + 1) * step)
        for p in range(half // PAIR):
            cols = part_of(base // PAIR + p, PAIR * dk)
            full_k = dkp[c // 2][local, cols].astype(F32) + dot(v_ref[rows, cols], turned[p], NN)
            full_v = dvp[c // 2][local, cols].astype(F32) + dot(k_ref[rows, cols], after[p], NN)
            for i in range(PAIR):
                mine = pl.ds(c * step * heads + base + p * PAIR + i, step, stride=heads)
                wide_k[mine, :] = full_k[:, i * dk : (i + 1) * dk]
                wide_v[mine, :] = full_v[:, i * dk : (i + 1) * dk]
        if last:
            raw = slice(c * step * heads, (c + 1) * step * heads)
            for i, (wide, low, out) in enumerate(((wide_k, low_k, dk_ref), (wide_v, low_v, dv_ref))):
                low[c] = wide[raw, :].astype(BF16)
                copy = pltpu.make_async_copy(low.at[c], out.at[pl.ds(c * step * heads, step * heads)], sem.at[i, c])
                copy.start()
                copies.append(copy)
    for copy in copies:
        copy.wait()


def finish(k, v, dkp, dvp, suffix, token, held, heads, dk):
    tokens, width = k.shape
    n = tokens // CHUNK
    last = held is not None
    raw = (tokens * heads, dk)
    args = [k, v, suffix, token, *dkp, *dvp]
    in_specs = [WHOLE] * 3 + [ANYWHERE] + [WHOLE] * (2 * n)
    out_shape = [shape(raw, F32)] * 2
    out_specs = [WHOLE] * 2
    scratch = [pltpu.VMEM((heads // 2 // PAIR, PAIR * dk, PAIR * dk), BF16)] * 2
    aliases = {}
    if last:
        aliases = {len(args): 2, len(args) + 1: 3}
        args += held
        in_specs += [WHOLE] * 2
        out_shape = [shape(raw, BF16)] * 2 + out_shape
        out_specs = [ANYWHERE] * 2 + out_specs
        scratch += [pltpu.VMEM((2 * n, CHUNK // 2 * heads, dk), BF16)] * 2 + [pltpu.SemaphoreType.DMA((2, 2 * n))]
    else:
        out_shape.append(shape(TOKEN, F32))
        out_specs.append(WHOLE)
    kernel = functools.partial(finish_kernel, heads, dk, n, int(last))
    return call(kernel, "finish", args, in_specs, out_shape, out_specs, scratch, aliases)


def swap(array, axis, size, bit):
    return lax.ppermute(array, axis, [(i, i ^ bit) for i in range(size)])


def shifted(array, size, step):
    return lax.ppermute(array, "ctx", [(i, i + step) for i in range(size) if 0 <= i + step < size])


class Order:
    def __init__(self):
        self.token = None

    def tie(self, array):
        array, self.token = lax.optimization_barrier((array, self.token))
        return array


def total_kernel(*refs):
    *terms, out = refs
    total = terms[0][...].astype(F32)
    for term in terms[1:]:
        total = total + term[...].astype(F32)
    out[...] = total.astype(BF16)


def ends_kernel(later_is_odd, own, came, *refs):
    *got, give, mine = refs
    exclusive = got[0][...].astype(F32)
    for term in got[1:]:
        exclusive = exclusive + term[...].astype(F32)
    later = (lax.axis_index("ctx") % 2 == 1) == later_is_odd
    give[...] = jnp.where(later, exclusive, exclusive + own[...].astype(F32)).astype(BF16)
    mine[...] = jnp.where(later, exclusive + came[...].astype(F32), exclusive).astype(BF16)


def scan_states(keep, send, size, direction, order):
    terms = [[own, swap(away, "ctx", size, 1)] for own, away in zip(keep, send)]
    yield None
    like = shape(keep[0].shape, BF16)
    step = 2
    while step < size:
        for part in terms:
            total = call(total_kernel, "total", part, [WHOLE] * len(part), like, WHOLE)
            part.append(shifted(order.tie(total), size, direction * step))
        yield None
        step *= 2
    kernel = functools.partial(ends_kernel, direction == 1)
    mine, other = [], []
    for part in terms:
        give, own = call(kernel, "ends", part, [WHOLE] * len(part), [like] * 2, [WHOLE] * 2)
        mine.append(own)
        other.append(swap(order.tie(give), "ctx", size, 1))
    yield mine, other


def body(n_ctx, n_head, queries, keys, values, d_layer, out_weight):
    tokens, heads, dk = queries.shape
    n = tokens // CHUNK
    near = n_head // 2
    far = 1
    groups = [(1, n - 1), (0, 1)]
    order = Order()
    beside = swap(d_layer, "head", n_head, far)
    *pieces, order.token = cut(d_layer, groups)
    across = {c: swap(piece, "head", n_head, near) for (c, _), piece in zip(groups, pieces)}

    flat = (tokens * heads, dk)
    q, k, v, qt, vt, before, scale, keep, send, order.token = prepare(
        queries.reshape(flat), keys.reshape(flat), values.reshape(flat), order.token, tokens, heads, dk
    )
    forward = scan_states([keep], [send], n_ctx, 1, order)
    next(forward)
    starts = [c * CHUNK for c, _ in groups]
    part, order.token = early(pieces, starts, beside, out_weight, order.token)

    prefix = None
    while prefix is None:
        prefix = next(forward)
    prefix = [prefix[0][0], prefix[1][0]]
    d, after, dq, dkp, dvp = {}, {}, {}, {}, {}

    def inner(c):
        others = dict(dq) if c == 0 else {}
        dq[c], dkp[c], dvp[c], order.token = within(
            c, q, k, v, qt, vt, *d[c], scale, before, *prefix, order.token, after[c], others, heads, dk
        )

    state = None
    for c, m in groups[:-1]:
        after[c + m - 1] = None if state is None else (state, 0)
        piece = order.tie(across[c])
        both = swap(piece, "head", n_head, far)
        low, order.token, state = late(
            c * CHUNK, None, near, piece, both, out_weight, part, scale, qt, order.token, state, heads, dk
        )
        for i in range(m):
            d[c + i] = (low, low, i)
            if i < m - 1:
                after[c + i] = (state, i + 1)
        for i in reversed(range(m)):
            if c + i > 2:
                inner(c + i)
    after[0] = (state, 0)
    piece = order.tie(across[0])
    both = swap(piece, "head", n_head, far)
    part, order.token = middle(0, near, piece, out_weight, part, order.token)
    low_send, order.token, send, turned = late(
        0, 1, near, None, both, out_weight, part, scale, qt, order.token, state, heads, dk
    )
    low_keep, order.token, keep = late(
        0, 0, near, None, turned, out_weight, part, scale, qt, order.token, state, heads, dk
    )
    d[0] = (low_keep, low_send, None)
    backward = scan_states([keep], [send], n_ctx, -1, order)
    next(backward)
    plan = [[c for c in range(n) if c > 1 and c not in dq], [1, 0]]
    suffix = None
    while suffix is None:
        suffix = next(backward)
        for c in plan.pop(0) if plan else []:
            inner(c)
    parts = [[dkp[c] for c in range(n)], [dvp[c] for c in range(n)]]
    *held, order.token = finish(k, v, *parts, suffix[0][0], order.token, None, heads, dk)
    d_keys, d_values, *_ = finish(k, v, *parts, suffix[1][0], order.token, held, heads, dk)
    return tuple(a.reshape(tokens, heads, dk) for a in (dq[0], d_keys, d_values))


def solution(mesh):
    in_specs = (
        P("ctx", "head", None),
        P("ctx", "head", None),
        P("ctx", "head", None),
        P("ctx", "head"),
        P("head", None),
    )
    out_specs = (P("ctx", "head", None), P("ctx", "head", None), P("ctx", "head", None))

    def program(queries, keys, values, d_layer, out_weight):
        return body(mesh.shape["ctx"], mesh.shape["head"], queries, keys, values, d_layer, out_weight)

    return jax.shard_map(program, mesh=mesh, in_specs=in_specs, out_specs=out_specs, check_vma=False)
```

```python
import functools

import jax
import jax.numpy as jnp
from jax import lax
from jax.experimental import pallas as pl
from jax.experimental.pallas import tpu as pltpu
from jax.sharding import PartitionSpec as P

CHUNK = 256
PAIR = 2
F32 = jnp.float32
BF16 = jnp.bfloat16
TOKEN = (8, 128)
NT = (((1,), (1,)), ((), ()))
NN = (((1,), (0,)), ((), ()))
FREE = pl.CostEstimate(flops=0, bytes_accessed=0, transcendentals=0)
VMEM_LIMIT = 14 * 1024 * 1024
WHOLE = pl.BlockSpec(memory_space=pltpu.VMEM)
ANYWHERE = pl.BlockSpec(memory_space=pl.ANY)


def dot(a, b, dims):
    return lax.dot_general(a, b, dims, preferred_element_type=F32)


def shape(dims, dtype):
    return jax.ShapeDtypeStruct(dims, dtype)


def outside(*arrays):
    return [pltpu.with_memory_space_constraint(a, pltpu.HBM) for a in arrays]


def part_of(i, size):
    return slice(i * size, (i + 1) * size) if isinstance(i, int) else pl.ds(pl.multiple_of(i * size, size), size)


def call(kernel, name, args, in_specs, out_shape, out_specs, scratch=(), aliases=None):
    return pl.pallas_call(
        kernel,
        in_specs=in_specs,
        out_specs=out_specs,
        out_shape=out_shape,
        scratch_shapes=scratch,
        input_output_aliases=aliases or {},
        compiler_params=pltpu.CompilerParams(vmem_limit_bytes=VMEM_LIMIT),
        cost_estimate=FREE,
        name=name,
    )(*args)


def cut_kernel(starts, source, *refs):
    pieces, token_ref, sem = refs[: len(starts)], refs[-2], refs[-1]
    token_ref[...] = jnp.zeros_like(token_ref)
    copies = []
    for start, piece in zip(starts, pieces):
        for row in range(0, piece.shape[0], CHUNK // 2):
            rows = pl.ds(start + row, CHUNK // 2)
            copies.append(
                pltpu.make_async_copy(source.at[rows], piece.at[pl.ds(row, CHUNK // 2)], sem.at[len(copies)])
            )
    for copy in copies:
        copy.start()
    for copy in copies:
        copy.wait()


def cut(d_layer, groups):
    features = d_layer.shape[1]
    return call(
        functools.partial(cut_kernel, [c * CHUNK for c, _ in groups]),
        "cut",
        outside(d_layer),
        [ANYWHERE],
        [shape((m * CHUNK, features), d_layer.dtype) for _, m in groups] + [shape(TOKEN, F32)],
        [WHOLE] * (len(groups) + 1),
        [pltpu.SemaphoreType.DMA((d_layer.shape[0] // (CHUNK // 2),))],
    )


def prepare_kernel(
    heads, dk, q_ref, k_ref, v_ref, _, qf_ref, kf_ref, vf_ref, qt_ref, vt_ref, before_ref, scale_ref, keep_ref, send_ref, token_ref,
    raw, wides, acc, sem
):
    n = qf_ref.shape[0] // CHUNK

    def load(i, c):
        source = (q_ref, k_ref, v_ref)[i].at[part_of(c, CHUNK * heads)]
        return pltpu.make_async_copy(source, raw.at[i, c], sem.at[i, c])

    for c in range(n):
        for i in range(3):
            load(i, c).start()
    token_ref[...] = jnp.zeros_like(token_ref)
    acc[...] = jnp.zeros_like(acc)
    tokens = scale_ref.shape[0]
    position = lax.axis_index("ctx") * tokens + lax.broadcasted_iota(jnp.int32, scale_ref.shape, 0)
    scale_ref[...] = lax.rsqrt((dk * (position + 1)).astype(F32))

    def one_chunk(c, _):
        rows = part_of(c, CHUNK)
        before_ref[c] = acc[...]
        for i in range(3):
            load(i, c).wait()
            wides[i] = raw[i, c].astype(F32)
        for h in range(heads):
            cols = slice(h * dk, (h + 1) * dk)
            mine = pl.ds(h, CHUNK, stride=heads)
            q, k, v = (wides[i, mine, :].astype(BF16) for i in range(3))
            qf_ref[rows, cols] = q
            kf_ref[rows, cols] = k
            vf_ref[rows, cols] = v
            qt_ref[cols, rows] = q.T
            vt = v.T
            vt_ref[cols, rows] = vt
            acc[h] += dot(vt, k, NN)
        return 0

    lax.fori_loop(0, n, one_chunk, 0)
    low, high = acc[: heads // 2].astype(BF16), acc[heads // 2 :].astype(BF16)
    first = lax.axis_index("ctx") % 2 == 0
    keep_ref[...] = jnp.where(first, low, high)
    send_ref[...] = jnp.where(first, high, low)


def prepare(q, k, v, token, tokens, heads, dk):
    n = tokens // CHUNK
    width = heads * dk
    return call(
        functools.partial(prepare_kernel, heads, dk),
        "prepare",
        [*outside(q, k, v), token],
        [ANYWHERE] * 4,
        [shape((tokens, width), BF16)] * 3
        + [shape((width, tokens), BF16)] * 2
        + [shape((n, heads, dk, dk), F32), shape((tokens, dk), F32)]
        + [shape((heads // 2, dk, dk), BF16)] * 2
        + [shape(TOKEN, F32)],
        [WHOLE] * 10,
        [
            pltpu.VMEM((3, n, CHUNK * heads, dk), BF16),
            pltpu.VMEM((3, CHUNK * heads, dk), F32),
            pltpu.VMEM((heads, dk, dk), F32),
            pltpu.SemaphoreType.DMA((3, n)),
        ],
    )


def early_kernel(starts, *refs):
    count = len(starts)
    pieces, besides, (w_ref, _, out_ref, token_ref) = refs[:count], refs[count:-4], refs[-4:]
    token_ref[...] = jnp.zeros_like(token_ref)
    features = w_ref.shape[1] // lax.axis_size("head")
    place = lax.axis_index("head")
    first, second = part_of(place, features), part_of(place ^ 1, features)

    def one_tile(j, _):
        tile = part_of(j, PAIR * 128)
        wa, wb = w_ref[tile, first].T, w_ref[tile, second].T
        for start, piece in zip(starts, pieces):
            for row in range(0, piece.shape[0], CHUNK):
                b_ref = besides[(start + row) // CHUNK]
                product = dot(piece[row : row + CHUNK, :], wa, NN) + dot(b_ref[...], wb, NN)
                out_ref[start + row : start + row + CHUNK, tile] = product
        return 0

    lax.fori_loop(0, out_ref.shape[1] // (PAIR * 128), one_tile, 0)


def early(pieces, starts, besides, weight, token):
    tokens = sum(b.shape[0] for b in besides)
    width = weight.shape[0]
    return call(
        functools.partial(early_kernel, starts),
        "early",
        [*pieces, *besides, weight, token],
        [WHOLE] * (len(pieces) + len(besides) + 1) + [ANYWHERE],
        [shape((tokens, width), F32), shape(TOKEN, F32)],
        [WHOLE] * 2,
    )


def late_kernel(half, first, start, near, dk, b_ref, w_ref, part_ref, scale_ref, qt_ref, _, *refs):
    a_ref, refs = (refs[0], refs[1:]) if half is None else (None, refs)
    state_ref, refs = (None, refs) if first else (refs[0], refs[1:])
    d_ref, token_ref = refs[:2]
    tile = PAIR * dk
    steps = d_ref.shape[1] // tile
    out_ref, refs = refs[2], refs[3:]
    token_ref[...] = jnp.zeros_like(token_ref)
    if half is None:
        at, bt = refs
        at[...] = a_ref[...].T
        bt[...] = b_ref[...].T
    elif half == 1:
        (bt,) = refs
        bt[...] = b_ref[...].T
    else:
        bt = b_ref
    features, count = bt.shape
    place = lax.axis_index("head")
    one, two = part_of(place ^ near, features), part_of(place ^ near ^ 1, features)
    here = slice(start, start + count)
    base = 0 if half is None else steps * (lax.axis_index("ctx") % 2 ^ half)

    def one_tile(local, _):
        j = base + local
        wide = part_of(j, tile)
        turned = dot(w_ref[wide, two], bt[...], NN)
        if half is None:
            turned = turned + dot(w_ref[wide, one], at[...], NN)
        low = (part_ref[here if half is None else slice(0, count), wide] + turned.T).astype(BF16)
        d_ref[:, part_of(local, tile)] = low
        states = [None if first else state_ref[0, j * PAIR + i] for i in range(PAIR)]
        for c in reversed(range(count // CHUNK)):
            rows = slice(c * CHUNK, (c + 1) * CHUNK)
            there = slice(start + c * CHUNK, start + (c + 1) * CHUNK)
            for i in range(PAIR):
                grad = (low[rows, i * dk : (i + 1) * dk].astype(F32) * scale_ref[there, :]).astype(BF16)
                state = dot(qt_ref[part_of(j * PAIR + i, dk), there], grad, NN)
                states[i] = state if states[i] is None else states[i] + state
                if half is None:
                    out_ref[c, j * PAIR + i] = states[i]
        if half is not None:
            for i in range(PAIR):
                out_ref[local * PAIR + i] = states[i].astype(BF16)
        return 0

    if half is None:
        lax.fori_loop(0, steps, one_tile, 0)
    else:
        for local in range(steps):
            one_tile(local, 0)


def middle_kernel(start, near, a_ref, w_ref, part_ref, _, out_ref, token_ref, at):
    token_ref[...] = jnp.zeros_like(token_ref)
    at[...] = a_ref[...].T
    features, count = at.shape
    one = part_of(lax.axis_index("head") ^ near, features)
    tile = PAIR * 128
    for j in range(out_ref.shape[1] // tile):
        wide = slice(j * tile, (j + 1) * tile)
        out_ref[:, wide] = part_ref[start : start + count, wide] + dot(w_ref[wide, one], at[...], NN).T


def middle(start, near, a, weight, part, token):
    return call(
        functools.partial(middle_kernel, start, near),
        "middle",
        [a, weight, part, token],
        [WHOLE] * 3 + [ANYWHERE],
        [shape((a.shape[0], part.shape[1]), F32), shape(TOKEN, F32)],
        [WHOLE] * 2,
        [pltpu.VMEM(a.shape[::-1], BF16)],
    )


def late(start, half, near, a, b, weight, part, scale, qt, token, state, heads, dk):
    features, rows = b.shape if half == 0 else b.shape[::-1]
    width = weight.shape[0]
    args = [b, weight, part, scale, qt, token]
    in_specs = [WHOLE] * 5 + [ANYWHERE]
    if half is None:
        args.append(a)
        in_specs.append(WHOLE)
    if state is not None:
        args.append(state)
        in_specs.append(WHOLE)
    if half is None:
        out_shape = [shape((rows, width), BF16), shape(TOKEN, F32), shape((rows // CHUNK, heads, dk, dk), F32)]
    else:
        out_shape = [shape((rows, width // 2), BF16), shape(TOKEN, F32)]
        out_shape.append(shape((heads // 2, dk, dk), BF16))
    scratch = [pltpu.VMEM((features, rows), BF16)] * 2 if half is None else []
    if half == 1:
        out_shape.append(shape((features, rows), BF16))
    return call(
        functools.partial(late_kernel, half, state is None, start, near, dk),
        "late",
        args,
        in_specs,
        out_shape,
        [WHOLE] * len(out_shape),
        scratch,
    )


def within_kernel(
    heads, dk, chunk, at, level, others,
    q_ref, k_ref, v_ref, qt_ref, vt_ref, d_ref, also_ref, scale_ref, before_ref, own_ref, other_ref, _, *refs
):
    state_ref, refs = (None, refs) if level is None else (refs[0], refs[1:])
    earlier_dq, refs = refs[: len(others)], refs[len(others) :]
    dq_ref, dk_ref, dv_ref, token_ref, wide = refs[:5]
    token_ref[...] = jnp.zeros_like(token_ref)
    if others:
        low_ref, sem = refs[5:]
        copies = [
            pltpu.make_async_copy(source, dq_ref.at[pl.ds(c * CHUNK * heads, CHUNK * heads)], sem.at[i])
            for i, (c, source) in enumerate(zip(others, earlier_dq))
        ]
        for copy in copies:
            copy.start()
    rows = slice(chunk * CHUNK, (chunk + 1) * CHUNK)
    there = None if at is None else slice(at * CHUNK, (at + 1) * CHUNK)
    t = lax.broadcasted_iota(jnp.int32, (CHUNK, CHUNK), 0)
    s = lax.broadcasted_iota(jnp.int32, (CHUNK, CHUNK), 1)
    lower = s <= t
    upper = t <= s
    scale = scale_ref[rows, :]
    half = heads // 2

    for g, prefix_ref in enumerate((own_ref, other_ref)):
        for i in range(half):
            h = (lax.axis_index("ctx") % 2 ^ g) * half + i
            cols = part_of(h, dk)
            q, k, v = q_ref[rows, cols], k_ref[rows, cols], v_ref[rows, cols]
            if at is None:
                d = (d_ref, also_ref)[g][:, i * dk : (i + 1) * dk]
            else:
                d = d_ref[there, cols]
            grad = (d.astype(F32) * scale).astype(BF16)
            score_grad = jnp.where(lower, dot(grad, vt_ref[cols, rows], NN), 0.0).astype(BF16)
            score_grad_t = jnp.where(upper, dot(v, grad, NT), 0.0).astype(BF16)
            score_keys_t = jnp.where(upper, dot(k, qt_ref[cols, rows], NN), 0.0).astype(BF16)
            earlier = prefix_ref[i].astype(F32) + before_ref[chunk, h]
            dq = scale * dot(d, earlier.astype(BF16), NN) + dot(score_grad, k, NN)
            dkey = dot(score_grad_t, q, NN)
            dval = dot(score_keys_t, grad, NN)
            if state_ref is not None:
                after = state_ref[level, h].astype(BF16)
                dkey = dkey + dot(v, after, NT)
                dval = dval + dot(k, after, NN)
            wide[pl.ds(h, CHUNK, stride=heads), :] = dq
            dk_ref[:, cols] = dkey.astype(BF16)
            dv_ref[:, cols] = dval.astype(BF16)
    if others:
        low_ref[...] = wide[...].astype(BF16)
        last = pltpu.make_async_copy(
            low_ref, dq_ref.at[pl.ds(chunk * CHUNK * heads, CHUNK * heads)], sem.at[len(others)]
        )
        last.start()
        for copy in copies + [last]:
            copy.wait()
    else:
        dq_ref[...] = wide[...].astype(BF16)


def within(chunk, q, k, v, qt, vt, d, also, at, scale, before, own, other, token, state, others, heads, dk):
    tokens, width = q.shape
    args = [q, k, v, qt, vt, d, also, scale, before, own, other, token]
    in_specs = [WHOLE] * 11 + [ANYWHERE]
    level = None
    if state is not None:
        level = state[1]
        args.append(state[0])
        in_specs.append(WHOLE)
    args += list(others.values())
    in_specs += [WHOLE] * len(others)
    scratch = [pltpu.VMEM((CHUNK * heads, dk), F32)]
    rows = tokens if others else CHUNK
    if others:
        scratch += [pltpu.VMEM((CHUNK * heads, dk), BF16), pltpu.SemaphoreType.DMA((len(others) + 1,))]
    return call(
        functools.partial(within_kernel, heads, dk, chunk, at, level, list(others)),
        "within",
        args,
        in_specs,
        [shape((rows * heads, dk), BF16)] + [shape((CHUNK, width), BF16)] * 2 + [shape(TOKEN, F32)],
        [ANYWHERE if others else WHOLE] + [WHOLE] * 3,
        scratch,
    )


def finish_kernel(heads, dk, n, last, k_ref, v_ref, suffix_ref, _, *refs):
    half = heads // 2
    dkp, dvp, refs = refs[:n], refs[n : 2 * n], refs[2 * n :]
    if last:
        dk_ref, dv_ref, wide_k, wide_v, after, turned, low_k, low_v, sem = refs[2:]
    else:
        wide_k, wide_v, token_ref, after, turned = refs
        token_ref[...] = jnp.zeros_like(token_ref)
    base = half * (lax.axis_index("ctx") % 2 ^ last)
    after[...] = jnp.zeros_like(after)
    turned[...] = jnp.zeros_like(turned)
    for h in range(half):
        cols = slice(h % PAIR * dk, (h % PAIR + 1) * dk)
        after[h // PAIR, cols, cols] = suffix_ref[h]
        turned[h // PAIR, cols, cols] = suffix_ref[h].T
    copies = []
    step = CHUNK // 2
    for c in range(2 * n):
        rows = slice(c * step, (c + 1) * step)
        local = slice(c % 2 * step, (c % 2 + 1) * step)
        for p in range(half // PAIR):
            cols = part_of(base // PAIR + p, PAIR * dk)
            full_k = dkp[c // 2][local, cols].astype(F32) + dot(v_ref[rows, cols], turned[p], NN)
            full_v = dvp[c // 2][local, cols].astype(F32) + dot(k_ref[rows, cols], after[p], NN)
            for i in range(PAIR):
                mine = pl.ds(c * step * heads + base + p * PAIR + i, step, stride=heads)
                wide_k[mine, :] = full_k[:, i * dk : (i + 1) * dk]
                wide_v[mine, :] = full_v[:, i * dk : (i + 1) * dk]
        if last:
            raw = slice(c * step * heads, (c + 1) * step * heads)
            for i, (wide, low, out) in enumerate(((wide_k, low_k, dk_ref), (wide_v, low_v, dv_ref))):
                low[c] = wide[raw, :].astype(BF16)
                copy = pltpu.make_async_copy(low.at[c], out.at[pl.ds(c * step * heads, step * heads)], sem.at[i, c])
                copy.start()
                copies.append(copy)
    for copy in copies:
        copy.wait()


def finish(k, v, dkp, dvp, suffix, token, held, heads, dk):
    tokens, width = k.shape
    n = tokens // CHUNK
    last = held is not None
    raw = (tokens * heads, dk)
    args = [k, v, suffix, token, *dkp, *dvp]
    in_specs = [WHOLE] * 3 + [ANYWHERE] + [WHOLE] * (2 * n)
    out_shape = [shape(raw, F32)] * 2
    out_specs = [WHOLE] * 2
    scratch = [pltpu.VMEM((heads // 2 // PAIR, PAIR * dk, PAIR * dk), BF16)] * 2
    aliases = {}
    if last:
        aliases = {len(args): 2, len(args) + 1: 3}
        args += held
        in_specs += [WHOLE] * 2
        out_shape = [shape(raw, BF16)] * 2 + out_shape
        out_specs = [ANYWHERE] * 2 + out_specs
        scratch += [pltpu.VMEM((2 * n, CHUNK // 2 * heads, dk), BF16)] * 2 + [pltpu.SemaphoreType.DMA((2, 2 * n))]
    else:
        out_shape.append(shape(TOKEN, F32))
        out_specs.append(WHOLE)
    kernel = functools.partial(finish_kernel, heads, dk, n, int(last))
    return call(kernel, "finish", args, in_specs, out_shape, out_specs, scratch, aliases)


def swap(array, axis, size, bit):
    return lax.ppermute(array, axis, [(i, i ^ bit) for i in range(size)])


def shifted(array, size, step):
    return lax.ppermute(array, "ctx", [(i, i + step) for i in range(size) if 0 <= i + step < size])


class Order:
    def __init__(self):
        self.token = None

    def tie(self, array):
        array, self.token = lax.optimization_barrier((array, self.token))
        return array


def total_kernel(*refs):
    *terms, out = refs
    total = terms[0][...].astype(F32)
    for term in terms[1:]:
        total = total + term[...].astype(F32)
    out[...] = total.astype(BF16)


def ends_kernel(later_is_odd, own, came, *refs):
    *got, give, mine = refs
    exclusive = got[0][...].astype(F32)
    for term in got[1:]:
        exclusive = exclusive + term[...].astype(F32)
    later = (lax.axis_index("ctx") % 2 == 1) == later_is_odd
    give[...] = jnp.where(later, exclusive, exclusive + own[...].astype(F32)).astype(BF16)
    mine[...] = jnp.where(later, exclusive + came[...].astype(F32), exclusive).astype(BF16)


def scan_states(keep, send, size, direction, order):
    terms = [[own, swap(away, "ctx", size, 1)] for own, away in zip(keep, send)]
    yield None
    like = shape(keep[0].shape, BF16)
    step = 2
    while step < size:
        for part in terms:
            total = call(total_kernel, "total", part, [WHOLE] * len(part), like, WHOLE)
            part.append(shifted(order.tie(total), size, direction * step))
        yield None
        step *= 2
    kernel = functools.partial(ends_kernel, direction == 1)
    mine, other = [], []
    for part in terms:
        give, own = call(kernel, "ends", part, [WHOLE] * len(part), [like] * 2, [WHOLE] * 2)
        mine.append(own)
        other.append(swap(order.tie(give), "ctx", size, 1))
    yield mine, other


def body(n_ctx, n_head, queries, keys, values, d_layer, out_weight):
    tokens, heads, dk = queries.shape
    n = tokens // CHUNK
    near = n_head // 2
    far = 1
    groups = [(1, n - 1), (0, 1)]
    order = Order()
    *pieces, order.token = cut(d_layer, groups)
    across = {c: swap(piece, "head", n_head, near) for (c, _), piece in zip(groups, pieces)}

    flat = (tokens * heads, dk)
    q, k, v, qt, vt, before, scale, keep, send, order.token = prepare(
        queries.reshape(flat), keys.reshape(flat), values.reshape(flat), order.token, tokens, heads, dk
    )
    forward = scan_states([keep], [send], n_ctx, 1, order)
    next(forward)
    *blocks, order.token = cut(order.tie(d_layer), [(c, 1) for c in range(n)])
    beside = [swap(one, "head", n_head, far) for one in blocks]
    starts = [c * CHUNK for c, _ in groups]
    part, order.token = early(pieces, starts, beside, out_weight, order.token)

    prefix = None
    while prefix is None:
        prefix = next(forward)
    prefix = [prefix[0][0], prefix[1][0]]
    d, after, dq, dkp, dvp = {}, {}, {}, {}, {}

    def inner(c):
        others = dict(dq) if c == 0 else {}
        dq[c], dkp[c], dvp[c], order.token = within(
            c, q, k, v, qt, vt, *d[c], scale, before, *prefix, order.token, after[c], others, heads, dk
        )

    state = None
    for c, m in groups[:-1]:
        after[c + m - 1] = None if state is None else (state, 0)
        piece = order.tie(across[c])
        both = swap(piece, "head", n_head, far)
        low, order.token, state = late(
            c * CHUNK, None, near, piece, both, out_weight, part, scale, qt, order.token, state, heads, dk
        )
        for i in range(m):
            d[c + i] = (low, low, i)
            if i < m - 1:
                after[c + i] = (state, i + 1)
        for i in reversed(range(m)):
            if c + i > 2:
                inner(c + i)
    after[0] = (state, 0)
    piece = order.tie(across[0])
    both = swap(piece, "head", n_head, far)
    part, order.token = middle(0, near, piece, out_weight, part, order.token)
    low_send, order.token, send, turned = late(
        0, 1, near, None, both, out_weight, part, scale, qt, order.token, state, heads, dk
    )
    low_keep, order.token, keep = late(
        0, 0, near, None, turned, out_weight, part, scale, qt, order.token, state, heads, dk
    )
    d[0] = (low_keep, low_send, None)
    backward = scan_states([keep], [send], n_ctx, -1, order)
    next(backward)
    plan = [[c for c in range(n) if c > 1 and c not in dq], [1, 0]]
    suffix = None
    while suffix is None:
        suffix = next(backward)
        for c in plan.pop(0) if plan else []:
            inner(c)
    parts = [[dkp[c] for c in range(n)], [dvp[c] for c in range(n)]]
    *held, order.token = finish(k, v, *parts, suffix[0][0], order.token, None, heads, dk)
    d_keys, d_values, *_ = finish(k, v, *parts, suffix[1][0], order.token, held, heads, dk)
    return tuple(a.reshape(tokens, heads, dk) for a in (dq[0], d_keys, d_values))


def solution(mesh):
    in_specs = (
        P("ctx", "head", None),
        P("ctx", "head", None),
        P("ctx", "head", None),
        P("ctx", "head"),
        P("head", None),
    )
    out_specs = (P("ctx", "head", None), P("ctx", "head", None), P("ctx", "head", None))

    def program(queries, keys, values, d_layer, out_weight):
        return body(mesh.shape["ctx"], mesh.shape["head"], queries, keys, values, d_layer, out_weight)

    return jax.shard_map(program, mesh=mesh, in_specs=in_specs, out_specs=out_specs, check_vma=False)
```

```python
import functools

import jax
import jax.numpy as jnp
from jax import lax
from jax.experimental import pallas as pl
from jax.experimental.pallas import tpu as pltpu
from jax.sharding import PartitionSpec as P

CHUNK = 256
PAIR = 2
F32 = jnp.float32
BF16 = jnp.bfloat16
TOKEN = (8, 128)
NT = (((1,), (1,)), ((), ()))
NN = (((1,), (0,)), ((), ()))
FREE = pl.CostEstimate(flops=0, bytes_accessed=0, transcendentals=0)
VMEM_LIMIT = 14 * 1024 * 1024
WHOLE = pl.BlockSpec(memory_space=pltpu.VMEM)
ANYWHERE = pl.BlockSpec(memory_space=pl.ANY)


def dot(a, b, dims):
    return lax.dot_general(a, b, dims, preferred_element_type=F32)


def shape(dims, dtype):
    return jax.ShapeDtypeStruct(dims, dtype)


def outside(*arrays):
    return [pltpu.with_memory_space_constraint(a, pltpu.HBM) for a in arrays]


def part_of(i, size):
    return slice(i * size, (i + 1) * size) if isinstance(i, int) else pl.ds(pl.multiple_of(i * size, size), size)


def call(kernel, name, args, in_specs, out_shape, out_specs, scratch=(), aliases=None):
    return pl.pallas_call(
        kernel,
        in_specs=in_specs,
        out_specs=out_specs,
        out_shape=out_shape,
        scratch_shapes=scratch,
        input_output_aliases=aliases or {},
        compiler_params=pltpu.CompilerParams(vmem_limit_bytes=VMEM_LIMIT),
        cost_estimate=FREE,
        name=name,
    )(*args)


def cut_kernel(starts, source, *refs):
    pieces, token_ref, sem = refs[: len(starts)], refs[-2], refs[-1]
    token_ref[...] = jnp.zeros_like(token_ref)
    copies = []
    for start, piece in zip(starts, pieces):
        for row in range(0, piece.shape[0], CHUNK // 2):
            rows = pl.ds(start + row, CHUNK // 2)
            copies.append(
                pltpu.make_async_copy(source.at[rows], piece.at[pl.ds(row, CHUNK // 2)], sem.at[len(copies)])
            )
    for copy in copies:
        copy.start()
    for copy in copies:
        copy.wait()


def cut(d_layer, groups):
    features = d_layer.shape[1]
    return call(
        functools.partial(cut_kernel, [c * CHUNK for c, _ in groups]),
        "cut",
        outside(d_layer),
        [ANYWHERE],
        [shape((m * CHUNK, features), d_layer.dtype) for _, m in groups] + [shape(TOKEN, F32)],
        [WHOLE] * (len(groups) + 1),
        [pltpu.SemaphoreType.DMA((sum(m for _, m in groups) * 2,))],
    )


def prepare_kernel(
    heads, dk, q_ref, k_ref, v_ref, _, qf_ref, kf_ref, vf_ref, qt_ref, vt_ref, before_ref, scale_ref, keep_ref, send_ref, token_ref,
    raw, wides, acc, sem
):
    n = qf_ref.shape[0] // CHUNK

    def load(i, c):
        source = (q_ref, k_ref, v_ref)[i].at[part_of(c, CHUNK * heads)]
        return pltpu.make_async_copy(source, raw.at[i, c], sem.at[i, c])

    for c in range(n):
        for i in range(3):
            load(i, c).start()
    token_ref[...] = jnp.zeros_like(token_ref)
    acc[...] = jnp.zeros_like(acc)
    tokens = scale_ref.shape[0]
    position = lax.axis_index("ctx") * tokens + lax.broadcasted_iota(jnp.int32, scale_ref.shape, 0)
    scale_ref[...] = lax.rsqrt((dk * (position + 1)).astype(F32))

    def one_chunk(c, _):
        rows = part_of(c, CHUNK)
        before_ref[c] = acc[...]
        for i in range(3):
            load(i, c).wait()
            wides[i] = raw[i, c].astype(F32)
        for h in range(heads):
            cols = slice(h * dk, (h + 1) * dk)
            mine = pl.ds(h, CHUNK, stride=heads)
            q, k, v = (wides[i, mine, :].astype(BF16) for i in range(3))
            qf_ref[rows, cols] = q
            kf_ref[rows, cols] = k
            vf_ref[rows, cols] = v
            qt_ref[cols, rows] = q.T
            vt = v.T
            vt_ref[cols, rows] = vt
            acc[h] += dot(vt, k, NN)
        return 0

    lax.fori_loop(0, n, one_chunk, 0)
    low, high = acc[: heads // 2].astype(BF16), acc[heads // 2 :].astype(BF16)
    first = lax.axis_index("ctx") % 2 == 0
    keep_ref[...] = jnp.where(first, low, high)
    send_ref[...] = jnp.where(first, high, low)


def prepare(q, k, v, token, tokens, heads, dk):
    n = tokens // CHUNK
    width = heads * dk
    return call(
        functools.partial(prepare_kernel, heads, dk),
        "prepare",
        [*outside(q, k, v), token],
        [ANYWHERE] * 4,
        [shape((tokens, width), BF16)] * 3
        + [shape((width, tokens), BF16)] * 2
        + [shape((n, heads, dk, dk), F32), shape((tokens, dk), F32)]
        + [shape((heads // 2, dk, dk), BF16)] * 2
        + [shape(TOKEN, F32)],
        [WHOLE] * 10,
        [
            pltpu.VMEM((3, n, CHUNK * heads, dk), BF16),
            pltpu.VMEM((3, CHUNK * heads, dk), F32),
            pltpu.VMEM((heads, dk, dk), F32),
            pltpu.SemaphoreType.DMA((3, n)),
        ],
    )


def early_kernel(starts, *refs):
    count = len(starts)
    pieces, besides, (w_ref, _, out_ref, token_ref) = refs[:count], refs[count:-4], refs[-4:]
    token_ref[...] = jnp.zeros_like(token_ref)
    features = w_ref.shape[1] // lax.axis_size("head")
    place = lax.axis_index("head")
    first, second = part_of(place, features), part_of(place ^ 1, features)

    def one_tile(j, _):
        tile = part_of(j, PAIR * 128)
        wa, wb = w_ref[tile, first].T, w_ref[tile, second].T
        for start, piece in zip(starts, pieces):
            for row in range(0, piece.shape[0], CHUNK):
                b_ref = besides[(start + row) // CHUNK]
                product = dot(piece[row : row + CHUNK, :], wa, NN) + dot(b_ref[...], wb, NN)
                out_ref[start + row : start + row + CHUNK, tile] = product
        return 0

    lax.fori_loop(0, out_ref.shape[1] // (PAIR * 128), one_tile, 0)


def early(pieces, starts, besides, weight, token):
    tokens = sum(b.shape[0] for b in besides)
    width = weight.shape[0]
    return call(
        functools.partial(early_kernel, starts),
        "early",
        [*pieces, *besides, weight, token],
        [WHOLE] * (len(pieces) + len(besides) + 1) + [ANYWHERE],
        [shape((tokens, width), F32), shape(TOKEN, F32)],
        [WHOLE] * 2,
    )


def late_kernel(half, first, start, near, dk, b_ref, w_ref, part_ref, scale_ref, qt_ref, _, *refs):
    a_ref, refs = (refs[0], refs[1:]) if half is None else (None, refs)
    state_ref, refs = (None, refs) if first else (refs[0], refs[1:])
    d_ref, token_ref = refs[:2]
    tile = PAIR * dk
    steps = d_ref.shape[1] // tile
    out_ref, refs = refs[2], refs[3:]
    token_ref[...] = jnp.zeros_like(token_ref)
    if half is None:
        at, bt = refs
        at[...] = a_ref[...].T
        bt[...] = b_ref[...].T
    elif half == 1:
        (bt,) = refs
        bt[...] = b_ref[...].T
    else:
        bt = b_ref
    features, count = bt.shape
    place = lax.axis_index("head")
    one, two = part_of(place ^ near, features), part_of(place ^ near ^ 1, features)
    here = slice(start, start + count)
    base = 0 if half is None else steps * (lax.axis_index("ctx") % 2 ^ half)

    def one_tile(local, _):
        j = base + local
        wide = part_of(j, tile)
        turned = dot(w_ref[wide, two], bt[...], NN)
        if half is None:
            turned = turned + dot(w_ref[wide, one], at[...], NN)
        low = (part_ref[here if half is None else slice(0, count), wide] + turned.T).astype(BF16)
        d_ref[:, part_of(local, tile)] = low
        states = [None if first else state_ref[0, j * PAIR + i] for i in range(PAIR)]
        for c in reversed(range(count // CHUNK)):
            rows = slice(c * CHUNK, (c + 1) * CHUNK)
            there = slice(start + c * CHUNK, start + (c + 1) * CHUNK)
            for i in range(PAIR):
                grad = (low[rows, i * dk : (i + 1) * dk].astype(F32) * scale_ref[there, :]).astype(BF16)
                state = dot(qt_ref[part_of(j * PAIR + i, dk), there], grad, NN)
                states[i] = state if states[i] is None else states[i] + state
                if half is None:
                    out_ref[c, j * PAIR + i] = states[i]
        if half is not None:
            for i in range(PAIR):
                out_ref[local * PAIR + i] = states[i].astype(BF16)
        return 0

    if half is None:
        lax.fori_loop(0, steps, one_tile, 0)
    else:
        for local in range(steps):
            one_tile(local, 0)


def middle_kernel(start, near, a_ref, w_ref, part_ref, _, out_ref, token_ref, at):
    token_ref[...] = jnp.zeros_like(token_ref)
    at[...] = a_ref[...].T
    features, count = at.shape
    one = part_of(lax.axis_index("head") ^ near, features)
    tile = PAIR * 128
    for j in range(out_ref.shape[1] // tile):
        wide = slice(j * tile, (j + 1) * tile)
        out_ref[:, wide] = part_ref[start : start + count, wide] + dot(w_ref[wide, one], at[...], NN).T


def middle(start, near, a, weight, part, token):
    return call(
        functools.partial(middle_kernel, start, near),
        "middle",
        [a, weight, part, token],
        [WHOLE] * 3 + [ANYWHERE],
        [shape((a.shape[0], part.shape[1]), F32), shape(TOKEN, F32)],
        [WHOLE] * 2,
        [pltpu.VMEM(a.shape[::-1], BF16)],
    )


def late(start, half, near, a, b, weight, part, scale, qt, token, state, heads, dk):
    features, rows = b.shape if half == 0 else b.shape[::-1]
    width = weight.shape[0]
    args = [b, weight, part, scale, qt, token]
    in_specs = [WHOLE] * 5 + [ANYWHERE]
    if half is None:
        args.append(a)
        in_specs.append(WHOLE)
    if state is not None:
        args.append(state)
        in_specs.append(WHOLE)
    if half is None:
        out_shape = [shape((rows, width), BF16), shape(TOKEN, F32), shape((rows // CHUNK, heads, dk, dk), F32)]
    else:
        out_shape = [shape((rows, width // 2), BF16), shape(TOKEN, F32)]
        out_shape.append(shape((heads // 2, dk, dk), BF16))
    scratch = [pltpu.VMEM((features, rows), BF16)] * 2 if half is None else []
    if half == 1:
        out_shape.append(shape((features, rows), BF16))
    return call(
        functools.partial(late_kernel, half, state is None, start, near, dk),
        "late",
        args,
        in_specs,
        out_shape,
        [WHOLE] * len(out_shape),
        scratch,
    )


def within_kernel(
    heads, dk, chunk, at, level, others,
    q_ref, k_ref, v_ref, qt_ref, vt_ref, d_ref, also_ref, scale_ref, before_ref, own_ref, other_ref, _, *refs
):
    state_ref, refs = (None, refs) if level is None else (refs[0], refs[1:])
    earlier_dq, refs = refs[: len(others)], refs[len(others) :]
    dq_ref, dk_ref, dv_ref, token_ref, wide = refs[:5]
    token_ref[...] = jnp.zeros_like(token_ref)
    if others:
        low_ref, sem = refs[5:]
        copies = [
            pltpu.make_async_copy(source, dq_ref.at[pl.ds(c * CHUNK * heads, CHUNK * heads)], sem.at[i])
            for i, (c, source) in enumerate(zip(others, earlier_dq))
        ]
        for copy in copies:
            copy.start()
    rows = slice(chunk * CHUNK, (chunk + 1) * CHUNK)
    there = None if at is None else slice(at * CHUNK, (at + 1) * CHUNK)
    t = lax.broadcasted_iota(jnp.int32, (CHUNK, CHUNK), 0)
    s = lax.broadcasted_iota(jnp.int32, (CHUNK, CHUNK), 1)
    lower = s <= t
    upper = t <= s
    scale = scale_ref[rows, :]
    half = heads // 2

    for g, prefix_ref in enumerate((own_ref, other_ref)):
        for i in range(half):
            h = (lax.axis_index("ctx") % 2 ^ g) * half + i
            cols = part_of(h, dk)
            q, k, v = q_ref[rows, cols], k_ref[rows, cols], v_ref[rows, cols]
            if at is None:
                d = (d_ref, also_ref)[g][:, i * dk : (i + 1) * dk]
            else:
                d = d_ref[there, cols]
            grad = (d.astype(F32) * scale).astype(BF16)
            score_grad = jnp.where(lower, dot(grad, vt_ref[cols, rows], NN), 0.0).astype(BF16)
            score_grad_t = jnp.where(upper, dot(v, grad, NT), 0.0).astype(BF16)
            score_keys_t = jnp.where(upper, dot(k, qt_ref[cols, rows], NN), 0.0).astype(BF16)
            earlier = prefix_ref[i].astype(F32) + before_ref[chunk, h]
            dq = scale * dot(d, earlier.astype(BF16), NN) + dot(score_grad, k, NN)
            dkey = dot(score_grad_t, q, NN)
            dval = dot(score_keys_t, grad, NN)
            if state_ref is not None:
                after = state_ref[level, h].astype(BF16)
                dkey = dkey + dot(v, after, NT)
                dval = dval + dot(k, after, NN)
            wide[pl.ds(h, CHUNK, stride=heads), :] = dq
            dk_ref[:, cols] = dkey.astype(BF16)
            dv_ref[:, cols] = dval.astype(BF16)
    if others:
        low_ref[...] = wide[...].astype(BF16)
        last = pltpu.make_async_copy(
            low_ref, dq_ref.at[pl.ds(chunk * CHUNK * heads, CHUNK * heads)], sem.at[len(others)]
        )
        last.start()
        for copy in copies + [last]:
            copy.wait()
    else:
        dq_ref[...] = wide[...].astype(BF16)


def within(chunk, q, k, v, qt, vt, d, also, at, scale, before, own, other, token, state, others, heads, dk):
    tokens, width = q.shape
    args = [q, k, v, qt, vt, d, also, scale, before, own, other, token]
    in_specs = [WHOLE] * 11 + [ANYWHERE]
    level = None
    if state is not None:
        level = state[1]
        args.append(state[0])
        in_specs.append(WHOLE)
    args += list(others.values())
    in_specs += [WHOLE] * len(others)
    scratch = [pltpu.VMEM((CHUNK * heads, dk), F32)]
    rows = tokens if others else CHUNK
    if others:
        scratch += [pltpu.VMEM((CHUNK * heads, dk), BF16), pltpu.SemaphoreType.DMA((len(others) + 1,))]
    return call(
        functools.partial(within_kernel, heads, dk, chunk, at, level, list(others)),
        "within",
        args,
        in_specs,
        [shape((rows * heads, dk), BF16)] + [shape((CHUNK, width), BF16)] * 2 + [shape(TOKEN, F32)],
        [ANYWHERE if others else WHOLE] + [WHOLE] * 3,
        scratch,
    )


def finish_kernel(heads, dk, n, last, k_ref, v_ref, suffix_ref, _, *refs):
    half = heads // 2
    dkp, dvp, refs = refs[:n], refs[n : 2 * n], refs[2 * n :]
    if last:
        dk_ref, dv_ref, wide_k, wide_v, after, turned, low_k, low_v, sem = refs[2:]
    else:
        wide_k, wide_v, token_ref, after, turned = refs
        token_ref[...] = jnp.zeros_like(token_ref)
    base = half * (lax.axis_index("ctx") % 2 ^ last)
    after[...] = jnp.zeros_like(after)
    turned[...] = jnp.zeros_like(turned)
    for h in range(half):
        cols = slice(h % PAIR * dk, (h % PAIR + 1) * dk)
        after[h // PAIR, cols, cols] = suffix_ref[h]
        turned[h // PAIR, cols, cols] = suffix_ref[h].T
    copies = []
    step = CHUNK // 2
    for c in range(2 * n):
        rows = slice(c * step, (c + 1) * step)
        local = slice(c % 2 * step, (c % 2 + 1) * step)
        for p in range(half // PAIR):
            cols = part_of(base // PAIR + p, PAIR * dk)
            full_k = dkp[c // 2][local, cols].astype(F32) + dot(v_ref[rows, cols], turned[p], NN)
            full_v = dvp[c // 2][local, cols].astype(F32) + dot(k_ref[rows, cols], after[p], NN)
            for i in range(PAIR):
                mine = pl.ds(c * step * heads + base + p * PAIR + i, step, stride=heads)
                wide_k[mine, :] = full_k[:, i * dk : (i + 1) * dk]
                wide_v[mine, :] = full_v[:, i * dk : (i + 1) * dk]
        if last:
            raw = slice(c * step * heads, (c + 1) * step * heads)
            for i, (wide, low, out) in enumerate(((wide_k, low_k, dk_ref), (wide_v, low_v, dv_ref))):
                low[c] = wide[raw, :].astype(BF16)
                copy = pltpu.make_async_copy(low.at[c], out.at[pl.ds(c * step * heads, step * heads)], sem.at[i, c])
                copy.start()
                copies.append(copy)
    for copy in copies:
        copy.wait()


def finish(k, v, dkp, dvp, suffix, token, held, heads, dk):
    tokens, width = k.shape
    n = tokens // CHUNK
    last = held is not None
    raw = (tokens * heads, dk)
    args = [k, v, suffix, token, *dkp, *dvp]
    in_specs = [WHOLE] * 3 + [ANYWHERE] + [WHOLE] * (2 * n)
    out_shape = [shape(raw, F32)] * 2
    out_specs = [WHOLE] * 2
    scratch = [pltpu.VMEM((heads // 2 // PAIR, PAIR * dk, PAIR * dk), BF16)] * 2
    aliases = {}
    if last:
        aliases = {len(args): 2, len(args) + 1: 3}
        args += held
        in_specs += [WHOLE] * 2
        out_shape = [shape(raw, BF16)] * 2 + out_shape
        out_specs = [ANYWHERE] * 2 + out_specs
        scratch += [pltpu.VMEM((2 * n, CHUNK // 2 * heads, dk), BF16)] * 2 + [pltpu.SemaphoreType.DMA((2, 2 * n))]
    else:
        out_shape.append(shape(TOKEN, F32))
        out_specs.append(WHOLE)
    kernel = functools.partial(finish_kernel, heads, dk, n, int(last))
    return call(kernel, "finish", args, in_specs, out_shape, out_specs, scratch, aliases)


def swap(array, axis, size, bit):
    return lax.ppermute(array, axis, [(i, i ^ bit) for i in range(size)])


def shifted(array, size, step):
    return lax.ppermute(array, "ctx", [(i, i + step) for i in range(size) if 0 <= i + step < size])


class Order:
    def __init__(self):
        self.token = None

    def tie(self, array):
        array, self.token = lax.optimization_barrier((array, self.token))
        return array


def total_kernel(*refs):
    *terms, out = refs
    total = terms[0][...].astype(F32)
    for term in terms[1:]:
        total = total + term[...].astype(F32)
    out[...] = total.astype(BF16)


def ends_kernel(later_is_odd, own, came, *refs):
    *got, give, mine = refs
    exclusive = got[0][...].astype(F32)
    for term in got[1:]:
        exclusive = exclusive + term[...].astype(F32)
    later = (lax.axis_index("ctx") % 2 == 1) == later_is_odd
    give[...] = jnp.where(later, exclusive, exclusive + own[...].astype(F32)).astype(BF16)
    mine[...] = jnp.where(later, exclusive + came[...].astype(F32), exclusive).astype(BF16)


def scan_states(keep, send, size, direction, order):
    terms = [[own, swap(away, "ctx", size, 1)] for own, away in zip(keep, send)]
    yield None
    like = shape(keep[0].shape, BF16)
    step = 2
    while step < size:
        for part in terms:
            total = call(total_kernel, "total", part, [WHOLE] * len(part), like, WHOLE)
            part.append(shifted(order.tie(total), size, direction * step))
        yield None
        step *= 2
    kernel = functools.partial(ends_kernel, direction == 1)
    mine, other = [], []
    for part in terms:
        give, own = call(kernel, "ends", part, [WHOLE] * len(part), [like] * 2, [WHOLE] * 2)
        mine.append(own)
        other.append(swap(order.tie(give), "ctx", size, 1))
    yield mine, other


def body(n_ctx, n_head, queries, keys, values, d_layer, out_weight):
    tokens, heads, dk = queries.shape
    n = tokens // CHUNK
    near = n_head // 2
    far = 1
    groups = [(1, n - 1), (0, 1)]
    order = Order()
    *pieces, order.token = cut(d_layer, groups[:-1])
    across = {c: swap(piece, "head", n_head, near) for (c, _), piece in zip(groups, pieces)}

    flat = (tokens * heads, dk)
    q, k, v, qt, vt, before, scale, keep, send, order.token = prepare(
        queries.reshape(flat), keys.reshape(flat), values.reshape(flat), order.token, tokens, heads, dk
    )
    forward = scan_states([keep], [send], n_ctx, 1, order)
    next(forward)
    *blocks, order.token = cut(order.tie(d_layer), [(c, 1) for c in range(n)])
    beside = [swap(one, "head", n_head, far) for one in blocks]
    across[0] = swap(blocks[0], "head", n_head, near)
    starts = [c * CHUNK for c in range(n)]
    part, order.token = early(blocks, starts, beside, out_weight, order.token)

    prefix = None
    while prefix is None:
        prefix = next(forward)
    prefix = [prefix[0][0], prefix[1][0]]
    d, after, dq, dkp, dvp = {}, {}, {}, {}, {}

    def inner(c):
        others = dict(dq) if c == 0 else {}
        dq[c], dkp[c], dvp[c], order.token = within(
            c, q, k, v, qt, vt, *d[c], scale, before, *prefix, order.token, after[c], others, heads, dk
        )

    state = None
    for c, m in groups[:-1]:
        after[c + m - 1] = None if state is None else (state, 0)
        piece = order.tie(across[c])
        both = swap(piece, "head", n_head, far)
        low, order.token, state = late(
            c * CHUNK, None, near, piece, both, out_weight, part, scale, qt, order.token, state, heads, dk
        )
        for i in range(m):
            d[c + i] = (low, low, i)
            if i < m - 1:
                after[c + i] = (state, i + 1)
        for i in reversed(range(m)):
            if c + i > 2:
                inner(c + i)
    after[0] = (state, 0)
    piece = order.tie(across[0])
    both = swap(piece, "head", n_head, far)
    part, order.token = middle(0, near, piece, out_weight, part, order.token)
    low_send, order.token, send, turned = late(
        0, 1, near, None, both, out_weight, part, scale, qt, order.token, state, heads, dk
    )
    low_keep, order.token, keep = late(
        0, 0, near, None, turned, out_weight, part, scale, qt, order.token, state, heads, dk
    )
    d[0] = (low_keep, low_send, None)
    backward = scan_states([keep], [send], n_ctx, -1, order)
    next(backward)
    plan = [[c for c in range(n) if c > 1 and c not in dq], [1, 0]]
    suffix = None
    while suffix is None:
        suffix = next(backward)
        for c in plan.pop(0) if plan else []:
            inner(c)
    parts = [[dkp[c] for c in range(n)], [dvp[c] for c in range(n)]]
    *held, order.token = finish(k, v, *parts, suffix[0][0], order.token, None, heads, dk)
    d_keys, d_values, *_ = finish(k, v, *parts, suffix[1][0], order.token, held, heads, dk)
    return tuple(a.reshape(tokens, heads, dk) for a in (dq[0], d_keys, d_values))


def solution(mesh):
    in_specs = (
        P("ctx", "head", None),
        P("ctx", "head", None),
        P("ctx", "head", None),
        P("ctx", "head"),
        P("head", None),
    )
    out_specs = (P("ctx", "head", None), P("ctx", "head", None), P("ctx", "head", None))

    def program(queries, keys, values, d_layer, out_weight):
        return body(mesh.shape["ctx"], mesh.shape["head"], queries, keys, values, d_layer, out_weight)

    return jax.shard_map(program, mesh=mesh, in_specs=in_specs, out_specs=out_specs, check_vma=False)
```
